128 devices in a mesh: lon: 16 (over y, z_hi, core), lat: 8 (over z_lo, x).
Axes of the slice: x: 4, y: 4, z: 4 (z_hi: 2, z_lo: 2; z = z_hi * 2 + z_lo), core: 2. Of those that a mesh axis runs over, the one named last changes fastest.
Arguments:
- tokens: bfloat16 [2, 48, 768, 192], P(None, 'lat', 'lon'), may hold values from -80 to 80
- cotangent: bfloat16 [2, 48, 768, 192], P(None, 'lat', 'lon'), may hold values from -6 to 6
- ln1_gain: float32 [192], replicated, may hold values from 0.1 to 1.9
- w_qkv: bfloat16 [192, 576], replicated, may hold values from -0.4375 to 0.4375
- w_proj: bfloat16 [192, 192], replicated, may hold values from -0.4375 to 0.4375
- ln2_gain: float32 [192], replicated, may hold values from 0.1 to 1.9
- w_up: bfloat16 [192, 768], replicated, may hold values from -0.4375 to 0.4375
- w_down: bfloat16 [768, 192], replicated, may hold values from -0.21875 to 0.21875
- bias_table: float32 [8, 6, 3312], P('lat'), may hold values from -4 to 402
Outputs:
- d_tokens: bfloat16 [2, 48, 768, 192], P(None, 'lat', 'lon')
- d_ln1_gain: float32 [192], replicated
- d_w_qkv: float32 [192, 576], replicated
- d_w_proj: float32 [192, 192], replicated
- d_ln2_gain: float32 [192], replicated
- d_w_up: float32 [192, 768], replicated
- d_w_down: float32 [768, 192], replicated
- d_bias_table: float32 [8, 6, 3312], P('lat')
The draws below stay inside these ranges and needn't reach their ends.
All inputs are finite; a program needn't handle non-finite values.
Results may differ from the reference program's by a relative error of at most 0.019.
Values may be sent and summed in bfloat16 or wider, within the bound.
No kernel may reach another device: no remote copies, remote signals or barrier semaphores. Data moves between devices by JAX's collectives and lax.ppermute only.
A program may use at most 128 MiB of HBM per device.

```python
import math
import jax
import jax.numpy as jnp
from jax import lax

D = 192
HEADS = 6
MLP_WIDTH = 768
LEVELS = 2
WIN_LAT = 6
WIN_LON = 12
NLAT = 48
NLON = 768
TYPES = 8
POSITIONS = 3312
TOKENS = 73728


def draw_tokens(key, part):
    key = jax.random.fold_in(key, 11)
    row_key, chan_key, base_key = jax.random.split(key, 3)
    full_shape = (LEVELS, NLAT, NLON, D)
    row_scale = jnp.exp(jax.random.uniform(row_key, (LEVELS, NLAT, NLON, 1), jnp.float32) * math.log(10.0))
    chan_scale = jnp.exp(jax.random.uniform(chan_key, (D,), jnp.float32, math.log(0.5), math.log(2.0)))
    base_vals = jnp.clip(jax.random.normal(base_key, full_shape, jnp.float32), -4.0, 4.0)
    return (base_vals * row_scale * chan_scale).astype(jnp.bfloat16)


def draw_bias_table(key, part):
    key = jax.random.fold_in(key, 23)
    base_key = jax.random.fold_in(key, 0)
    full_shape = (TYPES, HEADS, POSITIONS)
    base_vals = jnp.clip(jax.random.normal(base_key, full_shape, jnp.float32), -4.0, 4.0)
    return base_vals.astype(jnp.float32)


def steps_of(rng, dims, cuts, least, largest):
    gain = 1.0
    for dim, shards_of in cuts:
        heights = jax.random.uniform(jax.random.fold_in(jax.random.fold_in(rng, 6), dim), (shards_of,), jnp.float32, least / len(cuts), largest / len(cuts))
        gain = gain * jnp.repeat(jnp.exp(heights), dims[dim] // shards_of).reshape((-1,) + (1,) * (len(dims) - 1 - dim))
    return gain


def gaussian(rng, extent, width, limit, cuts=(), dtype=jnp.bfloat16):
    entries = jax.random.normal(rng, extent, jnp.float32) * width
    if len(cuts) > 0:
        entries = steps_of(rng, extent, cuts, -0.22, 0.18) * entries
    return jnp.clip(entries, min=-limit, max=limit).astype(dtype)


def setup_inputs(seed: int = 0) -> dict:
    key_of = jax.random.split(jax.random.key(seed), 10)
    return {
        "tokens": draw_tokens(jax.random.fold_in(key_of[9], 71), 0),
        "cotangent": gaussian(key_of[1], (LEVELS, NLAT, NLON, D), 1.0, 6.0, ((1, 8), (2, 16))),
        "ln1_gain": jnp.clip(1.0 + 0.18 * jax.random.normal(key_of[2], (D,), jnp.float32), 0.1, 1.9),
        "w_qkv": gaussian(key_of[3], (D, 3 * D), D ** -0.5, 0.4375),
        "w_proj": gaussian(key_of[4], (D, D), D ** -0.5, 0.4375),
        "ln2_gain": jnp.clip(1.0 + 0.18 * jax.random.normal(key_of[5], (D,), jnp.float32), 0.1, 1.9),
        "w_up": gaussian(key_of[6], (D, MLP_WIDTH), D ** -0.5, 0.4375),
        "w_down": gaussian(key_of[7], (MLP_WIDTH, D), MLP_WIDTH ** -0.5, 0.21875),
        "bias_table": draw_bias_table(jax.random.fold_in(key_of[9], 71), 0),
    }


def mult(formula, left_op, right_op):
    return jnp.einsum(formula, left_op.astype(jnp.float32), right_op.astype(jnp.float32), precision=lax.Precision.HIGHEST)

def rounded(values_in):
    return lax.optimization_barrier(values_in.astype(jnp.bfloat16))

def layer_norm(values_in, gain_in):
    mean_val = lax.optimization_barrier(jnp.mean(values_in, axis=-1, keepdims=True))
    centred = values_in - mean_val
    variance = lax.optimization_barrier(jnp.mean(centred * centred, axis=-1, keepdims=True))
    return centred * lax.rsqrt(variance + 1e-05) * gain_in

def window_bias(bias_rows):
    band_count, head_count, _ = bias_rows.shape
    levels_in = LEVELS
    offsets = 2 * WIN_LON - 1
    bias_grid = bias_rows.reshape(band_count, head_count, levels_in, levels_in, WIN_LAT, WIN_LAT, offsets)
    lon_from = jnp.arange(WIN_LON).astype(jnp.int32)
    gap_idx = lon_from[:, None] - lon_from[None, :] + WIN_LON - 1
    onehot = (gap_idx[None, :, :] == jnp.arange(offsets).astype(jnp.int32)[:, None, None]).astype(jnp.float32)
    spread = mult('rhyzabd,dio->rhyzabio', bias_grid, onehot)
    window_len = levels_in * WIN_LAT * WIN_LON
    return spread.transpose(0, 1, 2, 4, 6, 3, 5, 7).reshape(band_count, head_count, window_len, window_len)

def window_mask(row_start, nlat_in, band_count, levels_in):
    inner_rows = jnp.arange(levels_in * WIN_LAT * WIN_LON).astype(jnp.int32) // WIN_LON % WIN_LAT
    row_index = row_start + jnp.arange(band_count).astype(jnp.int32)[:, None] * WIN_LAT + inner_rows[None, :]
    late_rows = row_index >= nlat_in - WIN_LAT // 2
    same_group = late_rows[:, :, None] == late_rows[:, None, :]
    return jnp.where(same_group, 0.0, -1000000000.0).astype(jnp.float32)

def attn_half(block_x, norm_gain, qkv_float, proj_float, bias_rows, row_start, nlat_in):
    levels_in, rows_in, cols_in, width_in = block_x.shape
    head_count = bias_rows.shape[1]
    head_size = width_in // head_count
    band_count = rows_in // WIN_LAT
    across_count = cols_in // WIN_LON
    window_len = levels_in * WIN_LAT * WIN_LON
    wide_x = block_x.astype(jnp.float32)
    normed = rounded(layer_norm(wide_x, norm_gain))
    windows = normed.reshape(levels_in, band_count, WIN_LAT, across_count, WIN_LON, width_in)
    windows = windows.transpose(1, 3, 0, 2, 4, 5).reshape(band_count, across_count, window_len, width_in)
    packed = rounded(mult('rctd,de->rcte', windows, qkv_float))
    packed = packed.reshape(band_count, across_count, window_len, 3, head_count, head_size)
    query_rows = packed[:, :, :, 0]
    key_rows = packed[:, :, :, 1]
    value_rows = packed[:, :, :, 2]
    scores = mult('rcqhe,rckhe->rchqk', query_rows, key_rows) * head_size ** (-0.5)
    scores = scores + window_bias(bias_rows)[:, None]
    scores = scores + window_mask(row_start, nlat_in, band_count, levels_in)[:, None, None]
    probs = rounded(jax.nn.softmax(scores, axis=-1))
    mixed_heads = rounded(mult('rchqk,rckhe->rcqhe', probs, value_rows))
    mixed_heads = mixed_heads.reshape(band_count, across_count, window_len, width_in)
    output = mult('rctd,de->rcte', mixed_heads, proj_float)
    output = output.reshape(band_count, across_count, levels_in, WIN_LAT, WIN_LON, width_in)
    output = output.transpose(2, 0, 3, 1, 4, 5).reshape(levels_in, rows_in, cols_in, width_in)
    return wide_x + output

def mlp_half(hidden_x, norm_gain, up_float, down_float):
    normed = rounded(layer_norm(hidden_x, norm_gain))
    activated = rounded(jax.nn.gelu(mult('zrcd,df->zrcf', normed, up_float), approximate=False))
    return hidden_x + mult('zrcf,fd->zrcd', activated, down_float)

def reference(tokens, cotangent, ln1_gain, w_qkv, w_proj, ln2_gain, w_up, w_down, bias_table):

    def forward(tokens_in, gain_one, qkv_float, proj_float, gain_two, up_float, down_float, table_in):
        width_in = tokens_in.shape[3]
        shifted = jnp.roll(tokens_in, (-(WIN_LAT // 2), -(WIN_LON // 2)), axis=(1, 2))
        groups = shifted.reshape(LEVELS, TYPES, WIN_LAT, NLON, width_in).transpose(1, 0, 2, 3, 4)
        starts = (jnp.arange(TYPES) * WIN_LAT).astype(jnp.int32)

        def one_group(pieces):
            block_x, bias_row, row_start = pieces
            hidden_x = attn_half(block_x, gain_one, qkv_float, proj_float, bias_row[None], row_start, NLAT)
            return mlp_half(hidden_x, gain_two, up_float, down_float).astype(jnp.bfloat16)
        result = lax.map(jax.checkpoint(one_group), (groups, table_in, starts))
        result = result.transpose(1, 0, 2, 3, 4).reshape(tokens_in.shape)
        return jnp.roll(result, (WIN_LAT // 2, WIN_LON // 2), axis=(1, 2))
    result, pull_back = jax.vjp(forward, tokens, ln1_gain, w_qkv.astype(jnp.float32), w_proj.astype(jnp.float32), ln2_gain, w_up.astype(jnp.float32), w_down.astype(jnp.float32), bias_table)
    grads = pull_back(cotangent)
    grad_scale = 1.0 / math.sqrt(TOKENS)
    return (grads[0], grads[1] * grad_scale, grads[2] * grad_scale, grads[3] * grad_scale, grads[4] * grad_scale, grads[5] * grad_scale, grads[6] * grad_scale, grads[7])
```

```python
import functools
import math

import jax
import jax.numpy as jnp
import numpy as np
from jax import lax
from jax.experimental import pallas as pl
from jax.experimental.pallas import tpu as pltpu
from jax.sharding import Mesh
from jax.sharding import PartitionSpec as P

BF = jnp.bfloat16
F32 = jnp.float32
D = 192
HEADS = 6
DH = 32
MLP = 768
WIN_LAT = 6
WIN_LON = 12
HALF_LAT = 3
HALF_LON = 6
RA = 12
WIN = 144
COLS = 48
WINDOWS = 4
OFFS = 2 * WIN_LON - 1
SPAN = OFFS * RA
SCALE = DH ** (-0.5)
W_CHUNKS = 54
B_CHUNKS = 5
VMEM = 56 * 1024 * 1024

LON = ("y", "zh", "c")
LAT = ("zl", "x")
CHIPS = ("y", "zh", "zl", "x")


def nn(a, b):
    return lax.dot_general(a, b, (((1,), (0,)), ((), ())), preferred_element_type=F32)


def nt(a, b):
    return lax.dot_general(a, b, (((1,), (1,)), ((), ())), preferred_element_type=F32)


def tn(a, b):
    return lax.dot_general(a, b, (((0,), (0,)), ((), ())), preferred_element_type=F32)


def put_rows(dst, start, count, rows):
    rows = rows.astype(F32)
    spare = jnp.zeros((count, 256 - D), F32)
    dst[0, pl.ds(start, count, stride=RA), :] = rows[:, :128]
    dst[1, pl.ds(start, count, stride=RA), :] = jnp.concatenate((rows[:, 128:], spare), axis=1)


def get_rows(src, start, count):
    low = src[0, pl.ds(start, count, stride=RA), :]
    high = src[1, pl.ds(start, count, stride=RA), :]
    return jnp.concatenate((low, high[:, : D - 128]), axis=1).astype(BF)


def window_rows(src, base):
    return jnp.concatenate((src[0, pl.ds(base, WIN), :], src[1, pl.ds(base, WIN), : D - 128]), axis=1)


def norm_stats(values):
    mean = jnp.mean(values, axis=-1, keepdims=True)
    centred = values - mean
    variance = jnp.mean(centred * centred, axis=-1, keepdims=True)
    rstd = lax.rsqrt(variance + 1e-05)
    return centred * rstd, rstd


def norm_back(d_hat, hat, rstd):
    m1 = jnp.mean(d_hat, axis=-1, keepdims=True)
    m2 = jnp.mean(d_hat * hat, axis=-1, keepdims=True)
    return rstd * (d_hat - m1 - hat * m2)


def block_kernel(
    ids, x_ref, dy_ref, na_ref, nb_ref, nc_ref, g1_ref, wqkv_ref, wqkvt_ref, wproj_ref, g2_ref,
    wup_ref, wdown_ref, t2_ref, perm_ref, mask_ref,
    own_ref, ga_ref, gb_ref, gc_ref, mine_ref, send_ref,
    xs, ys, gs, bias, d_bias, kblk, vblk, probs, o_t, dp_t, m_acc, qkv_acc, g_acc, dw,
):
    core = ids[0]
    last = ids[1]

    def place(ref, dst, base, own):
        for l in range(2):
            for r in range(HALF_LAT):
                if own:
                    put_rows(dst, l * 6 + r, COLS, ref[l, r + HALF_LAT])
                else:
                    put_rows(dst, l * 6 + r + HALF_LAT, COLS, ref[base + l, r])

    def place_east(ref, dst, base, shift):
        for l in range(2):
            for r in range(HALF_LAT):
                put_rows(dst, COLS * RA + l * 6 + r + shift, HALF_LON, ref[base + l, r])

    place(x_ref, xs, 0, True)
    place(dy_ref, ys, 0, True)
    place(na_ref, xs, 0, False)
    place(na_ref, ys, 2, False)
    place_east(nb_ref, xs, 0, 0)
    place_east(nb_ref, ys, 2, 0)
    place_east(nc_ref, xs, 0, HALF_LAT)
    place_east(nc_ref, ys, 2, HALF_LAT)

    t2 = t2_ref[...]
    hi = t2.astype(BF)
    rest = t2 - hi.astype(F32)
    mid = rest.astype(BF)
    low = (rest - mid.astype(F32)).astype(BF)
    perm = perm_ref[...]
    wide = nn(hi, perm) + nn(mid, perm) + nn(low, perm)
    mask_rows = mask_ref[...] * last.astype(F32)
    for oi in range(WIN_LON):
        start = (WIN_LON - 1 - oi) * RA
        piece = wide[:, start : start + WIN]
        for h in range(HEADS):
            bias[h, oi * RA : (oi + 1) * RA, :] = piece[h * RA : (h + 1) * RA, :]
    for h in range(HEADS):
        bias[h] = bias[h] + mask_rows
    d_bias[...] = jnp.zeros_like(d_bias)
    kblk[...] = jnp.zeros_like(kblk)
    vblk[...] = jnp.zeros_like(vblk)
    m_acc[...] = jnp.zeros_like(m_acc)
    qkv_acc[...] = jnp.zeros_like(qkv_acc)
    g_acc[...] = jnp.zeros_like(g_acc)
    dw[...] = jnp.zeros_like(dw)
    gs[:, : HALF_LON * RA, :] = jnp.zeros((2, HALF_LON * RA, 128), F32)

    g1 = g1_ref[...]
    g2 = g2_ref[...]

    def window(w, carry):
        base = pl.multiple_of(HALF_LON * RA + w * WIN, 8)
        x = window_rows(xs, base)
        dy = window_rows(ys, base)
        hat1, rstd1 = norm_stats(x)
        n1 = (hat1 * g1).astype(BF)
        qn = nn(n1, wqkv_ref[:, :D]).astype(BF)
        packed_t = nt(wqkvt_ref[...], n1).astype(BF)
        q_t = packed_t[:D]
        k_t = packed_t[D : 2 * D]
        v_t = packed_t[2 * D :]
        for h in range(HEADS):
            rows = slice(h * DH, (h + 1) * DH)
            kblk[h, rows, :] = k_t[rows]
            vblk[h, rows, :] = v_t[rows]
        for h in range(HEADS):
            rows = slice(h * DH, (h + 1) * DH)
            s = nn(qn, kblk[h]) * SCALE + bias[h]
            e = jnp.exp(s - jnp.max(s, axis=-1, keepdims=True))
            p = (e * (1.0 / jnp.sum(e, axis=-1, keepdims=True))).astype(BF)
            probs[h] = p
            o_t[rows, :] = nt(v_t[rows], p).astype(BF)
        mixed_t = o_t[...]
        hidden = x + tn(mixed_t, wproj_ref[...])
        hat2, rstd2 = norm_stats(hidden)
        n2 = (hat2 * g2).astype(BF)
        u = nn(n2, wup_ref[...])
        cdf = 0.5 + 0.5 * lax.erf(u * (0.5**0.5))
        act = (u * cdf).astype(BF)
        slope = cdf + u * jnp.exp(-0.5 * u * u) * (1.0 / math.sqrt(2.0 * math.pi))
        dyb = dy.astype(BF)
        d_act = nt(dyb, wdown_ref[...]).astype(BF).astype(F32)
        d_u = (d_act * slope).astype(BF)
        m_acc[2 * D :, :] += tn(dyb, act)
        m_acc[D : 2 * D, :] += tn(n2, d_u)
        d_n2 = nt(d_u, wup_ref[...]).astype(BF).astype(F32)
        g_acc[1:2, :D] += jnp.sum(d_n2 * hat2, axis=0, keepdims=True)
        d_hidden = dy + norm_back(d_n2 * g2, hat2, rstd2)
        dhb = d_hidden.astype(BF)
        m_acc[:D, 3 * D :] += nn(mixed_t, dhb)
        do_n = nt(dhb, wproj_ref[...]).astype(BF)
        do_t = nt(wproj_ref[...], dhb).astype(BF)
        for h in range(HEADS):
            rows = slice(h * DH, (h + 1) * DH)
            p = probs[h]
            pf = p.astype(F32)
            dp = nn(do_n, vblk[h])
            prod = pf * dp
            ds = prod - pf * jnp.sum(prod, axis=-1, keepdims=True)
            d_bias[h] = d_bias[h] + ds
            dsb = ds.astype(BF)
            dp_t[rows, :] = (nt(k_t[rows], dsb) * SCALE).astype(BF)
            dp_t[D + h * DH : D + (h + 1) * DH, :] = (nn(q_t[rows], dsb) * SCALE).astype(BF)
            dp_t[2 * D + h * DH : 2 * D + (h + 1) * DH, :] = nn(do_t[rows], p).astype(BF)
        d_packed_t = dp_t[...]
        qkv_acc[...] += nn(d_packed_t, n1)
        d_n1 = nn(wqkv_ref[...], d_packed_t).T.astype(BF).astype(F32)
        g_acc[0:1, :D] += jnp.sum(d_n1 * hat1, axis=0, keepdims=True)
        d_x = d_hidden + norm_back(d_n1 * g1, hat1, rstd1)
        gs[0, pl.ds(base, WIN), :] = d_x[:, :128]
        gs[1, pl.ds(base, WIN), : D - 128] = d_x[:, 128:]
        return carry

    lax.fori_loop(0, WINDOWS, window, 0)

    for l in range(2):
        for r in range(HALF_LAT):
            own_ref[l, r] = get_rows(gs, l * 6 + r, COLS)
            ga_ref[l, r] = get_rows(gs, l * 6 + r + HALF_LAT, COLS)
            gb_ref[l, r] = get_rows(gs, COLS * RA + l * 6 + r, HALF_LON)
            gc_ref[l, r] = get_rows(gs, COLS * RA + l * 6 + r + HALF_LAT, HALF_LON)

    for oi in range(WIN_LON):
        start = (WIN_LON - 1 - oi) * RA
        for h in range(HEADS):
            dw[h * RA : (h + 1) * RA, start : start + WIN] += d_bias[h, oi * RA : (oi + 1) * RA, :]
    dwv = dw[: HEADS * RA, :SPAN]
    dw_hi = dwv.astype(BF)
    dw_lo = (dwv - dw_hi.astype(F32)).astype(BF)
    d_t2 = nt(dw_hi, perm) + nt(dw_lo, perm)
    dw[...] = jnp.zeros_like(dw)
    dw[: HEADS * RA, :SPAN] = d_t2

    m_acc[:D, : 3 * D] = qkv_acc[...].T

    mine_half = pl.multiple_of(core * 288, 32)
    send_half = pl.multiple_of((1 - core) * 288, 32)
    for i in range(9):
        for b in range(6):
            cols = slice(b * 128, (b + 1) * 128)
            mine_ref[i * 6 + b] = m_acc[pl.ds(mine_half + 32 * i, 32), cols].astype(BF)
            send_ref[i * 6 + b] = m_acc[pl.ds(send_half + 32 * i, 32), cols].astype(BF)
    zero = jnp.zeros((32, 128), BF)
    for ref, half in ((mine_ref, core), (send_ref, 1 - core)):
        for k in range(W_CHUNKS, 64):
            ref[k] = zero

        @pl.when(half == 0)
        def _(ref=ref):
            for k in range(5):
                ref[W_CHUNKS + k] = dw[32 * (k // 3) : 32 * (k // 3) + 32, 128 * (k % 3) : 128 * (k % 3) + 128].astype(BF)
            ref[W_CHUNKS + B_CHUNKS] = g_acc[:, :128].astype(BF)
            ref[W_CHUNKS + B_CHUNKS + 1] = g_acc[:, 128:].astype(BF)

        @pl.when(half == 1)
        def _(ref=ref):
            for k in range(5, 9):
                ref[W_CHUNKS + k - 5] = dw[32 * (k // 3) : 32 * (k // 3) + 32, 128 * (k % 3) : 128 * (k % 3) + 128].astype(BF)


def reply_kernel(ids, got_ref, out_ref):
    chip = ids[2]
    is_bias = jnp.logical_and(chip >= W_CHUNKS, chip < W_CHUNKS + B_CHUNKS).astype(F32)
    total = jnp.zeros((32, 128), F32)
    bands = []
    for lat in range(8):
        s = got_ref[lat].astype(F32)
        for j in range(1, 8):
            s = s + got_ref[j * 8 + lat].astype(F32)
        bands.append(s)
        total = total + s
    for lat in range(8):
        s = jnp.where(is_bias > 0.5, bands[lat], total).astype(BF)
        for j in range(8):
            out_ref[j * 8 + lat] = s


def finish_kernel(
    ids, a_ref, b_ref, own_ref, na_ref, nb_ref, nc_ref,
    dx_ref, dg1_ref, dqkv_ref, dproj_ref, dg2_ref, dup_ref, ddown_ref, dt_ref,
    m_acc, dw, g_acc, line, grad_scale,
):
    core = ids[0]
    a_half = pl.multiple_of(core * 288, 32)
    b_half = pl.multiple_of((1 - core) * 288, 32)
    for i in range(9):
        for b in range(6):
            cols = slice(b * 128, (b + 1) * 128)
            m_acc[pl.ds(a_half + 32 * i, 32), cols] = a_ref[i * 6 + b].astype(F32) * grad_scale
            m_acc[pl.ds(b_half + 32 * i, 32), cols] = b_ref[i * 6 + b].astype(F32) * grad_scale
    for ref, half in ((a_ref, core), (b_ref, 1 - core)):

        @pl.when(half == 0)
        def _(ref=ref):
            for k in range(5):
                dw[32 * (k // 3) : 32 * (k // 3) + 32, 128 * (k % 3) : 128 * (k % 3) + 128] = ref[W_CHUNKS + k].astype(F32)
            g_acc[:, :128] = ref[W_CHUNKS + B_CHUNKS].astype(F32) * grad_scale
            g_acc[:, 128:] = ref[W_CHUNKS + B_CHUNKS + 1].astype(F32) * grad_scale

        @pl.when(half == 1)
        def _(ref=ref):
            for k in range(5, 9):
                dw[32 * (k // 3) : 32 * (k // 3) + 32, 128 * (k % 3) : 128 * (k % 3) + 128] = ref[W_CHUNKS + k - 5].astype(F32)

    dqkv_ref[...] = m_acc[:D, : 3 * D]
    dproj_ref[...] = m_acc[:D, 3 * D :]
    dup_ref[...] = m_acc[D : 2 * D, :]
    ddown_ref[...] = m_acc[2 * D :, :].T
    dg1_ref[...] = g_acc[0:1, :D]
    dg2_ref[...] = g_acc[1:2, :D]
    for h in range(HEADS):
        for li in range(2):
            rows = dw[(h * 2 + li) * 6 : (h * 2 + li) * 6 + 6, :]
            for lj in range(2):
                dt_ref[h, li, lj] = rows[:, lj * 138 : (lj + 1) * 138]

    for l in range(2):
        for r in range(HALF_LAT):
            line[...] = own_ref[l, r].astype(F32)
            line[:HALF_LON, :] = nb_ref[l, r].astype(F32)
            dx_ref[l, r + HALF_LAT] = line[...].astype(BF)
            line[...] = na_ref[l, r].astype(F32)
            line[:HALF_LON, :] = nc_ref[l, r].astype(F32)
            dx_ref[l, r] = line[...].astype(BF)


def diagonal_order():
    perm = np.zeros((SPAN, SPAN), np.float32)
    for lj in range(2):
        for aj in range(6):
            for d in range(OFFS):
                perm[(lj * 6 + aj) * OFFS + d, (OFFS - 1 - d) * RA + lj * 6 + aj] = 1.0
    return perm


def wrap_rows():
    late = (np.arange(WIN) % WIN_LAT) >= HALF_LAT
    return np.where(late[:, None] == late[None, :], 0.0, -1e9).astype(np.float32)


def shift_pairs(lon_by, lat_by):
    pairs = []
    for lon in range(16):
        for lat in range(8):
            pairs.append((lon * 8 + lat, ((lon + lon_by) % 16) * 8 + (lat + lat_by) % 8))
    return pairs


def one_axis(length, by):
    return [(i, (i + by) % length) for i in range(length)]


def vmem_spec():
    return pl.BlockSpec(memory_space=pltpu.VMEM)


def smem_spec():
    return pl.BlockSpec(memory_space=pltpu.SMEM)


def local(tokens, cotangent, ln1_gain, w_qkv, w_proj, ln2_gain, w_up, w_down, bias_table):
    core = lax.axis_index("c")
    lat = lax.axis_index(LAT)
    chip = lax.axis_index(CHIPS)
    ids = jnp.stack([core, (lat == 7).astype(jnp.int32), chip]).astype(jnp.int32)
    both = (tokens, cotangent)
    part_a = jnp.concatenate([t[:, :HALF_LAT] for t in both], axis=0)
    part_b = jnp.concatenate([t[:, HALF_LAT:, :HALF_LON] for t in both], axis=0)
    part_c = jnp.concatenate([t[:, :HALF_LAT, :HALF_LON] for t in both], axis=0)
    na = lax.ppermute(part_a, LAT, one_axis(8, -1))
    nb = lax.ppermute(part_b, LON, one_axis(16, -1))
    nc = lax.ppermute(part_c, LON + LAT, shift_pairs(-1, -1))

    t2 = bias_table.reshape(HEADS, 2, 2, 6, 6 * OFFS).transpose(0, 1, 3, 2, 4).reshape(HEADS * RA, SPAN)
    shape = jax.ShapeDtypeStruct
    own, ga, gb, gc, mine, send = pl.pallas_call(
        block_kernel,
        out_shape=(
            shape((2, HALF_LAT, COLS, D), BF),
            shape((2, HALF_LAT, COLS, D), BF),
            shape((2, HALF_LAT, HALF_LON, D), BF),
            shape((2, HALF_LAT, HALF_LON, D), BF),
            shape((64, 32, 128), BF),
            shape((64, 32, 128), BF),
        ),
        in_specs=[smem_spec()] + [vmem_spec()] * 15,
        out_specs=[vmem_spec()] * 6,
        scratch_shapes=[
            pltpu.VMEM((2, 54 * RA, 128), F32),
            pltpu.VMEM((2, 54 * RA, 128), F32),
            pltpu.VMEM((2, 54 * RA, 128), F32),
            pltpu.VMEM((HEADS, WIN, WIN), F32),
            pltpu.VMEM((HEADS, WIN, WIN), F32),
            pltpu.VMEM((HEADS, D, WIN), BF),
            pltpu.VMEM((HEADS, D, WIN), BF),
            pltpu.VMEM((HEADS, WIN, WIN), BF),
            pltpu.VMEM((D, WIN), BF),
            pltpu.VMEM((3 * D, WIN), BF),
            pltpu.VMEM((3 * D, MLP), F32),
            pltpu.VMEM((3 * D, D), F32),
            pltpu.VMEM((32, 256), F32),
            pltpu.VMEM((96, 384), F32),
        ],
        compiler_params=pltpu.CompilerParams(vmem_limit_bytes=VMEM),
    )(
        ids, tokens, cotangent, na, nb, nc, ln1_gain.reshape(1, D), w_qkv, w_qkv.T, w_proj, ln2_gain.reshape(1, D),
        w_up, w_down, t2, jnp.asarray(diagonal_order(), BF), jnp.asarray(wrap_rows()),
    )

    back_a = lax.ppermute(ga, LAT, one_axis(8, 1))
    back_b = lax.ppermute(gb, LON, one_axis(16, 1))
    back_c = lax.ppermute(gc, LON + LAT, shift_pairs(1, 1))
    pair = [(0, 1), (1, 0)]
    got = lax.ppermute(send, "c", pair)
    summed = (mine.astype(F32) + got.astype(F32)).astype(BF)
    spread = lax.all_to_all(summed, CHIPS, 0, 0, tiled=True)
    reply = pl.pallas_call(
        reply_kernel,
        out_shape=shape((64, 32, 128), BF),
        in_specs=[smem_spec(), vmem_spec()],
        out_specs=vmem_spec(),
        compiler_params=pltpu.CompilerParams(vmem_limit_bytes=VMEM),
    )(ids, spread)
    half_a = lax.all_to_all(reply, CHIPS, 0, 0, tiled=True)
    half_b = lax.ppermute(half_a, "c", pair)
    total_tokens = 128 * tokens.shape[0] * tokens.shape[1] * tokens.shape[2]
    dx, dg1, dqkv, dproj, dg2, dup, ddown, dt = pl.pallas_call(
        functools.partial(finish_kernel, grad_scale=1.0 / math.sqrt(total_tokens)),
        out_shape=(
            shape(tokens.shape, BF),
            shape((1, D), F32),
            shape((D, 3 * D), F32),
            shape((D, D), F32),
            shape((1, D), F32),
            shape((D, MLP), F32),
            shape((MLP, D), F32),
            shape((HEADS, 2, 2, 6, 6 * OFFS), F32),
        ),
        in_specs=[smem_spec()] + [vmem_spec()] * 6,
        out_specs=[vmem_spec()] * 8,
        scratch_shapes=[
            pltpu.VMEM((3 * D, MLP), F32),
            pltpu.VMEM((96, 384), F32),
            pltpu.VMEM((32, 256), F32),
            pltpu.VMEM((COLS, D), F32),
        ],
        compiler_params=pltpu.CompilerParams(vmem_limit_bytes=VMEM),
    )(ids, half_a, half_b, own, back_a, back_b, back_c)
    return (
        dx,
        dg1.reshape(D),
        dqkv,
        dproj,
        dg2.reshape(D),
        dup,
        ddown,
        dt.reshape(1, HEADS, 4 * 6 * 6 * OFFS),
    )


def solution(mesh):
    parts = Mesh(mesh.devices.reshape(4, 2, 2, 2, 4), ("y", "zh", "c", "zl", "x"))
    grid = P(None, LAT, LON, None)
    in_specs = (grid, grid, P(), P(), P(), P(), P(), P(), P(LAT, None, None))
    out_specs = (grid, P(), P(), P(), P(), P(), P(), P(LAT, None, None))
    return jax.shard_map(local, mesh=parts, in_specs=in_specs, out_specs=out_specs, check_vma=False)
```

```python
import functools
import math

import jax
import jax.numpy as jnp
from jax import lax
from jax.experimental import pallas as pl
from jax.experimental.pallas import tpu as pltpu
from jax.sharding import Mesh
from jax.sharding import PartitionSpec as P

BF = jnp.bfloat16
F32 = jnp.float32
D = 192
HEADS = 6
DH = 32
MLP = 768
WIN_LAT = 6
WIN_LON = 12
HALF_LAT = 3
HALF_LON = 6
RA = 12
WIN = 144
COLS = 48
WINDOWS = 4
OFFS = 2 * WIN_LON - 1
SPAN = OFFS * RA
LINE = WIN_LAT * OFFS
POSITIONS = 4 * WIN_LAT * LINE
SCALE = DH ** (-0.5)
W_CHUNKS = 54
B_CHUNKS = 5
VMEM = 24 * 1024 * 1024
LOG2E = 1.0 / math.log(2.0)
UNROLL = True
TOK = WINDOWS * WIN

LON = ("y", "zh", "c")
LAT = ("zl", "x")
CHIPS = ("y", "zh", "zl", "x")


def nn(a, b):
    return lax.dot_general(a, b, (((1,), (0,)), ((), ())), preferred_element_type=F32)


def nt(a, b):
    return lax.dot_general(a, b, (((1,), (1,)), ((), ())), preferred_element_type=F32)


def tn(a, b):
    return lax.dot_general(a, b, (((0,), (0,)), ((), ())), preferred_element_type=F32)


def put_rows(dst, start, count, rows):
    rows = rows.astype(F32)
    spare = jnp.zeros((count, 256 - D), F32)
    dst[0, pl.ds(start, count, stride=RA), :] = rows[:, :128]
    dst[1, pl.ds(start, count, stride=RA), :] = jnp.concatenate((rows[:, 128:], spare), axis=1)


def put_pair(xs, ys, start, count, ref, l, r):
    pair = ref[l, r, 2].astype(F32)
    rows = pl.ds(start, count, stride=RA)
    xs[0, rows, :] = ref[l, r, 0].astype(F32)
    ys[0, rows, :] = ref[l, r, 1].astype(F32)
    xs[1, rows, :] = pair
    ys[1, rows, :] = pltpu.roll(pair, 64, 1)


def take_pair(src, out, r, first, second, count):
    first = pl.ds(first, count, stride=RA)
    second = pl.ds(second, count, stride=RA)
    out[r, 0] = src[0, first, :].astype(BF)
    out[r, 1] = src[0, second, :].astype(BF)
    lane = lax.broadcasted_iota(jnp.int32, (count, 128), 1)
    out[r, 2] = jnp.where(lane < 64, src[1, first, :], pltpu.roll(src[1, second, :], 64, 1)).astype(BF)


def open_pair(ref, r):
    pair = ref[r, 2].astype(F32)
    return (
        jnp.concatenate((ref[r, 0].astype(F32), pair[:, :64]), axis=1),
        jnp.concatenate((ref[r, 1].astype(F32), pair[:, 64:]), axis=1),
    )


def get_rows(src, start, count):
    low = src[0, pl.ds(start, count, stride=RA), :]
    high = src[1, pl.ds(start, count, stride=RA), :]
    return jnp.concatenate((low, high[:, : D - 128]), axis=1).astype(BF)


def token_rows(src, start, count):
    return jnp.concatenate((src[0, start : start + count, :], src[1, start : start + count, : D - 128]), axis=1)


def each_window(body):
    if UNROLL:
        for w in range(WINDOWS):
            body(w)
    else:
        pl.loop(0, WINDOWS)(body)


def norm_stats(values):
    mean = jnp.mean(values, axis=-1, keepdims=True)
    centred = values - mean
    variance = jnp.mean(centred * centred, axis=-1, keepdims=True)
    rstd = lax.rsqrt(variance + 1e-05)
    return centred * rstd, rstd


def gelu_pair(u):
    cdf = 0.5 + 0.5 * lax.erf(u * (0.5**0.5))
    slope = cdf + u * jnp.exp(-0.5 * u * u) * (1.0 / math.sqrt(2.0 * math.pi))
    return u * cdf, slope


def norm_back(d_hat, hat, rstd):
    m1 = jnp.mean(d_hat, axis=-1, keepdims=True)
    m2 = jnp.mean(d_hat * hat, axis=-1, keepdims=True)
    return rstd * (d_hat - m1 - hat * m2)


def pack_kernel(both_ref, pa_ref, pb_ref, pc_ref):
    def pack(out, l, r, row, count):
        x = both_ref[l, row].astype(F32)[:count]
        dy = both_ref[2 + l, row].astype(F32)[:count]
        out[l, r, 0] = x[:, :128].astype(BF)
        out[l, r, 1] = dy[:, :128].astype(BF)
        out[l, r, 2] = jnp.concatenate((x[:, 128:], dy[:, 128:]), axis=1).astype(BF)

    for l in range(2):
        for r in range(HALF_LAT):
            pack(pa_ref, l, r, r, COLS)
            pack(pb_ref, l, r, r + HALF_LAT, HALF_LON)
            pack(pc_ref, l, r, r, HALF_LON)


def diagonal_order():
    row = lax.broadcasted_iota(jnp.int32, (SPAN, SPAN), 0)
    col = lax.broadcasted_iota(jnp.int32, (SPAN, SPAN), 1)
    step = lax.shift_right_logical(col * 5462, 16)
    return jnp.where(row == (col - step * RA) * OFFS + OFFS - 1 - step, 1.0, 0.0).astype(BF)


def prepare_kernel(table_ref, w_ref, bias_ref, wqkvt_ref, table, lines, rows_first):
    last = lax.axis_index(LAT) == lax.axis_size(LAT) - 1
    wqkvt_ref[...] = w_ref[:, : 3 * D].T
    for h in range(HEADS):
        lines[h : h + 1, :] = table_ref[h]
    table[...] = jnp.zeros_like(table)
    for li in range(2):
        for ai in range(WIN_LAT):
            place = li * WIN_LAT + ai
            parts = []
            for lj in range(2):
                off = ((li * 2 + lj) * WIN_LAT + ai) * LINE
                parts.append(lines[:, off : off + LINE])
            parts.append(jnp.zeros((8, 384 - SPAN), F32))
            both = jnp.concatenate(parts, axis=1)
            for b in range(3):
                table[b, place * 8 : place * 8 + 8, :] = both[:, 128 * b : 128 * (b + 1)]
    t2 = jnp.concatenate((table[0], table[1], table[2, :, : SPAN - 256]), axis=1)
    hi = t2.astype(BF)
    rest = t2 - hi.astype(F32)
    mid = rest.astype(BF)
    low = (rest - mid.astype(F32)).astype(BF)
    perm = diagonal_order()
    wide = (nn(hi, perm) + nn(mid, perm) + nn(low, perm)) * LOG2E
    wide = jnp.concatenate((wide, jnp.zeros((8 * RA, 384 - SPAN), F32)), axis=1)
    for b in range(3):
        table[b] = wide[:, 128 * b : 128 * (b + 1)]
    key_late = lax.rem(lax.broadcasted_iota(jnp.int32, (WIN, WIN), 0), WIN_LAT) >= HALF_LAT
    query_late = lax.rem(lax.broadcasted_iota(jnp.int32, (WIN, WIN), 1), WIN_LAT) >= HALF_LAT
    split = jnp.logical_and(key_late != query_late, last)
    mask_rows = jnp.where(split, -1e9 * LOG2E, 0.0)
    for h in range(HEADS):
        wide_h = jnp.concatenate([table[b, pl.ds(h, RA, stride=8), :] for b in range(3)], axis=1)
        for oi in range(WIN_LON):
            start = (WIN_LON - 1 - oi) * RA
            rows_first[h, oi * RA : (oi + 1) * RA, :] = wide_h[:, start : start + WIN]
    for h in range(HEADS):
        bias_ref[h] = rows_first[h].T + mask_rows


def block_kernel(
    both_ref, na_ref, nb_ref, nc_ref, w_ref, wqkvt, table_ref, bias,
    own_ref, ga_ref, gb_ref, gc_ref, dp_t, n1s, d_bias, m_mlp, proj_ref, g_acc,
    xs, ys, gs, probs, heads_t, o_t, do_t, kvs, hid,
):
    for l in range(2):
        for r in range(HALF_LAT):
            put_rows(xs, l * 6 + r, COLS, both_ref[l, r + HALF_LAT])
            put_rows(ys, l * 6 + r, COLS, both_ref[2 + l, r + HALF_LAT])
            put_pair(xs, ys, l * 6 + r + HALF_LAT, COLS, na_ref, l, r)
            put_pair(xs, ys, COLS * RA + l * 6 + r, HALF_LON, nb_ref, l, r)
            put_pair(xs, ys, COLS * RA + l * 6 + r + HALF_LAT, HALF_LON, nc_ref, l, r)

    d_bias[...] = jnp.zeros_like(d_bias)
    g_acc[...] = jnp.zeros_like(g_acc)
    gs[:, : HALF_LON * RA, :] = jnp.zeros((2, HALF_LON * RA, 128), F32)

    g1 = table_ref[HEADS][:, :D]
    g2 = table_ref[HEADS + 1][:, :D]
    w_proj = w_ref[:, 3 * D : 4 * D]
    first = HALF_LON * RA

    def alone(value, h):
        parts = []
        if h > 0:
            parts.append(jnp.zeros((h * DH, WIN), BF))
        parts.append(value)
        if h < HEADS - 1:
            parts.append(jnp.zeros(((HEADS - 1 - h) * DH, WIN), BF))
        return jnp.concatenate(parts, axis=0)

    hat1, rstd1 = norm_stats(token_rows(xs, first, TOK))
    n1 = (hat1 * g1).astype(BF)
    n1s[...] = n1
    kvs[...] = nn(n1, w_ref[:, D : 3 * D]).astype(BF)

    def attend(w):
        rows = pl.ds(w * WIN, WIN)
        heads_t[w] = nt(wqkvt[...], n1s[rows, :]).astype(BF)
        for h in range(HEADS):
            part = slice(h * DH, (h + 1) * DH)
            s = nn(kvs[rows, :D], alone(heads_t[w, part, :], h)) * (SCALE * LOG2E) + bias[h]
            e = jnp.exp2(s - jnp.max(s, axis=0, keepdims=True))
            p = (e * (1.0 / jnp.sum(e, axis=0, keepdims=True))).astype(BF)
            probs[w, h] = p
            o_t[w, part, :] = nn(heads_t[w, 2 * D + h * DH : 2 * D + (h + 1) * DH, :], p).astype(BF)
        hid[rows, :] = tn(o_t[w], w_proj)

    each_window(attend)

    hidden = token_rows(xs, first, TOK) + hid[...]
    hat2, rstd2 = norm_stats(hidden)
    n2 = (hat2 * g2).astype(BF)
    n2_t = n2.T
    dy = token_rows(ys, first, TOK)
    dyb = dy.astype(BF)
    dy_t = dyb.T
    d_n2 = jnp.zeros((TOK, D), F32)
    for j in range(3):
        cols = slice(j * 256, (j + 1) * 256)
        act, slope = gelu_pair(nn(n2, w_ref[:, 4 * D + j * 256 : 4 * D + (j + 1) * 256]))
        d_act = nn(dyb, w_ref[:, 4 * D + MLP + j * 256 : 4 * D + MLP + (j + 1) * 256]).astype(BF).astype(F32)
        d_u = (d_act * slope).astype(BF)
        m_mlp[D:, cols] = nn(dy_t, act.astype(BF)).astype(BF)
        m_mlp[:D, cols] = nn(n2_t, d_u).astype(BF)
        d_n2 = d_n2 + nt(d_u, w_ref[:, 4 * D + j * 256 : 4 * D + (j + 1) * 256])
    d_n2 = d_n2.astype(BF).astype(F32)
    g_acc[1:2, :D] = jnp.sum(d_n2 * hat2, axis=0, keepdims=True)
    d_hidden = dy + norm_back(d_n2 * g2, hat2, rstd2)
    dhb = d_hidden.astype(BF)
    hid[...] = d_hidden
    d_proj = jnp.zeros((D, D), F32)
    for w in range(WINDOWS):
        rows = slice(w * WIN, (w + 1) * WIN)
        d_proj = d_proj + nn(o_t[w], dhb[rows])
        do_t[w] = nt(w_proj, dhb[rows]).astype(BF)
    proj_ref[...] = d_proj

    def attend_back(w):
        rows = pl.ds(w * WIN, WIN)
        for h in range(HEADS):
            part = slice(h * DH, (h + 1) * DH)
            p = probs[w, h]
            dot_h = do_t[w, part, :]
            dp = nn(kvs[rows, D:], alone(dot_h, h))
            pf = p.astype(F32)
            prod = pf * dp
            ds = prod - pf * jnp.sum(prod, axis=0, keepdims=True)
            d_bias[h] = d_bias[h] + ds
            dsb = ds.astype(BF)
            q_t = heads_t[w, part, :]
            k_t = heads_t[w, D + h * DH : D + (h + 1) * DH, :]
            dp_t[w, part, :] = (nn(k_t, dsb) * SCALE).astype(BF)
            dp_t[w, D + h * DH : D + (h + 1) * DH, :] = (nt(q_t, dsb) * SCALE).astype(BF)
            dp_t[w, 2 * D + h * DH : 2 * D + (h + 1) * DH, :] = nt(dot_h, p).astype(BF)

    each_window(attend_back)

    d_n1 = []
    for w in range(WINDOWS):
        d_n1.append(nn(w_ref[:, : 3 * D], dp_t[w]).T)
    d_n1 = jnp.concatenate(d_n1, axis=0).astype(BF).astype(F32)
    hat1, rstd1 = norm_stats(token_rows(xs, first, TOK))
    g_acc[0:1, :D] = jnp.sum(d_n1 * hat1, axis=0, keepdims=True)
    d_x = hid[...] + norm_back(d_n1 * g1, hat1, rstd1)
    gs[0, first:, :] = d_x[:, :128]
    gs[1, first:, : D - 128] = d_x[:, 128:]

    for l in range(2):
        for r in range(HALF_LAT):
            own_ref[l, r] = get_rows(gs, l * 6 + r, COLS)

    for r in range(HALF_LAT):
        take_pair(gs, ga_ref, r, r + HALF_LAT, r + 6 + HALF_LAT, COLS)
        take_pair(gs, gb_ref, r, COLS * RA + r, COLS * RA + r + 6, HALF_LON)
        take_pair(gs, gc_ref, r, COLS * RA + r + HALF_LAT, COLS * RA + r + 6 + HALF_LAT, HALF_LON)


def gather_kernel(
    dp_t, n1s, d_bias_ref, m_mlp, proj_ref, g_acc,
    mine_ref, send_ref,
    m_acc, d_bias, dw, table,
):
    core = lax.axis_index("c")
    perm = diagonal_order()
    dw[...] = jnp.zeros_like(dw)
    d_qkv = jnp.zeros((3 * D, D), F32)
    for w in range(WINDOWS):
        d_qkv = d_qkv + nn(dp_t[w], n1s[w * WIN : (w + 1) * WIN, :])
    m_acc[:D, :] = jnp.concatenate((d_qkv.T, proj_ref[...]), axis=1).astype(BF)
    m_acc[D:, :] = m_mlp[...]

    for h in range(HEADS):
        d_bias[h] = d_bias_ref[h].T
    for oi in range(WIN_LON):
        start = (WIN_LON - 1 - oi) * RA
        for h in range(HEADS):
            dw[h * RA : (h + 1) * RA, start : start + WIN] += d_bias[h, oi * RA : (oi + 1) * RA, :]
    dwv = dw[:, :SPAN]
    dw_hi = dwv.astype(BF)
    dw_lo = (dwv - dw_hi.astype(F32)).astype(BF)
    d_t2 = nt(dw_hi, perm) + nt(dw_lo, perm)
    d_t2 = jnp.concatenate((d_t2, jnp.zeros((HEADS * RA, 384 - SPAN), F32)), axis=1)
    table[...] = jnp.zeros_like(table)
    for h in range(HEADS):
        for b in range(3):
            table[b, pl.ds(h, RA, stride=8), :] = d_t2[h * RA : (h + 1) * RA, 128 * b : 128 * (b + 1)]

    mine_half = pl.multiple_of(core * 288, 32)
    send_half = pl.multiple_of((1 - core) * 288, 32)
    for i in range(9):
        for b in range(6):
            cols = slice(b * 128, (b + 1) * 128)
            mine_ref[i * 6 + b] = m_acc[pl.ds(mine_half + 32 * i, 32), cols]
            send_ref[i * 6 + b] = m_acc[pl.ds(send_half + 32 * i, 32), cols]
    zero = jnp.zeros((32, 128), BF)
    for ref, half in ((mine_ref, core), (send_ref, 1 - core)):
        for k in range(W_CHUNKS, 64):
            ref[k] = zero

        @pl.when(half == 0)
        def _(ref=ref):
            for k in range(5):
                ref[W_CHUNKS + k] = table[k % 3, 32 * (k // 3) : 32 * (k // 3) + 32, :].astype(BF)
            ref[W_CHUNKS + B_CHUNKS] = g_acc[:, :128].astype(BF)
            ref[W_CHUNKS + B_CHUNKS + 1] = g_acc[:, 128:].astype(BF)

        @pl.when(half == 1)
        def _(ref=ref):
            for k in range(5, 9):
                ref[W_CHUNKS + k - 5] = table[k % 3, 32 * (k // 3) : 32 * (k // 3) + 32, :].astype(BF)


def reply_kernel(got_ref, out_ref):
    chip = lax.axis_index(CHIPS)
    is_bias = jnp.logical_and(chip >= W_CHUNKS, chip < W_CHUNKS + B_CHUNKS).astype(F32)
    total = jnp.zeros((32, 128), F32)
    bands = []
    for lat in range(8):
        s = got_ref[lat].astype(F32)
        for j in range(1, 8):
            s = s + got_ref[j * 8 + lat].astype(F32)
        bands.append(s)
        total = total + s
    for lat in range(8):
        s = jnp.where(is_bias > 0.5, bands[lat], total).astype(BF)
        for j in range(8):
            out_ref[j * 8 + lat] = s


def finish_kernel(
    a_ref, b_ref, own_ref, na_ref, nb_ref, nc_ref,
    dx_ref, dg1_ref, dqkv_ref, dproj_ref, dg2_ref, dup_ref, ddown_ref, dt_ref,
    m_acc, table, g_acc, line, lines, grad_scale,
):
    core = lax.axis_index("c")
    a_half = pl.multiple_of(core * 288, 32)
    b_half = pl.multiple_of((1 - core) * 288, 32)
    for i in range(9):
        for b in range(6):
            cols = slice(b * 128, (b + 1) * 128)
            m_acc[pl.ds(a_half + 32 * i, 32), cols] = a_ref[i * 6 + b].astype(F32) * grad_scale
            m_acc[pl.ds(b_half + 32 * i, 32), cols] = b_ref[i * 6 + b].astype(F32) * grad_scale
    for ref, half in ((a_ref, core), (b_ref, 1 - core)):

        @pl.when(half == 0)
        def _(ref=ref):
            for k in range(5):
                table[k % 3, 32 * (k // 3) : 32 * (k // 3) + 32, :] = ref[W_CHUNKS + k].astype(F32)
            g_acc[:, :128] = ref[W_CHUNKS + B_CHUNKS].astype(F32) * grad_scale
            g_acc[:, 128:] = ref[W_CHUNKS + B_CHUNKS + 1].astype(F32) * grad_scale

        @pl.when(half == 1)
        def _(ref=ref):
            for k in range(5, 9):
                table[k % 3, 32 * (k // 3) : 32 * (k // 3) + 32, :] = ref[W_CHUNKS + k - 5].astype(F32)

    dqkv_ref[...] = m_acc[:D, : 3 * D]
    dproj_ref[...] = m_acc[:D, 3 * D :]
    dup_ref[...] = m_acc[D : 2 * D, :]
    ddown_ref[...] = m_acc[2 * D :, :]
    dg1_ref[...] = g_acc[0:1, :D]
    dg2_ref[...] = g_acc[1:2, :D]
    for li in range(2):
        for ai in range(WIN_LAT):
            place = li * WIN_LAT + ai
            rows = jnp.concatenate([table[b, place * 8 : place * 8 + 8, :] for b in range(3)], axis=1)
            for lj in range(2):
                off = ((li * 2 + lj) * WIN_LAT + ai) * LINE
                lines[:, off : off + LINE] = rows[:, lj * LINE : (lj + 1) * LINE]
    for h in range(HEADS):
        dt_ref[h] = lines[h : h + 1, :]

    for r in range(HALF_LAT):
        north = open_pair(na_ref, r)
        east = open_pair(nb_ref, r)
        corner = open_pair(nc_ref, r)
        for l in range(2):
            line[...] = own_ref[l, r].astype(F32)
            line[:HALF_LON, :] = east[l]
            dx_ref[l, r + HALF_LAT] = line[...].astype(BF)
            line[...] = north[l]
            line[:HALF_LON, :] = corner[l]
            dx_ref[l, r] = line[...].astype(BF)


def shift_pairs(lon_by, lat_by):
    pairs = []
    for lon in range(16):
        for lat in range(8):
            pairs.append((lon * 8 + lat, ((lon + lon_by) % 16) * 8 + (lat + lat_by) % 8))
    return pairs


def one_axis(length, by):
    return [(i, (i + by) % length) for i in range(length)]


def vmem_spec():
    return pl.BlockSpec(memory_space=pltpu.VMEM)


def prepare(table, weights):
    shape = jax.ShapeDtypeStruct
    return pl.pallas_call(
        prepare_kernel,
        out_shape=(shape((HEADS, WIN, WIN), F32), shape((3 * D, D), BF)),
        in_specs=[vmem_spec()] * 2,
        out_specs=[vmem_spec()] * 2,
        scratch_shapes=[
            pltpu.VMEM((3, 8 * RA, 128), F32),
            pltpu.VMEM((8, POSITIONS), F32),
            pltpu.VMEM((HEADS, WIN, WIN), F32),
        ],
        compiler_params=pltpu.CompilerParams(vmem_limit_bytes=VMEM),
    )(table, weights)


def pack_halos(both):
    shape = jax.ShapeDtypeStruct
    return pl.pallas_call(
        pack_kernel,
        out_shape=(
            shape((2, HALF_LAT, 3, COLS, 128), BF),
            shape((2, HALF_LAT, 3, HALF_LON, 128), BF),
            shape((2, HALF_LAT, 3, HALF_LON, 128), BF),
        ),
        in_specs=[vmem_spec()],
        out_specs=[vmem_spec()] * 3,
        compiler_params=pltpu.CompilerParams(vmem_limit_bytes=VMEM),
    )(both)


def run_block(both, na, nb, nc, weights, w_qkv_t, table, bias):
    shape = jax.ShapeDtypeStruct
    return pl.pallas_call(
        block_kernel,
        out_shape=(
            shape((2, HALF_LAT, COLS, D), BF),
            shape((HALF_LAT, 3, COLS, 128), BF),
            shape((HALF_LAT, 3, HALF_LON, 128), BF),
            shape((HALF_LAT, 3, HALF_LON, 128), BF),
            shape((WINDOWS, 3 * D, WIN), BF),
            shape((TOK, D), BF),
            shape((HEADS, WIN, WIN), F32),
            shape((2 * D, MLP), BF),
            shape((D, D), F32),
            shape((32, 256), F32),
        ),
        in_specs=[vmem_spec()] * 8,
        out_specs=[vmem_spec()] * 10,
        scratch_shapes=[
            pltpu.VMEM((2, 54 * RA, 128), F32),
            pltpu.VMEM((2, 54 * RA, 128), F32),
            pltpu.VMEM((2, 54 * RA, 128), F32),
            pltpu.VMEM((WINDOWS, HEADS, WIN, WIN), BF),
            pltpu.VMEM((WINDOWS, 3 * D, WIN), BF),
            pltpu.VMEM((WINDOWS, D, WIN), BF),
            pltpu.VMEM((WINDOWS, D, WIN), BF),
            pltpu.VMEM((TOK, 2 * D), BF),
            pltpu.VMEM((TOK, D), F32),
        ],
        compiler_params=pltpu.CompilerParams(vmem_limit_bytes=VMEM),
    )(both, na, nb, nc, weights, w_qkv_t, table, bias)


def gather_grads(grads):
    shape = jax.ShapeDtypeStruct
    return pl.pallas_call(
        gather_kernel,
        out_shape=(shape((64, 32, 128), BF), shape((64, 32, 128), BF)),
        in_specs=[vmem_spec()] * 6,
        out_specs=[vmem_spec()] * 2,
        scratch_shapes=[
            pltpu.VMEM((3 * D, MLP), BF),
            pltpu.VMEM((HEADS, WIN, WIN), F32),
            pltpu.VMEM((HEADS * RA, 384), F32),
            pltpu.VMEM((3, 8 * RA, 128), F32),
        ],
        compiler_params=pltpu.CompilerParams(vmem_limit_bytes=VMEM),
        cost_estimate=pl.CostEstimate(flops=2 * TOK * 3 * D * D, bytes_accessed=8 * 1024 * 1024, transcendentals=0),
    )(*grads)


def local(tokens, cotangent, ln1_gain, w_qkv, w_proj, ln2_gain, w_up, w_down, bias_table):
    both = jnp.concatenate((tokens, cotangent), axis=0)
    part_a, part_b, part_c = pack_halos(both)
    na = lax.ppermute(part_a, LAT, one_axis(8, -1))
    nb = lax.ppermute(part_b, LON, one_axis(16, -1))
    nc = lax.ppermute(part_c, LON + LAT, shift_pairs(-1, -1))

    weights = jnp.concatenate((w_qkv, w_proj, w_up, w_down.T), axis=1)
    gains = jnp.pad(jnp.stack((ln1_gain, ln2_gain)), ((0, 0), (0, POSITIONS - D)))
    table = jnp.concatenate((bias_table.reshape(HEADS, 1, POSITIONS), gains[:, None]), axis=0)
    bias, w_qkv_t = prepare(table, weights)
    own, ga, gb, gc, *grads = run_block(both, na, nb, nc, weights, w_qkv_t, table, bias)

    back_a = lax.ppermute(ga, LAT, one_axis(8, 1))
    back_b = lax.ppermute(gb, LON, one_axis(16, 1))
    back_c = lax.ppermute(gc, LON + LAT, shift_pairs(1, 1))
    mine, send = gather_grads(grads)
    pair = [(0, 1), (1, 0)]
    send, back_a, back_b, back_c = lax.optimization_barrier((send, back_a, back_b, back_c))
    got = lax.ppermute(send, "c", pair)
    summed = (mine.astype(F32) + got.astype(F32)).astype(BF)
    spread = lax.all_to_all(summed, CHIPS, 0, 0, tiled=True)
    reply = pl.pallas_call(
        reply_kernel,
        out_shape=jax.ShapeDtypeStruct((64, 32, 128), BF),
        in_specs=[vmem_spec()],
        out_specs=vmem_spec(),
        compiler_params=pltpu.CompilerParams(vmem_limit_bytes=VMEM),
    )(spread)
    half_a = lax.all_to_all(reply, CHIPS, 0, 0, tiled=True)
    half_b = lax.ppermute(half_a, "c", pair)
    shape = jax.ShapeDtypeStruct
    total_tokens = 128 * tokens.shape[0] * tokens.shape[1] * tokens.shape[2]
    dx, dg1, dqkv, dproj, dg2, dup, ddown, dt = pl.pallas_call(
        functools.partial(finish_kernel, grad_scale=1.0 / math.sqrt(total_tokens)),
        out_shape=(
            shape(tokens.shape, BF),
            shape((1, D), F32),
            shape((D, 3 * D), F32),
            shape((D, D), F32),
            shape((1, D), F32),
            shape((D, MLP), F32),
            shape((D, MLP), F32),
            shape((HEADS, 1, POSITIONS), F32),
        ),
        in_specs=[vmem_spec()] * 6,
        out_specs=[vmem_spec()] * 8,
        scratch_shapes=[
            pltpu.VMEM((3 * D, MLP), F32),
            pltpu.VMEM((3, 8 * RA, 128), F32),
            pltpu.VMEM((32, 256), F32),
            pltpu.VMEM((COLS, D), F32),
            pltpu.VMEM((8, POSITIONS), F32),
        ],
        compiler_params=pltpu.CompilerParams(vmem_limit_bytes=VMEM),
    )(half_a, half_b, own, back_a, back_b, back_c)
    return (
        dx,
        dg1.reshape(D),
        dqkv,
        dproj,
        dg2.reshape(D),
        dup,
        ddown.T,
        dt.reshape(1, HEADS, POSITIONS),
    )


def solution(mesh):
    parts = Mesh(mesh.devices.reshape(4, 2, 2, 2, 4), ("y", "zh", "c", "zl", "x"))
    grid = P(None, LAT, LON, None)
    in_specs = (grid, grid, P(), P(), P(), P(), P(), P(), P(LAT, None, None))
    out_specs = (grid, P(), P(), P(), P(), P(), P(), P(LAT, None, None))
    return jax.shard_map(local, mesh=parts, in_specs=in_specs, out_specs=out_specs, check_vma=False)
```

```python
import functools
import math

import jax
import jax.numpy as jnp
from jax import lax
from jax.experimental import pallas as pl
from jax.experimental.pallas import tpu as pltpu
from jax.sharding import Mesh
from jax.sharding import PartitionSpec as P

BF = jnp.bfloat16
F32 = jnp.float32
D = 192
HEADS = 6
DH = 32
MLP = 768
WIN_LAT = 6
WIN_LON = 12
HALF_LAT = 3
HALF_LON = 6
RA = 12
WIN = 144
COLS = 48
WINDOWS = 4
OFFS = 2 * WIN_LON - 1
SPAN = OFFS * RA
LINE = WIN_LAT * OFFS
POSITIONS = 4 * WIN_LAT * LINE
SCALE = DH ** (-0.5)
W_CHUNKS = 54
HALO = 8
NORTH_AT, EAST_AT, CORNER_AT, FLAT = 0, 384, 440, 512
B_CHUNKS = 5
VMEM = 24 * 1024 * 1024
LOG2E = 1.0 / math.log(2.0)
UNROLL = True
GROUP = 2
TOK = WINDOWS * WIN

LON = ("y", "zh", "c")
LAT = ("zl", "x")
CHIPS = ("y", "zh", "zl", "x")


def nn(a, b):
    return lax.dot_general(a, b, (((1,), (0,)), ((), ())), preferred_element_type=F32)


def nt(a, b):
    return lax.dot_general(a, b, (((1,), (1,)), ((), ())), preferred_element_type=F32)


def tn(a, b):
    return lax.dot_general(a, b, (((0,), (0,)), ((), ())), preferred_element_type=F32)


def put_rows(dst, start, count, rows):
    rows = rows.astype(F32)
    spare = jnp.zeros((count, 256 - D), F32)
    dst[0, pl.ds(start, count, stride=RA), :] = rows[:, :128]
    dst[1, pl.ds(start, count, stride=RA), :] = jnp.concatenate((rows[:, 128:], spare), axis=1)


def put_pair(xs, ys, start, count, ref, l, r):
    pair = ref[l, r, 2].astype(F32)
    rows = pl.ds(start, count, stride=RA)
    xs[0, rows, :] = ref[l, r, 0].astype(F32)
    ys[0, rows, :] = ref[l, r, 1].astype(F32)
    xs[1, rows, :] = pair
    ys[1, rows, :] = pltpu.roll(pair, 64, 1)


def take_pair(src, flat, at, first, second, count):
    first = pl.ds(first, count, stride=RA)
    second = pl.ds(second, count, stride=RA)
    lane = lax.broadcasted_iota(jnp.int32, (count, 128), 1)
    flat[at : at + count, :] = src[0, first, :]
    flat[at + count : at + 2 * count, :] = src[0, second, :]
    flat[at + 2 * count : at + 3 * count, :] = jnp.where(
        lane < 64, src[1, first, :], pltpu.roll(src[1, second, :], 64, 1)
    )


def open_pair(flat, at, count):
    pair = flat[at + 2 * count : at + 3 * count, :]
    return (
        jnp.concatenate((flat[at : at + count, :], pair[:, :64]), axis=1),
        jnp.concatenate((flat[at + count : at + 2 * count, :], pair[:, 64:]), axis=1),
    )


def get_rows(src, start, count):
    low = src[0, pl.ds(start, count, stride=RA), :]
    high = src[1, pl.ds(start, count, stride=RA), :]
    return jnp.concatenate((low, high[:, : D - 128]), axis=1).astype(BF)


def token_rows(src, start, count):
    return jnp.concatenate((src[0, start : start + count, :], src[1, start : start + count, : D - 128]), axis=1)


def each_window(body):
    if UNROLL:
        for w in range(0, WINDOWS, GROUP):
            body(range(w, w + GROUP))
    else:
        pl.loop(0, WINDOWS)(body)


def norm_stats(values):
    mean = jnp.mean(values, axis=-1, keepdims=True)
    centred = values - mean
    variance = jnp.mean(centred * centred, axis=-1, keepdims=True)
    rstd = lax.rsqrt(variance + 1e-05)
    return centred * rstd, rstd


def gelu_pair(u):
    cdf = 0.5 + 0.5 * lax.erf(u * (0.5**0.5))
    slope = cdf + u * jnp.exp(-0.5 * u * u) * (1.0 / math.sqrt(2.0 * math.pi))
    return u * cdf, slope


def norm_back(d_hat, hat, rstd):
    m1 = jnp.mean(d_hat, axis=-1, keepdims=True)
    m2 = jnp.mean(d_hat * hat, axis=-1, keepdims=True)
    return rstd * (d_hat - m1 - hat * m2)


def pack_kernel(both_ref, pa_ref, pb_ref, pc_ref):
    def pack(out, l, r, row, count):
        x = both_ref[l, row].astype(F32)[:count]
        dy = both_ref[2 + l, row].astype(F32)[:count]
        out[l, r, 0] = x[:, :128].astype(BF)
        out[l, r, 1] = dy[:, :128].astype(BF)
        out[l, r, 2] = jnp.concatenate((x[:, 128:], dy[:, 128:]), axis=1).astype(BF)

    for l in range(2):
        for r in range(HALF_LAT):
            pack(pa_ref, l, r, r, COLS)
            pack(pb_ref, l, r, r + HALF_LAT, HALF_LON)
            pack(pc_ref, l, r, r, HALF_LON)


def diagonal_order():
    row = lax.broadcasted_iota(jnp.int32, (SPAN, SPAN), 0)
    col = lax.broadcasted_iota(jnp.int32, (SPAN, SPAN), 1)
    step = lax.shift_right_logical(col * 5462, 16)
    return jnp.where(row == (col - step * RA) * OFFS + OFFS - 1 - step, 1.0, 0.0).astype(BF)


def prepare_kernel(table_ref, w_ref, bias_ref, wqkvt_ref, table, lines, rows_first):
    last = lax.axis_index(LAT) == lax.axis_size(LAT) - 1
    wqkvt_ref[...] = w_ref[:, : 3 * D].T
    for h in range(HEADS):
        lines[h : h + 1, :] = table_ref[h]
    table[...] = jnp.zeros_like(table)
    for li in range(2):
        for ai in range(WIN_LAT):
            place = li * WIN_LAT + ai
            parts = []
            for lj in range(2):
                off = ((li * 2 + lj) * WIN_LAT + ai) * LINE
                parts.append(lines[:, off : off + LINE])
            parts.append(jnp.zeros((8, 384 - SPAN), F32))
            both = jnp.concatenate(parts, axis=1)
            for b in range(3):
                table[b, place * 8 : place * 8 + 8, :] = both[:, 128 * b : 128 * (b + 1)]
    t2 = jnp.concatenate((table[0], table[1], table[2, :, : SPAN - 256]), axis=1)
    hi = t2.astype(BF)
    rest = t2 - hi.astype(F32)
    mid = rest.astype(BF)
    low = (rest - mid.astype(F32)).astype(BF)
    perm = diagonal_order()
    wide = (nn(hi, perm) + nn(mid, perm) + nn(low, perm)) * LOG2E
    wide = jnp.concatenate((wide, jnp.zeros((8 * RA, 384 - SPAN), F32)), axis=1)
    for b in range(3):
        table[b] = wide[:, 128 * b : 128 * (b + 1)]
    key_late = lax.rem(lax.broadcasted_iota(jnp.int32, (WIN, WIN), 0), WIN_LAT) >= HALF_LAT
    query_late = lax.rem(lax.broadcasted_iota(jnp.int32, (WIN, WIN), 1), WIN_LAT) >= HALF_LAT
    split = jnp.logical_and(key_late != query_late, last)
    mask_rows = jnp.where(split, -1e9 * LOG2E, 0.0)
    for h in range(HEADS):
        wide_h = jnp.concatenate([table[b, pl.ds(h, RA, stride=8), :] for b in range(3)], axis=1)
        for oi in range(WIN_LON):
            start = (WIN_LON - 1 - oi) * RA
            rows_first[h, oi * RA : (oi + 1) * RA, :] = wide_h[:, start : start + WIN]
    for h in range(HEADS):
        bias_ref[h] = rows_first[h].T + mask_rows


def block_kernel(
    both_ref, na_ref, nb_ref, nc_ref, w_ref, wqkvt, table_ref, bias,
    own_ref, halo_ref, mine_ref, send_ref,
    xs, ys, gs, probs, heads_t, o_t, do_t, kvs, hid, dss,
    dp_t, n1s, d_bias, m_acc, g_acc, dw, table, flat,
):
    for l in range(2):
        for r in range(HALF_LAT):
            put_rows(xs, l * 6 + r, COLS, both_ref[l, r + HALF_LAT])
            put_rows(ys, l * 6 + r, COLS, both_ref[2 + l, r + HALF_LAT])
            put_pair(xs, ys, l * 6 + r + HALF_LAT, COLS, na_ref, l, r)
            put_pair(xs, ys, COLS * RA + l * 6 + r, HALF_LON, nb_ref, l, r)
            put_pair(xs, ys, COLS * RA + l * 6 + r + HALF_LAT, HALF_LON, nc_ref, l, r)

    d_bias[...] = jnp.zeros_like(d_bias)
    g_acc[...] = jnp.zeros_like(g_acc)
    gs[:, : HALF_LON * RA, :] = jnp.zeros((2, HALF_LON * RA, 128), F32)

    g1 = table_ref[HEADS][:, :D]
    g2 = table_ref[HEADS + 1][:, :D]
    w_proj = w_ref[:, 3 * D : 4 * D]
    first = HALF_LON * RA

    hat1, rstd1 = norm_stats(token_rows(xs, first, TOK))
    n1 = (hat1 * g1).astype(BF)
    n1s[...] = n1
    kvs[...] = nn(n1, w_ref[:, D : 3 * D]).astype(BF)

    def attend(ws):
        jobs = [(w, h) for w in ws for h in range(HEADS)]
        rows = {w: pl.ds(w * WIN, WIN) for w in ws}
        parts = [slice(h * DH, (h + 1) * DH) for h in range(HEADS)]
        scores = [
            nn(kvs[rows[w], parts[h]], heads_t[w, parts[h], :]) * (SCALE * LOG2E) + bias[h] for w, h in jobs
        ]
        tops = [jnp.max(s, axis=0, keepdims=True) for s in scores]
        powers = [jnp.exp2(s - top) for s, top in zip(scores, tops)]
        shares = [1.0 / jnp.sum(e, axis=0, keepdims=True) for e in powers]
        for k, (w, h) in enumerate(jobs):
            probs[w, h] = (powers[k] * shares[k]).astype(BF)
        for w, h in jobs:
            o_t[w, parts[h], :] = nn(heads_t[w, 2 * D + h * DH : 2 * D + (h + 1) * DH, :], probs[w, h]).astype(BF)

    for w in range(WINDOWS):
        heads_t[w] = nt(wqkvt[...], n1[w * WIN : (w + 1) * WIN]).astype(BF)
    each_window(attend)
    for w in range(WINDOWS):
        hid[w * WIN : (w + 1) * WIN, :] = tn(o_t[w], w_proj)

    hidden = token_rows(xs, first, TOK) + hid[...]
    hat2, rstd2 = norm_stats(hidden)
    n2 = (hat2 * g2).astype(BF)
    n2_t = n2.T
    dy = token_rows(ys, first, TOK)
    dyb = dy.astype(BF)
    dy_t = dyb.T
    d_n2 = jnp.zeros((TOK, D), F32)
    for j in range(3):
        cols = slice(j * 256, (j + 1) * 256)
        act, slope = gelu_pair(nn(n2, w_ref[:, 4 * D + j * 256 : 4 * D + (j + 1) * 256]))
        d_act = nn(dyb, w_ref[:, 4 * D + MLP + j * 256 : 4 * D + MLP + (j + 1) * 256]).astype(BF).astype(F32)
        d_u = (d_act * slope).astype(BF)
        m_acc[2 * D :, cols] = nn(dy_t, act.astype(BF)).astype(BF)
        m_acc[D : 2 * D, cols] = nn(n2_t, d_u).astype(BF)
        d_n2 = d_n2 + nt(d_u, w_ref[:, 4 * D + j * 256 : 4 * D + (j + 1) * 256])
    d_n2 = d_n2.astype(BF).astype(F32)
    g_acc[1:2, :D] = jnp.sum(d_n2 * hat2, axis=0, keepdims=True)
    d_hidden = dy + norm_back(d_n2 * g2, hat2, rstd2)
    dhb = d_hidden.astype(BF)
    hid[...] = d_hidden
    d_proj = jnp.zeros((D, D), F32)
    for w in range(WINDOWS):
        rows = slice(w * WIN, (w + 1) * WIN)
        d_proj = d_proj + nn(o_t[w], dhb[rows])
        do_t[w] = nt(w_proj, dhb[rows]).astype(BF)

    def attend_back(ws):
        jobs = [(w, h) for w in ws for h in range(HEADS)]
        rows = {w: pl.ds(w * WIN, WIN) for w in ws}
        parts = [slice(h * DH, (h + 1) * DH) for h in range(HEADS)]
        d_probs = [
            nn(kvs[rows[w], D + h * DH : D + (h + 1) * DH], do_t[w, parts[h], :]) for w, h in jobs
        ]
        for k, (w, h) in enumerate(jobs):
            pf = probs[w, h].astype(F32)
            prod = pf * d_probs[k]
            ds = prod - pf * jnp.sum(prod, axis=0, keepdims=True)
            d_bias[h] = d_bias[h] + ds
            dss[k] = ds.astype(BF)
        for k, (w, h) in enumerate(jobs):
            part = parts[h]
            q_t = heads_t[w, part, :]
            k_t = heads_t[w, D + h * DH : D + (h + 1) * DH, :]
            dp_t[w, part, :] = (nn(k_t, dss[k]) * SCALE).astype(BF)
            dp_t[w, D + h * DH : D + (h + 1) * DH, :] = (nt(q_t, dss[k]) * SCALE).astype(BF)
            dp_t[w, 2 * D + h * DH : 2 * D + (h + 1) * DH, :] = nt(do_t[w, part, :], probs[w, h]).astype(BF)

    each_window(attend_back)

    d_n1 = []
    for w in range(WINDOWS):
        d_n1.append(nn(w_ref[:, : 3 * D], dp_t[w]).T)
    d_n1 = jnp.concatenate(d_n1, axis=0).astype(BF).astype(F32)
    hat1, rstd1 = norm_stats(token_rows(xs, first, TOK))
    g_acc[0:1, :D] = jnp.sum(d_n1 * hat1, axis=0, keepdims=True)
    d_x = hid[...] + norm_back(d_n1 * g1, hat1, rstd1)
    gs[0, first:, :] = d_x[:, :128]
    gs[1, first:, : D - 128] = d_x[:, 128:]

    for l in range(2):
        for r in range(HALF_LAT):
            own_ref[l, r] = get_rows(gs, l * 6 + r, COLS)

    flat[...] = jnp.zeros_like(flat)
    inner = COLS - HALF_LON
    for r in range(HALF_LAT):
        late = r + HALF_LAT
        take_pair(gs, flat, NORTH_AT + r * 3 * inner, first + late, first + 6 + late, inner)
        take_pair(gs, flat, EAST_AT + r * 3 * HALF_LON, COLS * RA + r, COLS * RA + r + 6, HALF_LON)
        take_pair(gs, flat, CORNER_AT + r * 3 * HALF_LON, COLS * RA + late, COLS * RA + late + 6, HALF_LON)
    for k in range(64):
        halo_ref[k] = flat[HALO * k : HALO * (k + 1), :].astype(BF)

    core = lax.axis_index("c")
    perm = diagonal_order()
    dw[...] = jnp.zeros_like(dw)
    d_qkv = jnp.zeros((3 * D, D), F32)
    for w in range(WINDOWS):
        d_qkv = d_qkv + nn(dp_t[w], n1s[w * WIN : (w + 1) * WIN, :])
    m_acc[:D, :] = jnp.concatenate((d_qkv.T, d_proj), axis=1).astype(BF)

    for h in range(HEADS):
        d_bias[h] = d_bias[h].T
    for oi in range(WIN_LON):
        start = (WIN_LON - 1 - oi) * RA
        for h in range(HEADS):
            dw[h * RA : (h + 1) * RA, start : start + WIN] += d_bias[h, oi * RA : (oi + 1) * RA, :]
    dwv = dw[:, :SPAN]
    dw_hi = dwv.astype(BF)
    dw_lo = (dwv - dw_hi.astype(F32)).astype(BF)
    d_t2 = nt(dw_hi, perm) + nt(dw_lo, perm)
    d_t2 = jnp.concatenate((d_t2, jnp.zeros((HEADS * RA, 384 - SPAN), F32)), axis=1)
    table[...] = jnp.zeros_like(table)
    for h in range(HEADS):
        for b in range(3):
            table[b, pl.ds(h, RA, stride=8), :] = d_t2[h * RA : (h + 1) * RA, 128 * b : 128 * (b + 1)]

    mine_half = pl.multiple_of(core * 288, 32)
    send_half = pl.multiple_of((1 - core) * 288, 32)
    for i in range(9):
        for b in range(6):
            cols = slice(b * 128, (b + 1) * 128)
            mine_ref[i * 6 + b] = m_acc[pl.ds(mine_half + 32 * i, 32), cols]
            send_ref[i * 6 + b] = m_acc[pl.ds(send_half + 32 * i, 32), cols]
    zero = jnp.zeros((32, 128), BF)
    for ref, half in ((mine_ref, core), (send_ref, 1 - core)):
        for k in range(W_CHUNKS, 64):
            ref[k] = zero

        @pl.when(half == 0)
        def _(ref=ref):
            for k in range(5):
                ref[W_CHUNKS + k] = table[k % 3, 32 * (k // 3) : 32 * (k // 3) + 32, :].astype(BF)
            ref[W_CHUNKS + B_CHUNKS] = g_acc[:, :128].astype(BF)
            ref[W_CHUNKS + B_CHUNKS + 1] = g_acc[:, 128:].astype(BF)

        @pl.when(half == 1)
        def _(ref=ref):
            for k in range(5, 9):
                ref[W_CHUNKS + k - 5] = table[k % 3, 32 * (k // 3) : 32 * (k // 3) + 32, :].astype(BF)


def join_kernel(mine_ref, got_ref, halo_ref, out_ref):
    for k in range(64):
        out_ref[k, :32] = (mine_ref[k].astype(F32) + got_ref[k].astype(F32)).astype(BF)
        out_ref[k, 32:] = halo_ref[k]


def reply_kernel(got_ref, out_ref):
    relay = lax.axis_index(CHIPS)
    is_bias = jnp.logical_and(relay >= W_CHUNKS, relay < W_CHUNKS + B_CHUNKS).astype(F32)
    total = jnp.zeros((32, 128), F32)
    bands = []
    for lat in range(8):
        s = got_ref[lat, :32].astype(F32)
        for j in range(1, 8):
            s = s + got_ref[j * 8 + lat, :32].astype(F32)
        bands.append(s)
        total = total + s
    by_lat = jnp.logical_or(relay < EAST_AT // HALO, relay >= CORNER_AT // HALO).astype(jnp.int32)
    by_lon = jnp.logical_and(relay >= EAST_AT // HALO, lax.axis_index("c") == 1).astype(jnp.int32)
    for lat in range(8):
        s = jnp.where(is_bias > 0.5, bands[lat], total).astype(BF)
        from_lat = lax.rem(lat + 7 * by_lat, 8)
        for j in range(8):
            out_ref[j * 8 + lat, :32] = s
            out_ref[j * 8 + lat, 32:] = got_ref[lax.rem(j + 7 * by_lon, 8) * 8 + from_lat, 32:]


def finish_kernel(
    a_ref, b_ref, own_ref,
    dx_ref, dg1_ref, dqkv_ref, dproj_ref, dg2_ref, dup_ref, ddown_ref, dt_ref,
    m_acc, table, g_acc, line, lines, flat, grad_scale,
):
    core = lax.axis_index("c")
    a_half = pl.multiple_of(core * 288, 32)
    b_half = pl.multiple_of((1 - core) * 288, 32)
    for i in range(9):
        for b in range(6):
            cols = slice(b * 128, (b + 1) * 128)
            m_acc[pl.ds(a_half + 32 * i, 32), cols] = a_ref[i * 6 + b, :32].astype(F32) * grad_scale
            m_acc[pl.ds(b_half + 32 * i, 32), cols] = b_ref[i * 6 + b, :32].astype(F32) * grad_scale
    for ref, half in ((a_ref, core), (b_ref, 1 - core)):

        @pl.when(half == 0)
        def _(ref=ref):
            for k in range(5):
                table[k % 3, 32 * (k // 3) : 32 * (k // 3) + 32, :] = ref[W_CHUNKS + k, :32].astype(F32)
            g_acc[:, :128] = ref[W_CHUNKS + B_CHUNKS, :32].astype(F32) * grad_scale
            g_acc[:, 128:] = ref[W_CHUNKS + B_CHUNKS + 1, :32].astype(F32) * grad_scale

        @pl.when(half == 1)
        def _(ref=ref):
            for k in range(5, 9):
                table[k % 3, 32 * (k // 3) : 32 * (k // 3) + 32, :] = ref[W_CHUNKS + k - 5, :32].astype(F32)

    dqkv_ref[...] = m_acc[:D, : 3 * D]
    dproj_ref[...] = m_acc[:D, 3 * D :]
    dup_ref[...] = m_acc[D : 2 * D, :]
    ddown_ref[...] = m_acc[2 * D :, :]
    dg1_ref[...] = g_acc[0:1, :D]
    dg2_ref[...] = g_acc[1:2, :D]
    for li in range(2):
        for ai in range(WIN_LAT):
            place = li * WIN_LAT + ai
            rows = jnp.concatenate([table[b, place * 8 : place * 8 + 8, :] for b in range(3)], axis=1)
            for lj in range(2):
                off = ((li * 2 + lj) * WIN_LAT + ai) * LINE
                lines[:, off : off + LINE] = rows[:, lj * LINE : (lj + 1) * LINE]
    for h in range(HEADS):
        dt_ref[h] = lines[h : h + 1, :]

    for k in range(64):
        ref = a_ref if k < EAST_AT // HALO else b_ref
        flat[HALO * k : HALO * (k + 1), :] = ref[k, 32:].astype(F32)
    inner = COLS - HALF_LON
    for r in range(HALF_LAT):
        north = open_pair(flat, NORTH_AT + r * 3 * inner, inner)
        east = open_pair(flat, EAST_AT + r * 3 * HALF_LON, HALF_LON)
        corner = open_pair(flat, CORNER_AT + r * 3 * HALF_LON, HALF_LON)
        for l in range(2):
            line[...] = own_ref[l, r].astype(F32)
            line[:HALF_LON, :] = east[l]
            dx_ref[l, r + HALF_LAT] = line[...].astype(BF)
            line[HALF_LON:, :] = north[l]
            line[:HALF_LON, :] = corner[l]
            dx_ref[l, r] = line[...].astype(BF)


def shift_pairs(lon_by, lat_by):
    pairs = []
    for lon in range(16):
        for lat in range(8):
            pairs.append((lon * 8 + lat, ((lon + lon_by) % 16) * 8 + (lat + lat_by) % 8))
    return pairs


def one_axis(length, by):
    return [(i, (i + by) % length) for i in range(length)]


def vmem_spec():
    return pl.BlockSpec(memory_space=pltpu.VMEM)


def prepare(table, weights):
    shape = jax.ShapeDtypeStruct
    return pl.pallas_call(
        prepare_kernel,
        out_shape=(shape((HEADS, WIN, WIN), F32), shape((3 * D, D), BF)),
        in_specs=[vmem_spec()] * 2,
        out_specs=[vmem_spec()] * 2,
        scratch_shapes=[
            pltpu.VMEM((3, 8 * RA, 128), F32),
            pltpu.VMEM((8, POSITIONS), F32),
            pltpu.VMEM((HEADS, WIN, WIN), F32),
        ],
        compiler_params=pltpu.CompilerParams(vmem_limit_bytes=VMEM),
    )(table, weights)


def pack_halos(both):
    shape = jax.ShapeDtypeStruct
    return pl.pallas_call(
        pack_kernel,
        out_shape=(
            shape((2, HALF_LAT, 3, COLS, 128), BF),
            shape((2, HALF_LAT, 3, HALF_LON, 128), BF),
            shape((2, HALF_LAT, 3, HALF_LON, 128), BF),
        ),
        in_specs=[vmem_spec()],
        out_specs=[vmem_spec()] * 3,
        compiler_params=pltpu.CompilerParams(vmem_limit_bytes=VMEM),
    )(both)


def run_block(both, na, nb, nc, weights, w_qkv_t, table, bias):
    shape = jax.ShapeDtypeStruct
    return pl.pallas_call(
        block_kernel,
        out_shape=(
            shape((2, HALF_LAT, COLS, D), BF),
            shape((64, HALO, 128), BF),
            shape((64, 32, 128), BF),
            shape((64, 32, 128), BF),
        ),
        in_specs=[vmem_spec()] * 8,
        out_specs=[vmem_spec()] * 4,
        scratch_shapes=[
            pltpu.VMEM((2, 54 * RA, 128), F32),
            pltpu.VMEM((2, 54 * RA, 128), F32),
            pltpu.VMEM((2, 54 * RA, 128), F32),
            pltpu.VMEM((WINDOWS, HEADS, WIN, WIN), BF),
            pltpu.VMEM((WINDOWS, 3 * D, WIN), BF),
            pltpu.VMEM((WINDOWS, D, WIN), BF),
            pltpu.VMEM((WINDOWS, D, WIN), BF),
            pltpu.VMEM((TOK, 2 * D), BF),
            pltpu.VMEM((TOK, D), F32),
            pltpu.VMEM((WINDOWS * HEADS, WIN, WIN), BF),
            pltpu.VMEM((WINDOWS, 3 * D, WIN), BF),
            pltpu.VMEM((TOK, D), BF),
            pltpu.VMEM((HEADS, WIN, WIN), F32),
            pltpu.VMEM((3 * D, MLP), BF),
            pltpu.VMEM((32, 256), F32),
            pltpu.VMEM((HEADS * RA, 384), F32),
            pltpu.VMEM((3, 8 * RA, 128), F32),
            pltpu.VMEM((FLAT, 128), F32),
        ],
        compiler_params=pltpu.CompilerParams(vmem_limit_bytes=VMEM),
    )(both, na, nb, nc, weights, w_qkv_t, table, bias)


def local(tokens, cotangent, ln1_gain, w_qkv, w_proj, ln2_gain, w_up, w_down, bias_table):
    edge = ((0, 0),) * 3
    both = jnp.pad(tokens, ((0, 2),) + edge) + jnp.pad(cotangent, ((2, 0),) + edge)
    part_a, part_b, part_c = pack_halos(both)
    na = lax.ppermute(part_a, LAT, one_axis(8, -1))
    nb = lax.ppermute(part_b, LON, one_axis(16, -1))
    nc = lax.ppermute(part_c, LON + LAT, shift_pairs(-1, -1))

    weights = jnp.concatenate((w_qkv, w_proj, w_up, w_down.T), axis=1)
    gains = jnp.pad(jnp.stack((ln1_gain, ln2_gain)), ((0, 0), (0, POSITIONS - D)))
    table = jnp.concatenate((bias_table.reshape(HEADS, 1, POSITIONS), gains[:, None]), axis=0)
    bias, w_qkv_t = prepare(table, weights)
    own, halo, mine, send = run_block(both, na, nb, nc, weights, w_qkv_t, table, bias)

    pair = [(0, 1), (1, 0)]
    got = lax.ppermute(send, "c", pair)
    chunks = jax.ShapeDtypeStruct((64, 32 + HALO, 128), BF)
    joined = pl.pallas_call(
        join_kernel,
        out_shape=chunks,
        in_specs=[vmem_spec()] * 3,
        out_specs=vmem_spec(),
        compiler_params=pltpu.CompilerParams(vmem_limit_bytes=VMEM),
    )(mine, got, halo)
    spread = lax.all_to_all(joined, CHIPS, 0, 0, tiled=True)
    reply = pl.pallas_call(
        reply_kernel,
        out_shape=chunks,
        in_specs=[vmem_spec()],
        out_specs=vmem_spec(),
        compiler_params=pltpu.CompilerParams(vmem_limit_bytes=VMEM),
    )(spread)
    half_a = lax.all_to_all(reply, CHIPS, 0, 0, tiled=True)
    half_b = lax.ppermute(half_a, "c", pair)
    shape = jax.ShapeDtypeStruct
    total_tokens = 128 * tokens.shape[0] * tokens.shape[1] * tokens.shape[2]
    dx, dg1, dqkv, dproj, dg2, dup, ddown, dt = pl.pallas_call(
        functools.partial(finish_kernel, grad_scale=1.0 / math.sqrt(total_tokens)),
        out_shape=(
            shape(tokens.shape, BF),
            shape((1, D), F32),
            shape((D, 3 * D), F32),
            shape((D, D), F32),
            shape((1, D), F32),
            shape((D, MLP), F32),
            shape((D, MLP), F32),
            shape((HEADS, 1, POSITIONS), F32),
        ),
        in_specs=[vmem_spec()] * 3,
        out_specs=[vmem_spec()] * 8,
        scratch_shapes=[
            pltpu.VMEM((3 * D, MLP), F32),
            pltpu.VMEM((3, 8 * RA, 128), F32),
            pltpu.VMEM((32, 256), F32),
            pltpu.VMEM((COLS, D), F32),
            pltpu.VMEM((8, POSITIONS), F32),
            pltpu.VMEM((FLAT, 128), F32),
        ],
        compiler_params=pltpu.CompilerParams(vmem_limit_bytes=VMEM),
    )(half_a, half_b, own)
    return (
        dx,
        dg1.reshape(D),
        dqkv,
        dproj,
        dg2.reshape(D),
        dup,
        ddown.T,
        dt.reshape(1, HEADS, POSITIONS),
    )


def solution(mesh):
    parts = Mesh(mesh.devices.reshape(4, 2, 2, 2, 4), ("y", "zh", "c", "zl", "x"))
    grid = P(None, LAT, LON, None)
    in_specs = (grid, grid, P(), P(), P(), P(), P(), P(), P(LAT, None, None))
    out_specs = (grid, P(), P(), P(), P(), P(), P(), P(LAT, None, None))
    return jax.shard_map(local, mesh=parts, in_specs=in_specs, out_specs=out_specs, check_vma=False)
```

```python
import functools
import math

import jax
import jax.numpy as jnp
from jax import lax
from jax.experimental import pallas as pl
from jax.experimental.pallas import tpu as pltpu
from jax.sharding import Mesh
from jax.sharding import PartitionSpec as P

BF = jnp.bfloat16
F32 = jnp.float32
D = 192
HEADS = 6
DH = 32
MLP = 768
WIN_LAT = 6
WIN_LON = 12
HALF_LAT = 3
HALF_LON = 6
RA = 12
WIN = 144
COLS = 48
WINDOWS = 4
OFFS = 2 * WIN_LON - 1
SPAN = OFFS * RA
LINE = WIN_LAT * OFFS
POSITIONS = 4 * WIN_LAT * LINE
SCALE = DH ** (-0.5)
W_CHUNKS = 54
GAIN_AT = 61
HALO = 8
NORTH_AT, EAST_AT, CORNER_AT, FLAT = 0, 384, 440, 512
B_CHUNKS = 5
VMEM = 24 * 1024 * 1024
LOG2E = 1.0 / math.log(2.0)
UNROLL = True
GROUP = 2
TOK = WINDOWS * WIN

LON = ("y", "zh", "c")
LAT = ("zl", "x")
CHIPS = ("y", "zh", "zl", "x")


def nn(a, b):
    return lax.dot_general(a, b, (((1,), (0,)), ((), ())), preferred_element_type=F32)


def nt(a, b):
    return lax.dot_general(a, b, (((1,), (1,)), ((), ())), preferred_element_type=F32)


def tn(a, b):
    return lax.dot_general(a, b, (((0,), (0,)), ((), ())), preferred_element_type=F32)


def put_rows(dst, start, count, rows):
    rows = rows.astype(F32)
    spare = jnp.zeros((count, 256 - D), F32)
    dst[0, pl.ds(start, count, stride=RA), :] = rows[:, :128]
    dst[1, pl.ds(start, count, stride=RA), :] = jnp.concatenate((rows[:, 128:], spare), axis=1)


def put_pair(xs, ys, start, count, ref, l, r):
    pair = ref[l, r, 2].astype(F32)
    rows = pl.ds(start, count, stride=RA)
    xs[0, rows, :] = ref[l, r, 0].astype(F32)
    ys[0, rows, :] = ref[l, r, 1].astype(F32)
    xs[1, rows, :] = pair
    ys[1, rows, :] = pltpu.roll(pair, 64, 1)


def take_pair(src, flat, at, first, second, count):
    first = pl.ds(first, count, stride=RA)
    second = pl.ds(second, count, stride=RA)
    lane = lax.broadcasted_iota(jnp.int32, (count, 128), 1)
    flat[at : at + count, :] = src[0, first, :]
    flat[at + count : at + 2 * count, :] = src[0, second, :]
    flat[at + 2 * count : at + 3 * count, :] = jnp.where(
        lane < 64, src[1, first, :], pltpu.roll(src[1, second, :], 64, 1)
    )


def open_pair(flat, at, count):
    pair = flat[at + 2 * count : at + 3 * count, :]
    return (
        jnp.concatenate((flat[at : at + count, :], pair[:, :64]), axis=1),
        jnp.concatenate((flat[at + count : at + 2 * count, :], pair[:, 64:]), axis=1),
    )


def get_rows(src, start, count):
    low = src[0, pl.ds(start, count, stride=RA), :]
    high = src[1, pl.ds(start, count, stride=RA), :]
    return jnp.concatenate((low, high[:, : D - 128]), axis=1).astype(BF)


def token_rows(src, start, count):
    return jnp.concatenate((src[0, start : start + count, :], src[1, start : start + count, : D - 128]), axis=1)


def each_window(body):
    if UNROLL:
        for w in range(0, WINDOWS, GROUP):
            body(range(w, w + GROUP))
    else:
        pl.loop(0, WINDOWS)(body)


def norm_stats(values):
    mean = jnp.mean(values, axis=-1, keepdims=True)
    centred = values - mean
    variance = jnp.mean(centred * centred, axis=-1, keepdims=True)
    rstd = lax.rsqrt(variance + 1e-05)
    return centred * rstd, rstd


def gelu_pair(u):
    cdf = 0.5 + 0.5 * lax.erf(u * (0.5**0.5))
    slope = cdf + u * jnp.exp(-0.5 * u * u) * (1.0 / math.sqrt(2.0 * math.pi))
    return u * cdf, slope


def norm_back(d_hat, hat, rstd):
    m1 = jnp.mean(d_hat, axis=-1, keepdims=True)
    m2 = jnp.mean(d_hat * hat, axis=-1, keepdims=True)
    return rstd * (d_hat - m1 - hat * m2)


def pack_kernel(both_ref, pa_ref, pb_ref, pc_ref):
    def pack(out, l, r, row, count):
        x = both_ref[l, row].astype(F32)[:count]
        dy = both_ref[2 + l, row].astype(F32)[:count]
        out[l, r, 0] = x[:, :128].astype(BF)
        out[l, r, 1] = dy[:, :128].astype(BF)
        out[l, r, 2] = jnp.concatenate((x[:, 128:], dy[:, 128:]), axis=1).astype(BF)

    for l in range(2):
        for r in range(HALF_LAT):
            pack(pa_ref, l, r, r, COLS)
            pack(pb_ref, l, r, r + HALF_LAT, HALF_LON)
            pack(pc_ref, l, r, r, HALF_LON)


def diagonal_order():
    row = lax.broadcasted_iota(jnp.int32, (SPAN, SPAN), 0)
    col = lax.broadcasted_iota(jnp.int32, (SPAN, SPAN), 1)
    step = lax.shift_right_logical(col * 5462, 16)
    return jnp.where(row == (col - step * RA) * OFFS + OFFS - 1 - step, 1.0, 0.0).astype(BF)


def prepare_kernel(table_ref, w_ref, bias_ref, wqkvt_ref, table, lines, rows_first):
    last = lax.axis_index(LAT) == lax.axis_size(LAT) - 1
    wqkvt_ref[...] = w_ref[:, : 3 * D].T
    for h in range(HEADS):
        lines[h : h + 1, :] = table_ref[h]
    table[...] = jnp.zeros_like(table)
    for li in range(2):
        for ai in range(WIN_LAT):
            place = li * WIN_LAT + ai
            parts = []
            for lj in range(2):
                off = ((li * 2 + lj) * WIN_LAT + ai) * LINE
                parts.append(lines[:, off : off + LINE])
            parts.append(jnp.zeros((8, 384 - SPAN), F32))
            both = jnp.concatenate(parts, axis=1)
            for b in range(3):
                table[b, place * 8 : place * 8 + 8, :] = both[:, 128 * b : 128 * (b + 1)]
    t2 = jnp.concatenate((table[0], table[1], table[2, :, : SPAN - 256]), axis=1)
    hi = t2.astype(BF)
    rest = t2 - hi.astype(F32)
    mid = rest.astype(BF)
    low = (rest - mid.astype(F32)).astype(BF)
    perm = diagonal_order()
    wide = (nn(hi, perm) + nn(mid, perm) + nn(low, perm)) * LOG2E
    wide = jnp.concatenate((wide, jnp.zeros((8 * RA, 384 - SPAN), F32)), axis=1)
    for b in range(3):
        table[b] = wide[:, 128 * b : 128 * (b + 1)]
    key_late = lax.rem(lax.broadcasted_iota(jnp.int32, (WIN, WIN), 0), WIN_LAT) >= HALF_LAT
    query_late = lax.rem(lax.broadcasted_iota(jnp.int32, (WIN, WIN), 1), WIN_LAT) >= HALF_LAT
    split = jnp.logical_and(key_late != query_late, last)
    mask_rows = jnp.where(split, -1e9 * LOG2E, 0.0)
    for h in range(HEADS):
        wide_h = jnp.concatenate([table[b, pl.ds(h, RA, stride=8), :] for b in range(3)], axis=1)
        for oi in range(WIN_LON):
            start = (WIN_LON - 1 - oi) * RA
            rows_first[h, oi * RA : (oi + 1) * RA, :] = wide_h[:, start : start + WIN]
    for h in range(HEADS):
        bias_ref[h] = rows_first[h].T + mask_rows


def block_kernel(
    both_ref, na_ref, nb_ref, nc_ref, w_ref, wqkvt, table_ref, bias,
    mine_ref, send_ref, dp_t, hid, xs,
    ys, probs, heads_t, o_t, do_t, kvs, dss,
    n1s, d_bias, m_acc, g_acc, dw, table,
):
    for l in range(2):
        for r in range(HALF_LAT):
            put_rows(xs, l * 6 + r, COLS, both_ref[l, r + HALF_LAT])
            put_rows(ys, l * 6 + r, COLS, both_ref[2 + l, r + HALF_LAT])
            put_pair(xs, ys, l * 6 + r + HALF_LAT, COLS, na_ref, l, r)
            put_pair(xs, ys, COLS * RA + l * 6 + r, HALF_LON, nb_ref, l, r)
            put_pair(xs, ys, COLS * RA + l * 6 + r + HALF_LAT, HALF_LON, nc_ref, l, r)

    d_bias[...] = jnp.zeros_like(d_bias)
    g_acc[...] = jnp.zeros_like(g_acc)

    g1 = table_ref[HEADS][:, :D]
    g2 = table_ref[HEADS + 1][:, :D]
    w_proj = w_ref[:, 3 * D : 4 * D]
    first = HALF_LON * RA

    hat1, rstd1 = norm_stats(token_rows(xs, first, TOK))
    n1 = (hat1 * g1).astype(BF)
    n1s[...] = n1
    kvs[...] = nn(n1, w_ref[:, D : 3 * D]).astype(BF)

    def attend(ws):
        jobs = [(w, h) for w in ws for h in range(HEADS)]
        rows = {w: pl.ds(w * WIN, WIN) for w in ws}
        parts = [slice(h * DH, (h + 1) * DH) for h in range(HEADS)]
        scores = [
            nn(kvs[rows[w], parts[h]], heads_t[w, parts[h], :]) * (SCALE * LOG2E) + bias[h] for w, h in jobs
        ]
        tops = [jnp.max(s, axis=0, keepdims=True) for s in scores]
        powers = [jnp.exp2(s - top) for s, top in zip(scores, tops)]
        shares = [1.0 / jnp.sum(e, axis=0, keepdims=True) for e in powers]
        for k, (w, h) in enumerate(jobs):
            probs[w, h] = (powers[k] * shares[k]).astype(BF)
        for w, h in jobs:
            o_t[w, parts[h], :] = nn(heads_t[w, 2 * D + h * DH : 2 * D + (h + 1) * DH, :], probs[w, h]).astype(BF)

    for w in range(WINDOWS):
        heads_t[w] = nt(wqkvt[...], n1[w * WIN : (w + 1) * WIN]).astype(BF)
    each_window(attend)
    for w in range(WINDOWS):
        hid[w * WIN : (w + 1) * WIN, :] = tn(o_t[w], w_proj)

    hidden = token_rows(xs, first, TOK) + hid[...]
    hat2, rstd2 = norm_stats(hidden)
    n2 = (hat2 * g2).astype(BF)
    n2_t = n2.T
    dy = token_rows(ys, first, TOK)
    dyb = dy.astype(BF)
    dy_t = dyb.T
    d_n2 = jnp.zeros((TOK, D), F32)
    for j in range(3):
        cols = slice(j * 256, (j + 1) * 256)
        act, slope = gelu_pair(nn(n2, w_ref[:, 4 * D + j * 256 : 4 * D + (j + 1) * 256]))
        d_act = nn(dyb, w_ref[:, 4 * D + MLP + j * 256 : 4 * D + MLP + (j + 1) * 256]).astype(BF).astype(F32)
        d_u = (d_act * slope).astype(BF)
        m_acc[2 * D :, cols] = nn(dy_t, act.astype(BF)).astype(BF)
        m_acc[D : 2 * D, cols] = nn(n2_t, d_u).astype(BF)
        d_n2 = d_n2 + nt(d_u, w_ref[:, 4 * D + j * 256 : 4 * D + (j + 1) * 256])
    d_n2 = d_n2.astype(BF).astype(F32)
    g_acc[1:2, :D] = jnp.sum(d_n2 * hat2, axis=0, keepdims=True)
    d_hidden = dy + norm_back(d_n2 * g2, hat2, rstd2)
    dhb = d_hidden.astype(BF)
    hid[...] = d_hidden
    d_proj = jnp.zeros((D, D), F32)
    for w in range(WINDOWS):
        rows = slice(w * WIN, (w + 1) * WIN)
        d_proj = d_proj + nn(o_t[w], dhb[rows])
        do_t[w] = nt(w_proj, dhb[rows]).astype(BF)

    def attend_back(ws):
        jobs = [(w, h) for w in ws for h in range(HEADS)]
        rows = {w: pl.ds(w * WIN, WIN) for w in ws}
        parts = [slice(h * DH, (h + 1) * DH) for h in range(HEADS)]
        d_probs = [
            nn(kvs[rows[w], D + h * DH : D + (h + 1) * DH], do_t[w, parts[h], :]) for w, h in jobs
        ]
        for k, (w, h) in enumerate(jobs):
            pf = probs[w, h].astype(F32)
            prod = pf * d_probs[k]
            ds = prod - pf * jnp.sum(prod, axis=0, keepdims=True)
            d_bias[h] = d_bias[h] + ds
            dss[k] = ds.astype(BF)
        for k, (w, h) in enumerate(jobs):
            part = parts[h]
            q_t = heads_t[w, part, :]
            k_t = heads_t[w, D + h * DH : D + (h + 1) * DH, :]
            dp_t[w, part, :] = (nn(k_t, dss[k]) * SCALE).astype(BF)
            dp_t[w, D + h * DH : D + (h + 1) * DH, :] = (nt(q_t, dss[k]) * SCALE).astype(BF)
            dp_t[w, 2 * D + h * DH : 2 * D + (h + 1) * DH, :] = nt(do_t[w, part, :], probs[w, h]).astype(BF)

    each_window(attend_back)

    core = lax.axis_index("c")
    perm = diagonal_order()
    dw[...] = jnp.zeros_like(dw)
    d_qkv = jnp.zeros((3 * D, D), F32)
    for w in range(WINDOWS):
        d_qkv = d_qkv + nn(dp_t[w], n1s[w * WIN : (w + 1) * WIN, :])
    m_acc[:D, :] = jnp.concatenate((d_qkv.T, d_proj), axis=1).astype(BF)

    for h in range(HEADS):
        d_bias[h] = d_bias[h].T
    for oi in range(WIN_LON):
        start = (WIN_LON - 1 - oi) * RA
        for h in range(HEADS):
            dw[h * RA : (h + 1) * RA, start : start + WIN] += d_bias[h, oi * RA : (oi + 1) * RA, :]
    dwv = dw[:, :SPAN]
    dw_hi = dwv.astype(BF)
    dw_lo = (dwv - dw_hi.astype(F32)).astype(BF)
    d_t2 = nt(dw_hi, perm) + nt(dw_lo, perm)
    d_t2 = jnp.concatenate((d_t2, jnp.zeros((HEADS * RA, 384 - SPAN), F32)), axis=1)
    table[...] = jnp.zeros_like(table)
    for h in range(HEADS):
        for b in range(3):
            table[b, pl.ds(h, RA, stride=8), :] = d_t2[h * RA : (h + 1) * RA, 128 * b : 128 * (b + 1)]

    mine_half = pl.multiple_of(core * 288, 32)
    send_half = pl.multiple_of((1 - core) * 288, 32)
    for i in range(9):
        for b in range(6):
            cols = slice(b * 128, (b + 1) * 128)
            mine_ref[i * 6 + b] = m_acc[pl.ds(mine_half + 32 * i, 32), cols]
            send_ref[i * 6 + b] = m_acc[pl.ds(send_half + 32 * i, 32), cols]
    zero = jnp.zeros((32, 128), BF)
    for ref, half in ((mine_ref, core), (send_ref, 1 - core)):
        for k in range(W_CHUNKS, 64):
            ref[k] = zero

        @pl.when(half == 0)
        def _(ref=ref):
            for k in range(5):
                ref[W_CHUNKS + k] = table[k % 3, 32 * (k // 3) : 32 * (k // 3) + 32, :].astype(BF)
            ref[W_CHUNKS + B_CHUNKS] = g_acc[:, :128].astype(BF)
            ref[W_CHUNKS + B_CHUNKS + 1] = g_acc[:, 128:].astype(BF)

        @pl.when(half == 1)
        def _(ref=ref):
            for k in range(5, 9):
                ref[W_CHUNKS + k - 5] = table[k % 3, 32 * (k // 3) : 32 * (k // 3) + 32, :].astype(BF)


def grad_kernel(dp_t, hid, xs, w_ref, table_ref, own_ref, halo_ref, gain_ref, gs, flat):
    g1 = table_ref[HEADS][:, :D]
    first = HALF_LON * RA
    gs[:, :first, :] = jnp.zeros((2, first, 128), F32)
    d_n1 = []
    for w in range(WINDOWS):
        d_n1.append(nn(w_ref[:, : 3 * D], dp_t[w]).T)
    d_n1 = jnp.concatenate(d_n1, axis=0).astype(BF).astype(F32)
    hat1, rstd1 = norm_stats(token_rows(xs, first, TOK))
    d_gain = jnp.sum(d_n1 * hat1, axis=0, keepdims=True)
    spare = jnp.zeros((1, 256 - D), F32)
    gain_ref[...] = jnp.concatenate(
        (d_gain[:, :128], jnp.concatenate((d_gain[:, 128:], spare), axis=1), jnp.zeros((30, 128), F32)), axis=0
    ).astype(BF)
    d_x = hid[...] + norm_back(d_n1 * g1, hat1, rstd1)
    gs[0, first:, :] = d_x[:, :128]
    gs[1, first:, : D - 128] = d_x[:, 128:]

    for l in range(2):
        for r in range(HALF_LAT):
            own_ref[l, r] = get_rows(gs, l * 6 + r, COLS)

    flat[...] = jnp.zeros_like(flat)
    inner = COLS - HALF_LON
    for r in range(HALF_LAT):
        late = r + HALF_LAT
        take_pair(gs, flat, NORTH_AT + r * 3 * inner, first + late, first + 6 + late, inner)
        take_pair(gs, flat, EAST_AT + r * 3 * HALF_LON, COLS * RA + r, COLS * RA + r + 6, HALF_LON)
        take_pair(gs, flat, CORNER_AT + r * 3 * HALF_LON, COLS * RA + late, COLS * RA + late + 6, HALF_LON)
    for k in range(64):
        halo_ref[k] = flat[HALO * k : HALO * (k + 1), :].astype(BF)


def join_kernel(mine_ref, got_ref, halo_ref, gain_ref, out_ref):
    for k in range(64):
        if k != GAIN_AT:
            out_ref[k, :32] = (mine_ref[k].astype(F32) + got_ref[k].astype(F32)).astype(BF)
        out_ref[k, 32:] = halo_ref[k]
    out_ref[GAIN_AT, :32] = gain_ref[...]


def reply_kernel(got_ref, out_ref):
    relay = lax.axis_index(CHIPS)
    is_bias = jnp.logical_and(relay >= W_CHUNKS, relay < W_CHUNKS + B_CHUNKS).astype(F32)
    total = jnp.zeros((32, 128), F32)
    bands = []
    for lat in range(8):
        s = got_ref[lat, :32].astype(F32)
        for j in range(1, 8):
            s = s + got_ref[j * 8 + lat, :32].astype(F32)
        bands.append(s)
        total = total + s
    by_lat = jnp.logical_or(relay < EAST_AT // HALO, relay >= CORNER_AT // HALO).astype(jnp.int32)
    by_lon = jnp.logical_and(relay >= EAST_AT // HALO, lax.axis_index("c") == 1).astype(jnp.int32)
    for lat in range(8):
        s = jnp.where(is_bias > 0.5, bands[lat], total).astype(BF)
        from_lat = lax.rem(lat + 7 * by_lat, 8)
        for j in range(8):
            out_ref[j * 8 + lat, :32] = s
            out_ref[j * 8 + lat, 32:] = got_ref[lax.rem(j + 7 * by_lon, 8) * 8 + from_lat, 32:]


def finish_kernel(
    a_ref, b_ref, own_ref,
    dx_ref, dg1_ref, dqkv_ref, dproj_ref, dg2_ref, dup_ref, ddown_ref, dt_ref,
    m_acc, table, g_acc, line, lines, flat, grad_scale,
):
    core = lax.axis_index("c")
    a_half = pl.multiple_of(core * 288, 32)
    b_half = pl.multiple_of((1 - core) * 288, 32)
    for i in range(9):
        for b in range(6):
            cols = slice(b * 128, (b + 1) * 128)
            m_acc[pl.ds(a_half + 32 * i, 32), cols] = a_ref[i * 6 + b, :32].astype(F32) * grad_scale
            m_acc[pl.ds(b_half + 32 * i, 32), cols] = b_ref[i * 6 + b, :32].astype(F32) * grad_scale
    for ref, half in ((a_ref, core), (b_ref, 1 - core)):

        @pl.when(half == 0)
        def _(ref=ref):
            for k in range(5):
                table[k % 3, 32 * (k // 3) : 32 * (k // 3) + 32, :] = ref[W_CHUNKS + k, :32].astype(F32)
            g_acc[:, :128] = ref[W_CHUNKS + B_CHUNKS, :32].astype(F32) * grad_scale
            g_acc[:, 128:] = ref[W_CHUNKS + B_CHUNKS + 1, :32].astype(F32) * grad_scale

        @pl.when(half == 1)
        def _(ref=ref):
            for k in range(5, 9):
                table[k % 3, 32 * (k // 3) : 32 * (k // 3) + 32, :] = ref[W_CHUNKS + k - 5, :32].astype(F32)

    dqkv_ref[...] = m_acc[:D, : 3 * D]
    dproj_ref[...] = m_acc[:D, 3 * D :]
    dup_ref[...] = m_acc[D : 2 * D, :]
    ddown_ref[...] = m_acc[2 * D :, :]
    d_gain = (a_ref[GAIN_AT, :32].astype(F32) + b_ref[GAIN_AT, :32].astype(F32)) * grad_scale
    dg1_ref[:, :128] = d_gain[0:1, :]
    dg1_ref[:, 128:] = d_gain[1:2, : D - 128]
    dg2_ref[...] = g_acc[1:2, :D]
    for li in range(2):
        for ai in range(WIN_LAT):
            place = li * WIN_LAT + ai
            rows = jnp.concatenate([table[b, place * 8 : place * 8 + 8, :] for b in range(3)], axis=1)
            for lj in range(2):
                off = ((li * 2 + lj) * WIN_LAT + ai) * LINE
                lines[:, off : off + LINE] = rows[:, lj * LINE : (lj + 1) * LINE]
    for h in range(HEADS):
        dt_ref[h] = lines[h : h + 1, :]

    for k in range(64):
        ref = a_ref if k < EAST_AT // HALO else b_ref
        flat[HALO * k : HALO * (k + 1), :] = ref[k, 32:].astype(F32)
    inner = COLS - HALF_LON
    for r in range(HALF_LAT):
        north = open_pair(flat, NORTH_AT + r * 3 * inner, inner)
        east = open_pair(flat, EAST_AT + r * 3 * HALF_LON, HALF_LON)
        corner = open_pair(flat, CORNER_AT + r * 3 * HALF_LON, HALF_LON)
        for l in range(2):
            line[...] = own_ref[l, r].astype(F32)
            line[:HALF_LON, :] = east[l]
            dx_ref[l, r + HALF_LAT] = line[...].astype(BF)
            line[HALF_LON:, :] = north[l]
            line[:HALF_LON, :] = corner[l]
            dx_ref[l, r] = line[...].astype(BF)


def shift_pairs(lon_by, lat_by):
    pairs = []
    for lon in range(16):
        for lat in range(8):
            pairs.append((lon * 8 + lat, ((lon + lon_by) % 16) * 8 + (lat + lat_by) % 8))
    return pairs


def one_axis(length, by):
    return [(i, (i + by) % length) for i in range(length)]


def vmem_spec():
    return pl.BlockSpec(memory_space=pltpu.VMEM)


def prepare(table, weights):
    shape = jax.ShapeDtypeStruct
    return pl.pallas_call(
        prepare_kernel,
        out_shape=(shape((HEADS, WIN, WIN), F32), shape((3 * D, D), BF)),
        in_specs=[vmem_spec()] * 2,
        out_specs=[vmem_spec()] * 2,
        scratch_shapes=[
            pltpu.VMEM((3, 8 * RA, 128), F32),
            pltpu.VMEM((8, POSITIONS), F32),
            pltpu.VMEM((HEADS, WIN, WIN), F32),
        ],
        compiler_params=pltpu.CompilerParams(vmem_limit_bytes=VMEM),
    )(table, weights)


def pack_halos(both):
    shape = jax.ShapeDtypeStruct
    return pl.pallas_call(
        pack_kernel,
        out_shape=(
            shape((2, HALF_LAT, 3, COLS, 128), BF),
            shape((2, HALF_LAT, 3, HALF_LON, 128), BF),
            shape((2, HALF_LAT, 3, HALF_LON, 128), BF),
        ),
        in_specs=[vmem_spec()],
        out_specs=[vmem_spec()] * 3,
        compiler_params=pltpu.CompilerParams(vmem_limit_bytes=VMEM),
    )(both)


def run_block(both, na, nb, nc, weights, w_qkv_t, table, bias):
    shape = jax.ShapeDtypeStruct
    return pl.pallas_call(
        block_kernel,
        out_shape=(
            shape((64, 32, 128), BF),
            shape((64, 32, 128), BF),
            shape((WINDOWS, 3 * D, WIN), BF),
            shape((TOK, D), F32),
            shape((2, 54 * RA, 128), F32),
        ),
        in_specs=[vmem_spec()] * 8,
        out_specs=[vmem_spec()] * 5,
        scratch_shapes=[
            pltpu.VMEM((2, 54 * RA, 128), F32),
            pltpu.VMEM((WINDOWS, HEADS, WIN, WIN), BF),
            pltpu.VMEM((WINDOWS, 3 * D, WIN), BF),
            pltpu.VMEM((WINDOWS, D, WIN), BF),
            pltpu.VMEM((WINDOWS, D, WIN), BF),
            pltpu.VMEM((TOK, 2 * D), BF),
            pltpu.VMEM((WINDOWS * HEADS, WIN, WIN), BF),
            pltpu.VMEM((TOK, D), BF),
            pltpu.VMEM((HEADS, WIN, WIN), F32),
            pltpu.VMEM((3 * D, MLP), BF),
            pltpu.VMEM((32, 256), F32),
            pltpu.VMEM((HEADS * RA, 384), F32),
            pltpu.VMEM((3, 8 * RA, 128), F32),
        ],
        compiler_params=pltpu.CompilerParams(vmem_limit_bytes=VMEM),
    )(both, na, nb, nc, weights, w_qkv_t, table, bias)


def input_grad(d_packed_t, d_hidden, tokens, weights, table):
    shape = jax.ShapeDtypeStruct
    return pl.pallas_call(
        grad_kernel,
        out_shape=(
            shape((2, HALF_LAT, COLS, D), BF),
            shape((64, HALO, 128), BF),
            shape((32, 128), BF),
        ),
        in_specs=[vmem_spec()] * 5,
        out_specs=[vmem_spec()] * 3,
        scratch_shapes=[pltpu.VMEM((2, 54 * RA, 128), F32), pltpu.VMEM((FLAT, 128), F32)],
        compiler_params=pltpu.CompilerParams(vmem_limit_bytes=VMEM),
    )(d_packed_t, d_hidden, tokens, weights, table)


def local(tokens, cotangent, ln1_gain, w_qkv, w_proj, ln2_gain, w_up, w_down, bias_table):
    edge = ((0, 0),) * 3
    both = jnp.pad(tokens, ((0, 2),) + edge) + jnp.pad(cotangent, ((2, 0),) + edge)
    part_a, part_b, part_c = pack_halos(both)
    na = lax.ppermute(part_a, LAT, one_axis(8, -1))
    nb = lax.ppermute(part_b, LON, one_axis(16, -1))
    nc = lax.ppermute(part_c, LON + LAT, shift_pairs(-1, -1))

    weights = jnp.concatenate((w_qkv, w_proj, w_up, w_down.T), axis=1)
    gains = jnp.pad(jnp.stack((ln1_gain, ln2_gain)), ((0, 0), (0, POSITIONS - D)))
    table = jnp.concatenate((bias_table.reshape(HEADS, 1, POSITIONS), gains[:, None]), axis=0)
    bias, w_qkv_t = prepare(table, weights)
    mine, send, d_packed_t, d_hidden, shifted = run_block(both, na, nb, nc, weights, w_qkv_t, table, bias)

    pair = [(0, 1), (1, 0)]
    got = lax.ppermute(send, "c", pair)
    own, halo, gain = input_grad(d_packed_t, d_hidden, shifted, weights, table)
    chunks = jax.ShapeDtypeStruct((64, 32 + HALO, 128), BF)
    joined = pl.pallas_call(
        join_kernel,
        out_shape=chunks,
        in_specs=[vmem_spec()] * 4,
        out_specs=vmem_spec(),
        compiler_params=pltpu.CompilerParams(vmem_limit_bytes=VMEM),
    )(mine, got, halo, gain)
    spread = lax.all_to_all(joined, CHIPS, 0, 0, tiled=True)
    reply = pl.pallas_call(
        reply_kernel,
        out_shape=chunks,
        in_specs=[vmem_spec()],
        out_specs=vmem_spec(),
        compiler_params=pltpu.CompilerParams(vmem_limit_bytes=VMEM),
    )(spread)
    half_a = lax.all_to_all(reply, CHIPS, 0, 0, tiled=True)
    half_b = lax.ppermute(half_a, "c", pair)
    shape = jax.ShapeDtypeStruct
    total_tokens = 128 * tokens.shape[0] * tokens.shape[1] * tokens.shape[2]
    dx, dg1, dqkv, dproj, dg2, dup, ddown, dt = pl.pallas_call(
        functools.partial(finish_kernel, grad_scale=1.0 / math.sqrt(total_tokens)),
        out_shape=(
            shape(tokens.shape, BF),
            shape((1, D), F32),
            shape((D, 3 * D), F32),
            shape((D, D), F32),
            shape((1, D), F32),
            shape((D, MLP), F32),
            shape((D, MLP), F32),
            shape((HEADS, 1, POSITIONS), F32),
        ),
        in_specs=[vmem_spec()] * 3,
        out_specs=[vmem_spec()] * 8,
        scratch_shapes=[
            pltpu.VMEM((3 * D, MLP), F32),
            pltpu.VMEM((3, 8 * RA, 128), F32),
            pltpu.VMEM((32, 256), F32),
            pltpu.VMEM((COLS, D), F32),
            pltpu.VMEM((8, POSITIONS), F32),
            pltpu.VMEM((FLAT, 128), F32),
        ],
        compiler_params=pltpu.CompilerParams(vmem_limit_bytes=VMEM),
    )(half_a, half_b, own)
    return (
        dx,
        dg1.reshape(D),
        dqkv,
        dproj,
        dg2.reshape(D),
        dup,
        ddown.T,
        dt.reshape(1, HEADS, POSITIONS),
    )


def solution(mesh):
    parts = Mesh(mesh.devices.reshape(4, 2, 2, 2, 4), ("y", "zh", "c", "zl", "x"))
    grid = P(None, LAT, LON, None)
    in_specs = (grid, grid, P(), P(), P(), P(), P(), P(), P(LAT, None, None))
    out_specs = (grid, P(), P(), P(), P(), P(), P(), P(LAT, None, None))
    return jax.shard_map(local, mesh=parts, in_specs=in_specs, out_specs=out_specs, check_vma=False)
```

```python
import functools
import math

import jax
import jax.numpy as jnp
from jax import lax
from jax.experimental import pallas as pl
from jax.experimental.pallas import tpu as pltpu
from jax.sharding import Mesh
from jax.sharding import PartitionSpec as P

BF = jnp.bfloat16
F32 = jnp.float32
D = 192
HEADS = 6
DH = 32
MLP = 768
WIN_LAT = 6
WIN_LON = 12
HALF_LAT = 3
HALF_LON = 6
RA = 12
WIN = 144
COLS = 48
INNER = COLS - HALF_LON
WINDOWS = 4
OFFS = 2 * WIN_LON - 1
SPAN = OFFS * RA
LINE = WIN_LAT * OFFS
POSITIONS = 4 * WIN_LAT * LINE
SCALE = DH ** (-0.5)
W_CHUNKS = 54
GAIN_AT = 61
HALO = 8
NORTH_AT, EAST_AT, CORNER_AT, FLAT = 0, 384, 440, 512
B_CHUNKS = 5
VMEM = 24 * 1024 * 1024
LOG2E = 1.0 / math.log(2.0)
UNROLL = True
GROUP = 2
TOK = WINDOWS * WIN

LON = ("y", "zh", "c")
LAT = ("zl", "x")
CHIPS = ("y", "zh", "zl", "x")


def nn(a, b):
    return lax.dot_general(a, b, (((1,), (0,)), ((), ())), preferred_element_type=F32)


def nt(a, b):
    return lax.dot_general(a, b, (((1,), (1,)), ((), ())), preferred_element_type=F32)


def tn(a, b):
    return lax.dot_general(a, b, (((0,), (0,)), ((), ())), preferred_element_type=F32)


def put_rows(dst, start, count, rows):
    rows = rows.astype(F32)
    spare = jnp.zeros((count, 256 - D), F32)
    dst[0, pl.ds(start, count, stride=RA), :] = rows[:, :128]
    dst[1, pl.ds(start, count, stride=RA), :] = jnp.concatenate((rows[:, 128:], spare), axis=1)


def put_parts(xs, ys, start, count, parts):
    rows = pl.ds(start, count, stride=RA)
    xs[0, rows, :] = parts[0]
    ys[0, rows, :] = parts[1]
    xs[1, rows, :] = parts[2]
    ys[1, rows, :] = pltpu.roll(parts[2], 64, 1)


def put_pair(xs, ys, start, count, ref, l, r):
    put_parts(xs, ys, start, count, [ref[l, r, k].astype(F32) for k in range(3)])


def take_pair(src, flat, at, first, second, count):
    first = pl.ds(first, count, stride=RA)
    second = pl.ds(second, count, stride=RA)
    lane = lax.broadcasted_iota(jnp.int32, (count, 128), 1)
    flat[at : at + count, :] = src[0, first, :]
    flat[at + count : at + 2 * count, :] = src[0, second, :]
    flat[at + 2 * count : at + 3 * count, :] = jnp.where(
        lane < 64, src[1, first, :], pltpu.roll(src[1, second, :], 64, 1)
    )


def open_pair(flat, at, count):
    pair = flat[at + 2 * count : at + 3 * count, :]
    return (
        jnp.concatenate((flat[at : at + count, :], pair[:, :64]), axis=1),
        jnp.concatenate((flat[at + count : at + 2 * count, :], pair[:, 64:]), axis=1),
    )


def get_rows(src, start, count):
    low = src[0, pl.ds(start, count, stride=RA), :]
    high = src[1, pl.ds(start, count, stride=RA), :]
    return jnp.concatenate((low, high[:, : D - 128]), axis=1).astype(BF)


def token_rows(src, start, count):
    return jnp.concatenate((src[0, start : start + count, :], src[1, start : start + count, : D - 128]), axis=1)


def each_window(body):
    if UNROLL:
        for w in range(0, WINDOWS, GROUP):
            body(range(w, w + GROUP))
    else:
        pl.loop(0, WINDOWS)(body)


def norm_stats(values):
    mean = jnp.mean(values, axis=-1, keepdims=True)
    centred = values - mean
    variance = jnp.mean(centred * centred, axis=-1, keepdims=True)
    rstd = lax.rsqrt(variance + 1e-05)
    return centred * rstd, rstd


def gelu_pair(u):
    cdf = 0.5 + 0.5 * lax.erf(u * (0.5**0.5))
    slope = cdf + u * jnp.exp(-0.5 * u * u) * (1.0 / math.sqrt(2.0 * math.pi))
    return u * cdf, slope


def norm_back(d_hat, hat, rstd):
    m1 = jnp.mean(d_hat, axis=-1, keepdims=True)
    m2 = jnp.mean(d_hat * hat, axis=-1, keepdims=True)
    return rstd * (d_hat - m1 - hat * m2)


def pack_kernel(both_ref, pa_ref, pb_ref, pc_ref):
    def parts(l, row, cols):
        x = both_ref[l, row].astype(F32)[cols]
        dy = both_ref[2 + l, row].astype(F32)[cols]
        return [x[:, :128], dy[:, :128], jnp.concatenate((x[:, 128:], dy[:, 128:]), axis=1)]

    for l in range(2):
        for r in range(HALF_LAT):
            rows = parts(l, r, slice(HALF_LON, COLS)) + [jnp.zeros((128 - 3 * INNER, 128), F32)]
            pa_ref[l, r] = jnp.concatenate(rows, axis=0).astype(BF)
            for k, rows in enumerate(parts(l, r + HALF_LAT, slice(0, HALF_LON))):
                pb_ref[l, r, k] = rows.astype(BF)
            for k, rows in enumerate(parts(l, r, slice(0, HALF_LON))):
                pc_ref[l, r, k] = rows.astype(BF)


def diagonal_order():
    row = lax.broadcasted_iota(jnp.int32, (SPAN, SPAN), 0)
    col = lax.broadcasted_iota(jnp.int32, (SPAN, SPAN), 1)
    step = lax.shift_right_logical(col * 5462, 16)
    return jnp.where(row == (col - step * RA) * OFFS + OFFS - 1 - step, 1.0, 0.0).astype(BF)


def prepare_kernel(table_ref, w_ref, bias_ref, wqkvt_ref, table, lines, rows_first):
    last = lax.axis_index(LAT) == lax.axis_size(LAT) - 1
    wqkvt_ref[...] = w_ref[:, : 3 * D].T
    for h in range(HEADS):
        lines[h : h + 1, :] = table_ref[h]
    table[...] = jnp.zeros_like(table)
    for li in range(2):
        for ai in range(WIN_LAT):
            place = li * WIN_LAT + ai
            parts = []
            for lj in range(2):
                off = ((li * 2 + lj) * WIN_LAT + ai) * LINE
                parts.append(lines[:, off : off + LINE])
            parts.append(jnp.zeros((8, 384 - SPAN), F32))
            both = jnp.concatenate(parts, axis=1)
            for b in range(3):
                table[b, place * 8 : place * 8 + 8, :] = both[:, 128 * b : 128 * (b + 1)]
    t2 = jnp.concatenate((table[0], table[1], table[2, :, : SPAN - 256]), axis=1)
    hi = t2.astype(BF)
    rest = t2 - hi.astype(F32)
    mid = rest.astype(BF)
    low = (rest - mid.astype(F32)).astype(BF)
    perm = diagonal_order()
    wide = (nn(hi, perm) + nn(mid, perm) + nn(low, perm)) * LOG2E
    wide = jnp.concatenate((wide, jnp.zeros((8 * RA, 384 - SPAN), F32)), axis=1)
    for b in range(3):
        table[b] = wide[:, 128 * b : 128 * (b + 1)]
    key_late = lax.rem(lax.broadcasted_iota(jnp.int32, (WIN, WIN), 0), WIN_LAT) >= HALF_LAT
    query_late = lax.rem(lax.broadcasted_iota(jnp.int32, (WIN, WIN), 1), WIN_LAT) >= HALF_LAT
    split = jnp.logical_and(key_late != query_late, last)
    mask_rows = jnp.where(split, -1e9 * LOG2E, 0.0)
    for h in range(HEADS):
        wide_h = jnp.concatenate([table[b, pl.ds(h, RA, stride=8), :] for b in range(3)], axis=1)
        for oi in range(WIN_LON):
            start = (WIN_LON - 1 - oi) * RA
            rows_first[h, oi * RA : (oi + 1) * RA, :] = wide_h[:, start : start + WIN]
    for h in range(HEADS):
        bias_ref[h] = rows_first[h].T + mask_rows


def block_kernel(
    both_ref, na_ref, nb_ref, nc_ref, w_ref, wqkvt, table_ref, bias,
    mine_ref, send_ref, dp_t, hid, xs,
    ys, probs, heads_t, o_t, do_t, kvs, dss,
    n1s, d_bias, m_acc, g_acc, dw, table,
):
    for l in range(2):
        for r in range(HALF_LAT):
            put_rows(xs, l * 6 + r, COLS, both_ref[l, r + HALF_LAT])
            put_rows(ys, l * 6 + r, COLS, both_ref[2 + l, r + HALF_LAT])
            north = na_ref[l, r].astype(F32)
            north = [north[k * INNER : (k + 1) * INNER] for k in range(3)]
            put_parts(xs, ys, HALF_LON * RA + l * 6 + r + HALF_LAT, INNER, north)
            put_pair(xs, ys, COLS * RA + l * 6 + r, HALF_LON, nb_ref, l, r)
            put_pair(xs, ys, COLS * RA + l * 6 + r + HALF_LAT, HALF_LON, nc_ref, l, r)

    d_bias[...] = jnp.zeros_like(d_bias)
    g_acc[...] = jnp.zeros_like(g_acc)

    g1 = table_ref[HEADS][:, :D]
    g2 = table_ref[HEADS + 1][:, :D]
    w_proj = w_ref[:, 3 * D : 4 * D]
    first = HALF_LON * RA

    hat1, rstd1 = norm_stats(token_rows(xs, first, TOK))
    n1 = (hat1 * g1).astype(BF)
    n1s[...] = n1
    kvs[...] = nn(n1, w_ref[:, D : 3 * D]).astype(BF)

    def attend(ws):
        jobs = [(w, h) for w in ws for h in range(HEADS)]
        rows = {w: pl.ds(w * WIN, WIN) for w in ws}
        parts = [slice(h * DH, (h + 1) * DH) for h in range(HEADS)]
        scores = [
            nn(kvs[rows[w], parts[h]], heads_t[w, parts[h], :]) * (SCALE * LOG2E) + bias[h] for w, h in jobs
        ]
        tops = [jnp.max(s, axis=0, keepdims=True) for s in scores]
        powers = [jnp.exp2(s - top) for s, top in zip(scores, tops)]
        shares = [1.0 / jnp.sum(e, axis=0, keepdims=True) for e in powers]
        for k, (w, h) in enumerate(jobs):
            probs[w, h] = (powers[k] * shares[k]).astype(BF)
        for w, h in jobs:
            o_t[w, parts[h], :] = nn(heads_t[w, 2 * D + h * DH : 2 * D + (h + 1) * DH, :], probs[w, h]).astype(BF)

    for w in range(WINDOWS):
        heads_t[w] = nt(wqkvt[...], n1[w * WIN : (w + 1) * WIN]).astype(BF)
    each_window(attend)
    for w in range(WINDOWS):
        hid[w * WIN : (w + 1) * WIN, :] = tn(o_t[w], w_proj)

    hidden = token_rows(xs, first, TOK) + hid[...]
    hat2, rstd2 = norm_stats(hidden)
    n2 = (hat2 * g2).astype(BF)
    n2_t = n2.T
    dy = token_rows(ys, first, TOK)
    dyb = dy.astype(BF)
    dy_t = dyb.T
    d_n2 = jnp.zeros((TOK, D), F32)
    for j in range(3):
        cols = slice(j * 256, (j + 1) * 256)
        act, slope = gelu_pair(nn(n2, w_ref[:, 4 * D + j * 256 : 4 * D + (j + 1) * 256]))
        d_act = nn(dyb, w_ref[:, 4 * D + MLP + j * 256 : 4 * D + MLP + (j + 1) * 256]).astype(BF).astype(F32)
        d_u = (d_act * slope).astype(BF)
        m_acc[2 * D :, cols] = nn(dy_t, act.astype(BF)).astype(BF)
        m_acc[D : 2 * D, cols] = nn(n2_t, d_u).astype(BF)
        d_n2 = d_n2 + nt(d_u, w_ref[:, 4 * D + j * 256 : 4 * D + (j + 1) * 256])
    d_n2 = d_n2.astype(BF).astype(F32)
    g_acc[1:2, :D] = jnp.sum(d_n2 * hat2, axis=0, keepdims=True)
    d_hidden = dy + norm_back(d_n2 * g2, hat2, rstd2)
    dhb = d_hidden.astype(BF)
    hid[...] = d_hidden
    d_proj = jnp.zeros((D, D), F32)
    for w in range(WINDOWS):
        rows = slice(w * WIN, (w + 1) * WIN)
        d_proj = d_proj + nn(o_t[w], dhb[rows])
        do_t[w] = nt(w_proj, dhb[rows]).astype(BF)

    def attend_back(ws):
        jobs = [(w, h) for w in ws for h in range(HEADS)]
        rows = {w: pl.ds(w * WIN, WIN) for w in ws}
        parts = [slice(h * DH, (h + 1) * DH) for h in range(HEADS)]
        d_probs = [
            nn(kvs[rows[w], D + h * DH : D + (h + 1) * DH], do_t[w, parts[h], :]) for w, h in jobs
        ]
        for k, (w, h) in enumerate(jobs):
            pf = probs[w, h].astype(F32)
            prod = pf * d_probs[k]
            ds = prod - pf * jnp.sum(prod, axis=0, keepdims=True)
            d_bias[h] = d_bias[h] + ds
            dss[k] = ds.astype(BF)
        for k, (w, h) in enumerate(jobs):
            part = parts[h]
            q_t = heads_t[w, part, :]
            k_t = heads_t[w, D + h * DH : D + (h + 1) * DH, :]
            dp_t[w, part, :] = (nn(k_t, dss[k]) * SCALE).astype(BF)
            dp_t[w, D + h * DH : D + (h + 1) * DH, :] = (nt(q_t, dss[k]) * SCALE).astype(BF)
            dp_t[w, 2 * D + h * DH : 2 * D + (h + 1) * DH, :] = nt(do_t[w, part, :], probs[w, h]).astype(BF)

    each_window(attend_back)

    core = lax.axis_index("c")
    perm = diagonal_order()
    dw[...] = jnp.zeros_like(dw)
    d_qkv = jnp.zeros((3 * D, D), F32)
    for w in range(WINDOWS):
        d_qkv = d_qkv + nn(dp_t[w], n1s[w * WIN : (w + 1) * WIN, :])
    m_acc[:D, :] = jnp.concatenate((d_qkv.T, d_proj), axis=1).astype(BF)

    for h in range(HEADS):
        d_bias[h] = d_bias[h].T
    for oi in range(WIN_LON):
        start = (WIN_LON - 1 - oi) * RA
        for h in range(HEADS):
            dw[h * RA : (h + 1) * RA, start : start + WIN] += d_bias[h, oi * RA : (oi + 1) * RA, :]
    dwv = dw[:, :SPAN]
    dw_hi = dwv.astype(BF)
    dw_lo = (dwv - dw_hi.astype(F32)).astype(BF)
    d_t2 = nt(dw_hi, perm) + nt(dw_lo, perm)
    d_t2 = jnp.concatenate((d_t2, jnp.zeros((HEADS * RA, 384 - SPAN), F32)), axis=1)
    table[...] = jnp.zeros_like(table)
    for h in range(HEADS):
        for b in range(3):
            table[b, pl.ds(h, RA, stride=8), :] = d_t2[h * RA : (h + 1) * RA, 128 * b : 128 * (b + 1)]

    mine_half = pl.multiple_of(core * 288, 32)
    send_half = pl.multiple_of((1 - core) * 288, 32)
    for i in range(9):
        for b in range(6):
            cols = slice(b * 128, (b + 1) * 128)
            mine_ref[i * 6 + b] = m_acc[pl.ds(mine_half + 32 * i, 32), cols]
            send_ref[i * 6 + b] = m_acc[pl.ds(send_half + 32 * i, 32), cols]
    zero = jnp.zeros((32, 128), BF)
    for ref, half in ((mine_ref, core), (send_ref, 1 - core)):
        for k in range(W_CHUNKS, 64):
            ref[k] = zero

        @pl.when(half == 0)
        def _(ref=ref):
            for k in range(5):
                ref[W_CHUNKS + k] = table[k % 3, 32 * (k // 3) : 32 * (k // 3) + 32, :].astype(BF)
            ref[W_CHUNKS + B_CHUNKS] = g_acc[:, :128].astype(BF)
            ref[W_CHUNKS + B_CHUNKS + 1] = g_acc[:, 128:].astype(BF)

        @pl.when(half == 1)
        def _(ref=ref):
            for k in range(5, 9):
                ref[W_CHUNKS + k - 5] = table[k % 3, 32 * (k // 3) : 32 * (k // 3) + 32, :].astype(BF)


def grad_kernel(dp_t, hid, xs, w_ref, table_ref, own_ref, halo_ref, gain_ref, gs, flat):
    g1 = table_ref[HEADS][:, :D]
    first = HALF_LON * RA
    gs[:, :first, :] = jnp.zeros((2, first, 128), F32)
    d_n1 = []
    for w in range(WINDOWS):
        d_n1.append(nn(w_ref[:, : 3 * D], dp_t[w]).T)
    d_n1 = jnp.concatenate(d_n1, axis=0).astype(BF).astype(F32)
    hat1, rstd1 = norm_stats(token_rows(xs, first, TOK))
    d_gain = jnp.sum(d_n1 * hat1, axis=0, keepdims=True)
    spare = jnp.zeros((1, 256 - D), F32)
    gain_ref[...] = jnp.concatenate(
        (d_gain[:, :128], jnp.concatenate((d_gain[:, 128:], spare), axis=1), jnp.zeros((30, 128), F32)), axis=0
    ).astype(BF)
    d_x = hid[...] + norm_back(d_n1 * g1, hat1, rstd1)
    gs[0, first:, :] = d_x[:, :128]
    gs[1, first:, : D - 128] = d_x[:, 128:]

    for l in range(2):
        for r in range(HALF_LAT):
            own_ref[l, r] = get_rows(gs, l * 6 + r, COLS)

    flat[...] = jnp.zeros_like(flat)
    inner = COLS - HALF_LON
    for r in range(HALF_LAT):
        late = r + HALF_LAT
        take_pair(gs, flat, NORTH_AT + r * 3 * inner, first + late, first + 6 + late, inner)
        take_pair(gs, flat, EAST_AT + r * 3 * HALF_LON, COLS * RA + r, COLS * RA + r + 6, HALF_LON)
        take_pair(gs, flat, CORNER_AT + r * 3 * HALF_LON, COLS * RA + late, COLS * RA + late + 6, HALF_LON)
    for k in range(64):
        halo_ref[k] = flat[HALO * k : HALO * (k + 1), :].astype(BF)


def join_kernel(mine_ref, got_ref, halo_ref, gain_ref, out_ref):
    for k in range(64):
        if k != GAIN_AT:
            out_ref[k, :32] = (mine_ref[k].astype(F32) + got_ref[k].astype(F32)).astype(BF)
        out_ref[k, 32:] = halo_ref[k]
    out_ref[GAIN_AT, :32] = gain_ref[...]


def reply_kernel(got_ref, out_ref):
    relay = lax.axis_index(CHIPS)
    is_bias = jnp.logical_and(relay >= W_CHUNKS, relay < W_CHUNKS + B_CHUNKS).astype(F32)
    total = jnp.zeros((32, 128), F32)
    bands = []
    for lat in range(8):
        s = got_ref[lat, :32].astype(F32)
        for j in range(1, 8):
            s = s + got_ref[j * 8 + lat, :32].astype(F32)
        bands.append(s)
        total = total + s
    by_lat = jnp.logical_or(relay < EAST_AT // HALO, relay >= CORNER_AT // HALO).astype(jnp.int32)
    by_lon = jnp.logical_and(relay >= EAST_AT // HALO, lax.axis_index("c") == 1).astype(jnp.int32)
    for lat in range(8):
        s = jnp.where(is_bias > 0.5, bands[lat], total).astype(BF)
        from_lat = lax.rem(lat + 7 * by_lat, 8)
        for j in range(8):
            out_ref[j * 8 + lat, :32] = s
            out_ref[j * 8 + lat, 32:] = got_ref[lax.rem(j + 7 * by_lon, 8) * 8 + from_lat, 32:]


def finish_kernel(
    a_ref, b_ref, own_ref,
    dx_ref, dg1_ref, dqkv_ref, dproj_ref, dg2_ref, dup_ref, ddown_ref, dt_ref,
    m_acc, table, g_acc, line, lines, flat, grad_scale,
):
    core = lax.axis_index("c")
    a_half = pl.multiple_of(core * 288, 32)
    b_half = pl.multiple_of((1 - core) * 288, 32)
    for i in range(9):
        for b in range(6):
            cols = slice(b * 128, (b + 1) * 128)
            m_acc[pl.ds(a_half + 32 * i, 32), cols] = a_ref[i * 6 + b, :32].astype(F32) * grad_scale
            m_acc[pl.ds(b_half + 32 * i, 32), cols] = b_ref[i * 6 + b, :32].astype(F32) * grad_scale
    for ref, half in ((a_ref, core), (b_ref, 1 - core)):

        @pl.when(half == 0)
        def _(ref=ref):
            for k in range(5):
                table[k % 3, 32 * (k // 3) : 32 * (k // 3) + 32, :] = ref[W_CHUNKS + k, :32].astype(F32)
            g_acc[:, :128] = ref[W_CHUNKS + B_CHUNKS, :32].astype(F32) * grad_scale
            g_acc[:, 128:] = ref[W_CHUNKS + B_CHUNKS + 1, :32].astype(F32) * grad_scale

        @pl.when(half == 1)
        def _(ref=ref):
            for k in range(5, 9):
                table[k % 3, 32 * (k // 3) : 32 * (k // 3) + 32, :] = ref[W_CHUNKS + k - 5, :32].astype(F32)

    dqkv_ref[...] = m_acc[:D, : 3 * D]
    dproj_ref[...] = m_acc[:D, 3 * D :]
    dup_ref[...] = m_acc[D : 2 * D, :]
    ddown_ref[...] = m_acc[2 * D :, :]
    d_gain = (a_ref[GAIN_AT, :32].astype(F32) + b_ref[GAIN_AT, :32].astype(F32)) * grad_scale
    dg1_ref[:, :128] = d_gain[0:1, :]
    dg1_ref[:, 128:] = d_gain[1:2, : D - 128]
    dg2_ref[...] = g_acc[1:2, :D]
    for li in range(2):
        for ai in range(WIN_LAT):
            place = li * WIN_LAT + ai
            rows = jnp.concatenate([table[b, place * 8 : place * 8 + 8, :] for b in range(3)], axis=1)
            for lj in range(2):
                off = ((li * 2 + lj) * WIN_LAT + ai) * LINE
                lines[:, off : off + LINE] = rows[:, lj * LINE : (lj + 1) * LINE]
    for h in range(HEADS):
        dt_ref[h] = lines[h : h + 1, :]

    for k in range(64):
        ref = a_ref if k < EAST_AT // HALO else b_ref
        flat[HALO * k : HALO * (k + 1), :] = ref[k, 32:].astype(F32)
    inner = COLS - HALF_LON
    for r in range(HALF_LAT):
        north = open_pair(flat, NORTH_AT + r * 3 * inner, inner)
        east = open_pair(flat, EAST_AT + r * 3 * HALF_LON, HALF_LON)
        corner = open_pair(flat, CORNER_AT + r * 3 * HALF_LON, HALF_LON)
        for l in range(2):
            line[...] = own_ref[l, r].astype(F32)
            line[:HALF_LON, :] = east[l]
            dx_ref[l, r + HALF_LAT] = line[...].astype(BF)
            line[HALF_LON:, :] = north[l]
            line[:HALF_LON, :] = corner[l]
            dx_ref[l, r] = line[...].astype(BF)


def shift_pairs(lon_by, lat_by):
    pairs = []
    for lon in range(16):
        for lat in range(8):
            pairs.append((lon * 8 + lat, ((lon + lon_by) % 16) * 8 + (lat + lat_by) % 8))
    return pairs


def one_axis(length, by):
    return [(i, (i + by) % length) for i in range(length)]


def vmem_spec():
    return pl.BlockSpec(memory_space=pltpu.VMEM)


def prepare(table, weights):
    shape = jax.ShapeDtypeStruct
    return pl.pallas_call(
        prepare_kernel,
        out_shape=(shape((HEADS, WIN, WIN), F32), shape((3 * D, D), BF)),
        in_specs=[vmem_spec()] * 2,
        out_specs=[vmem_spec()] * 2,
        scratch_shapes=[
            pltpu.VMEM((3, 8 * RA, 128), F32),
            pltpu.VMEM((8, POSITIONS), F32),
            pltpu.VMEM((HEADS, WIN, WIN), F32),
        ],
        compiler_params=pltpu.CompilerParams(vmem_limit_bytes=VMEM),
    )(table, weights)


def pack_halos(both):
    shape = jax.ShapeDtypeStruct
    return pl.pallas_call(
        pack_kernel,
        out_shape=(
            shape((2, HALF_LAT, 128, 128), BF),
            shape((2, HALF_LAT, 3, HALF_LON, 128), BF),
            shape((2, HALF_LAT, 3, HALF_LON, 128), BF),
        ),
        in_specs=[vmem_spec()],
        out_specs=[vmem_spec()] * 3,
        compiler_params=pltpu.CompilerParams(vmem_limit_bytes=VMEM),
    )(both)


def run_block(both, na, nb, nc, weights, w_qkv_t, table, bias):
    shape = jax.ShapeDtypeStruct
    return pl.pallas_call(
        block_kernel,
        out_shape=(
            shape((64, 32, 128), BF),
            shape((64, 32, 128), BF),
            shape((WINDOWS, 3 * D, WIN), BF),
            shape((TOK, D), F32),
            shape((2, 54 * RA, 128), F32),
        ),
        in_specs=[vmem_spec()] * 8,
        out_specs=[vmem_spec()] * 5,
        scratch_shapes=[
            pltpu.VMEM((2, 54 * RA, 128), F32),
            pltpu.VMEM((WINDOWS, HEADS, WIN, WIN), BF),
            pltpu.VMEM((WINDOWS, 3 * D, WIN), BF),
            pltpu.VMEM((WINDOWS, D, WIN), BF),
            pltpu.VMEM((WINDOWS, D, WIN), BF),
            pltpu.VMEM((TOK, 2 * D), BF),
            pltpu.VMEM((WINDOWS * HEADS, WIN, WIN), BF),
            pltpu.VMEM((TOK, D), BF),
            pltpu.VMEM((HEADS, WIN, WIN), F32),
            pltpu.VMEM((3 * D, MLP), BF),
            pltpu.VMEM((32, 256), F32),
            pltpu.VMEM((HEADS * RA, 384), F32),
            pltpu.VMEM((3, 8 * RA, 128), F32),
        ],
        compiler_params=pltpu.CompilerParams(vmem_limit_bytes=VMEM),
    )(both, na, nb, nc, weights, w_qkv_t, table, bias)


def input_grad(d_packed_t, d_hidden, tokens, weights, table):
    shape = jax.ShapeDtypeStruct
    return pl.pallas_call(
        grad_kernel,
        out_shape=(
            shape((2, HALF_LAT, COLS, D), BF),
            shape((64, HALO, 128), BF),
            shape((32, 128), BF),
        ),
        in_specs=[vmem_spec()] * 5,
        out_specs=[vmem_spec()] * 3,
        scratch_shapes=[pltpu.VMEM((2, 54 * RA, 128), F32), pltpu.VMEM((FLAT, 128), F32)],
        compiler_params=pltpu.CompilerParams(vmem_limit_bytes=VMEM),
    )(d_packed_t, d_hidden, tokens, weights, table)


def local(tokens, cotangent, ln1_gain, w_qkv, w_proj, ln2_gain, w_up, w_down, bias_table):
    edge = ((0, 0),) * 3
    both = jnp.pad(tokens, ((0, 2),) + edge) + jnp.pad(cotangent, ((2, 0),) + edge)
    part_a, part_b, part_c = pack_halos(both)
    na = lax.ppermute(part_a, LAT, one_axis(8, -1))
    nb = lax.ppermute(part_b, LON, one_axis(16, -1))
    nc = lax.ppermute(part_c, LON + LAT, shift_pairs(-1, -1))

    weights = jnp.concatenate((w_qkv, w_proj, w_up, w_down.T), axis=1)
    gains = jnp.pad(jnp.stack((ln1_gain, ln2_gain)), ((0, 0), (0, POSITIONS - D)))
    table = jnp.concatenate((bias_table.reshape(HEADS, 1, POSITIONS), gains[:, None]), axis=0)
    bias, w_qkv_t = prepare(table, weights)
    mine, send, d_packed_t, d_hidden, shifted = run_block(both, na, nb, nc, weights, w_qkv_t, table, bias)

    pair = [(0, 1), (1, 0)]
    got = lax.ppermute(send, "c", pair)
    own, halo, gain = input_grad(d_packed_t, d_hidden, shifted, weights, table)
    chunks = jax.ShapeDtypeStruct((64, 32 + HALO, 128), BF)
    joined = pl.pallas_call(
        join_kernel,
        out_shape=chunks,
        in_specs=[vmem_spec()] * 4,
        out_specs=vmem_spec(),
        compiler_params=pltpu.CompilerParams(vmem_limit_bytes=VMEM),
    )(mine, got, halo, gain)
    spread = lax.all_to_all(joined, CHIPS, 0, 0, tiled=True)
    reply = pl.pallas_call(
        reply_kernel,
        out_shape=chunks,
        in_specs=[vmem_spec()],
        out_specs=vmem_spec(),
        compiler_params=pltpu.CompilerParams(vmem_limit_bytes=VMEM),
    )(spread)
    half_a = lax.all_to_all(reply, CHIPS, 0, 0, tiled=True)
    half_b = lax.ppermute(half_a, "c", pair)
    shape = jax.ShapeDtypeStruct
    total_tokens = 128 * tokens.shape[0] * tokens.shape[1] * tokens.shape[2]
    dx, dg1, dqkv, dproj, dg2, dup, ddown, dt = pl.pallas_call(
        functools.partial(finish_kernel, grad_scale=1.0 / math.sqrt(total_tokens)),
        out_shape=(
            shape(tokens.shape, BF),
            shape((1, D), F32),
            shape((D, 3 * D), F32),
            shape((D, D), F32),
            shape((1, D), F32),
            shape((D, MLP), F32),
            shape((D, MLP), F32),
            shape((HEADS, 1, POSITIONS), F32),
        ),
        in_specs=[vmem_spec()] * 3,
        out_specs=[vmem_spec()] * 8,
        scratch_shapes=[
            pltpu.VMEM((3 * D, MLP), F32),
            pltpu.VMEM((3, 8 * RA, 128), F32),
            pltpu.VMEM((32, 256), F32),
            pltpu.VMEM((COLS, D), F32),
            pltpu.VMEM((8, POSITIONS), F32),
            pltpu.VMEM((FLAT, 128), F32),
        ],
        compiler_params=pltpu.CompilerParams(vmem_limit_bytes=VMEM),
    )(half_a, half_b, own)
    return (
        dx,
        dg1.reshape(D),
        dqkv,
        dproj,
        dg2.reshape(D),
        dup,
        ddown.T,
        dt.reshape(1, HEADS, POSITIONS),
    )


def solution(mesh):
    parts = Mesh(mesh.devices.reshape(4, 2, 2, 2, 4), ("y", "zh", "c", "zl", "x"))
    grid = P(None, LAT, LON, None)
    in_specs = (grid, grid, P(), P(), P(), P(), P(), P(), P(LAT, None, None))
    out_specs = (grid, P(), P(), P(), P(), P(), P(), P(LAT, None, None))
    return jax.shard_map(local, mesh=parts, in_specs=in_specs, out_specs=out_specs, check_vma=False)
```

```python
import functools
import math

import jax
import jax.numpy as jnp
from jax import lax
from jax.experimental import pallas as pl
from jax.experimental.pallas import tpu as pltpu
from jax.sharding import Mesh
from jax.sharding import PartitionSpec as P

BF = jnp.bfloat16
F32 = jnp.float32
D = 192
HEADS = 6
DH = 32
MLP = 768
WIN_LAT = 6
WIN_LON = 12
HALF_LAT = 3
HALF_LON = 6
RA = 12
WIN = 144
COLS = 48
INNER = COLS - HALF_LON
WINDOWS = 4
OFFS = 2 * WIN_LON - 1
SPAN = OFFS * RA
LINE = WIN_LAT * OFFS
POSITIONS = 4 * WIN_LAT * LINE
SCALE = DH ** (-0.5)
W_CHUNKS = 54
GAIN_AT = 61
HALO = 8
NORTH_AT, EAST_AT, CORNER_AT, FLAT = 0, 384, 440, 512
B_CHUNKS = 5
VMEM = 24 * 1024 * 1024
LOG2E = 1.0 / math.log(2.0)
UNROLL = True
GROUP = 2
TOK = WINDOWS * WIN

LON = ("y", "zh", "c")
LAT = ("zl", "x")
CHIPS = ("y", "zh", "zl", "x")


def nn(a, b):
    return lax.dot_general(a, b, (((1,), (0,)), ((), ())), preferred_element_type=F32)


def nt(a, b):
    return lax.dot_general(a, b, (((1,), (1,)), ((), ())), preferred_element_type=F32)


def tn(a, b):
    return lax.dot_general(a, b, (((0,), (0,)), ((), ())), preferred_element_type=F32)


def put_rows(dst, start, count, rows):
    rows = rows.astype(F32)
    spare = jnp.zeros((count, 256 - D), F32)
    dst[0, pl.ds(start, count, stride=RA), :] = rows[:, :128]
    dst[1, pl.ds(start, count, stride=RA), :] = jnp.concatenate((rows[:, 128:], spare), axis=1)


def put_parts(xs, ys, start, count, parts):
    rows = pl.ds(start, count, stride=RA)
    xs[0, rows, :] = parts[0]
    ys[0, rows, :] = parts[1]
    xs[1, rows, :] = parts[2]
    ys[1, rows, :] = pltpu.roll(parts[2], 64, 1)


def put_pair(xs, ys, start, count, ref, l, r):
    put_parts(xs, ys, start, count, [ref[l, r, k].astype(F32) for k in range(3)])


def take_pair(src, flat, at, first, second, count):
    first = pl.ds(first, count, stride=RA)
    second = pl.ds(second, count, stride=RA)
    lane = lax.broadcasted_iota(jnp.int32, (count, 128), 1)
    flat[at : at + count, :] = src[0, first, :]
    flat[at + count : at + 2 * count, :] = src[0, second, :]
    flat[at + 2 * count : at + 3 * count, :] = jnp.where(
        lane < 64, src[1, first, :], pltpu.roll(src[1, second, :], 64, 1)
    )


def open_pair(flat, at, count):
    pair = flat[at + 2 * count : at + 3 * count, :]
    return (
        jnp.concatenate((flat[at : at + count, :], pair[:, :64]), axis=1),
        jnp.concatenate((flat[at + count : at + 2 * count, :], pair[:, 64:]), axis=1),
    )


def get_rows(src, start, count):
    low = src[0, pl.ds(start, count, stride=RA), :]
    high = src[1, pl.ds(start, count, stride=RA), :]
    return jnp.concatenate((low, high[:, : D - 128]), axis=1).astype(BF)


def token_rows(src, start, count):
    return jnp.concatenate((src[0, start : start + count, :], src[1, start : start + count, : D - 128]), axis=1)


def each_window(body):
    if UNROLL:
        for w in range(0, WINDOWS, GROUP):
            body(range(w, w + GROUP))
    else:
        pl.loop(0, WINDOWS)(body)


def norm_stats(values):
    mean = jnp.mean(values, axis=-1, keepdims=True)
    centred = values - mean
    variance = jnp.mean(centred * centred, axis=-1, keepdims=True)
    rstd = lax.rsqrt(variance + 1e-05)
    return centred * rstd, rstd


def gelu_pair(u):
    cdf = 0.5 + 0.5 * lax.erf(u * (0.5**0.5))
    slope = cdf + u * jnp.exp(-0.5 * u * u) * (1.0 / math.sqrt(2.0 * math.pi))
    return u * cdf, slope


def norm_back(d_hat, hat, rstd):
    m1 = jnp.mean(d_hat, axis=-1, keepdims=True)
    m2 = jnp.mean(d_hat * hat, axis=-1, keepdims=True)
    return rstd * (d_hat - m1 - hat * m2)


def pack_kernel(both_ref, pa_ref, pb_ref, pc_ref):
    def parts(l, row, cols):
        x = both_ref[l, row].astype(F32)[cols]
        dy = both_ref[2 + l, row].astype(F32)[cols]
        return [x[:, :128], dy[:, :128], jnp.concatenate((x[:, 128:], dy[:, 128:]), axis=1)]

    for l in range(2):
        for r in range(HALF_LAT):
            rows = parts(l, r, slice(HALF_LON, COLS)) + [jnp.zeros((128 - 3 * INNER, 128), F32)]
            pa_ref[l, r] = jnp.concatenate(rows, axis=0).astype(BF)
            for k, rows in enumerate(parts(l, r + HALF_LAT, slice(0, HALF_LON))):
                pb_ref[l, r, k] = rows.astype(BF)
            for k, rows in enumerate(parts(l, r, slice(0, HALF_LON))):
                pc_ref[l, r, k] = rows.astype(BF)


def diagonal_order():
    row = lax.broadcasted_iota(jnp.int32, (SPAN, SPAN), 0)
    col = lax.broadcasted_iota(jnp.int32, (SPAN, SPAN), 1)
    step = lax.shift_right_logical(col * 5462, 16)
    return jnp.where(row == (col - step * RA) * OFFS + OFFS - 1 - step, 1.0, 0.0).astype(BF)


def prepare_kernel(table_ref, w_ref, bias_ref, wqkvt_ref, table, lines, rows_first):
    last = lax.axis_index(LAT) == lax.axis_size(LAT) - 1
    wqkvt_ref[...] = w_ref[:, : 3 * D].T
    for h in range(HEADS):
        lines[h : h + 1, :] = table_ref[h]
    table[...] = jnp.zeros_like(table)
    for li in range(2):
        for ai in range(WIN_LAT):
            place = li * WIN_LAT + ai
            parts = []
            for lj in range(2):
                off = ((li * 2 + lj) * WIN_LAT + ai) * LINE
                parts.append(lines[:, off : off + LINE])
            parts.append(jnp.zeros((8, 384 - SPAN), F32))
            both = jnp.concatenate(parts, axis=1)
            for b in range(3):
                table[b, place * 8 : place * 8 + 8, :] = both[:, 128 * b : 128 * (b + 1)]
    t2 = jnp.concatenate((table[0], table[1], table[2, :, : SPAN - 256]), axis=1)
    hi = t2.astype(BF)
    rest = t2 - hi.astype(F32)
    mid = rest.astype(BF)
    low = (rest - mid.astype(F32)).astype(BF)
    perm = diagonal_order()
    wide = (nn(hi, perm) + nn(mid, perm) + nn(low, perm)) * LOG2E
    wide = jnp.concatenate((wide, jnp.zeros((8 * RA, 384 - SPAN), F32)), axis=1)
    for b in range(3):
        table[b] = wide[:, 128 * b : 128 * (b + 1)]
    key_late = lax.rem(lax.broadcasted_iota(jnp.int32, (WIN, WIN), 0), WIN_LAT) >= HALF_LAT
    query_late = lax.rem(lax.broadcasted_iota(jnp.int32, (WIN, WIN), 1), WIN_LAT) >= HALF_LAT
    split = jnp.logical_and(key_late != query_late, last)
    mask_rows = jnp.where(split, -1e9 * LOG2E, 0.0)
    for h in range(HEADS):
        wide_h = jnp.concatenate([table[b, pl.ds(h, RA, stride=8), :] for b in range(3)], axis=1)
        for oi in range(WIN_LON):
            start = (WIN_LON - 1 - oi) * RA
            rows_first[h, oi * RA : (oi + 1) * RA, :] = wide_h[:, start : start + WIN]
    for h in range(HEADS):
        bias_ref[h] = rows_first[h].T + mask_rows


def block_kernel(
    both_ref, na_ref, nb_ref, nc_ref, w_ref, wqkvt, table_ref, bias,
    mine_ref, send_ref, dp_t, hid, xs,
    ys, probs, heads_t, o_t, do_t, kvs, dss,
    n1s, d_bias, m_acc, g_acc, dw, table,
):
    for l in range(2):
        for r in range(HALF_LAT):
            put_rows(xs, l * 6 + r, COLS, both_ref[l, r + HALF_LAT])
            put_rows(ys, l * 6 + r, COLS, both_ref[2 + l, r + HALF_LAT])
            north = na_ref[l, r].astype(F32)
            north = [north[k * INNER : (k + 1) * INNER] for k in range(3)]
            put_parts(xs, ys, HALF_LON * RA + l * 6 + r + HALF_LAT, INNER, north)
            put_pair(xs, ys, COLS * RA + l * 6 + r, HALF_LON, nb_ref, l, r)
            put_pair(xs, ys, COLS * RA + l * 6 + r + HALF_LAT, HALF_LON, nc_ref, l, r)

    d_bias[...] = jnp.zeros_like(d_bias)
    g_acc[...] = jnp.zeros_like(g_acc)

    g1 = table_ref[HEADS][:, :D]
    g2 = table_ref[HEADS + 1][:, :D]
    w_proj = w_ref[:, 3 * D : 4 * D]
    first = HALF_LON * RA

    hat1, rstd1 = norm_stats(token_rows(xs, first, TOK))
    n1 = (hat1 * g1).astype(BF)
    n1s[...] = n1
    kvs[...] = nn(n1, w_ref[:, D : 3 * D]).astype(BF)

    def attend(ws):
        jobs = [(w, h) for w in ws for h in range(HEADS)]
        rows = {w: pl.ds(w * WIN, WIN) for w in ws}
        parts = [slice(h * DH, (h + 1) * DH) for h in range(HEADS)]
        scores = [
            nn(kvs[rows[w], parts[h]], heads_t[w, parts[h], :]) * (SCALE * LOG2E) + bias[h] for w, h in jobs
        ]
        tops = [jnp.max(s, axis=0, keepdims=True) for s in scores]
        powers = [jnp.exp2(s - top) for s, top in zip(scores, tops)]
        shares = [1.0 / jnp.sum(e, axis=0, keepdims=True) for e in powers]
        for k, (w, h) in enumerate(jobs):
            probs[w, h] = (powers[k] * shares[k]).astype(BF)
        for w, h in jobs:
            o_t[w, parts[h], :] = nn(heads_t[w, 2 * D + h * DH : 2 * D + (h + 1) * DH, :], probs[w, h]).astype(BF)

    for w in range(WINDOWS):
        heads_t[w] = nt(wqkvt[...], n1[w * WIN : (w + 1) * WIN]).astype(BF)
    each_window(attend)
    for w in range(WINDOWS):
        hid[w * WIN : (w + 1) * WIN, :] = tn(o_t[w], w_proj)

    hidden = token_rows(xs, first, TOK) + hid[...]
    hat2, rstd2 = norm_stats(hidden)
    n2 = (hat2 * g2).astype(BF)
    n2_t = n2.T
    dy = token_rows(ys, first, TOK)
    dyb = dy.astype(BF)
    dy_t = dyb.T
    d_n2 = jnp.zeros((TOK, D), F32)
    for j in range(3):
        cols = slice(j * 256, (j + 1) * 256)
        act, slope = gelu_pair(nn(n2, w_ref[:, 4 * D + j * 256 : 4 * D + (j + 1) * 256]))
        d_act = nn(dyb, w_ref[:, 4 * D + MLP + j * 256 : 4 * D + MLP + (j + 1) * 256]).astype(BF).astype(F32)
        d_u = (d_act * slope).astype(BF)
        m_acc[2 * D :, cols] = nn(dy_t, act.astype(BF)).astype(BF)
        m_acc[D : 2 * D, cols] = nn(n2_t, d_u).astype(BF)
        d_n2 = d_n2 + nt(d_u, w_ref[:, 4 * D + j * 256 : 4 * D + (j + 1) * 256])
    d_n2 = d_n2.astype(BF).astype(F32)
    g_acc[1:2, :D] = jnp.sum(d_n2 * hat2, axis=0, keepdims=True)
    d_hidden = dy + norm_back(d_n2 * g2, hat2, rstd2)
    dhb = d_hidden.astype(BF)
    hid[...] = d_hidden
    d_proj = jnp.zeros((D, D), F32)
    for w in range(WINDOWS):
        rows = slice(w * WIN, (w + 1) * WIN)
        d_proj = d_proj + nn(o_t[w], dhb[rows])
        do_t[w] = nt(w_proj, dhb[rows]).astype(BF)

    def attend_back(ws):
        jobs = [(w, h) for w in ws for h in range(HEADS)]
        rows = {w: pl.ds(w * WIN, WIN) for w in ws}
        parts = [slice(h * DH, (h + 1) * DH) for h in range(HEADS)]
        d_probs = [
            nn(kvs[rows[w], D + h * DH : D + (h + 1) * DH], do_t[w, parts[h], :]) for w, h in jobs
        ]
        for k, (w, h) in enumerate(jobs):
            pf = probs[w, h].astype(F32)
            prod = pf * d_probs[k]
            ds = prod - pf * jnp.sum(prod, axis=0, keepdims=True)
            d_bias[h] = d_bias[h] + ds
            dss[k] = ds.astype(BF)
        for k, (w, h) in enumerate(jobs):
            part = parts[h]
            q_t = heads_t[w, part, :]
            k_t = heads_t[w, D + h * DH : D + (h + 1) * DH, :]
            dp_t[w, part, :] = (nn(k_t, dss[k]) * SCALE).astype(BF)
            dp_t[w, D + h * DH : D + (h + 1) * DH, :] = (nt(q_t, dss[k]) * SCALE).astype(BF)
            dp_t[w, 2 * D + h * DH : 2 * D + (h + 1) * DH, :] = nt(do_t[w, part, :], probs[w, h]).astype(BF)

    each_window(attend_back)

    core = lax.axis_index("c")
    perm = diagonal_order()
    dw[...] = jnp.zeros_like(dw)
    d_qkv = jnp.zeros((3 * D, D), F32)
    for w in range(WINDOWS):
        d_qkv = d_qkv + nn(dp_t[w], n1s[w * WIN : (w + 1) * WIN, :])
    m_acc[:D, :] = jnp.concatenate((d_qkv.T, d_proj), axis=1).astype(BF)

    for h in range(HEADS):
        d_bias[h] = d_bias[h].T
    for oi in range(WIN_LON):
        start = (WIN_LON - 1 - oi) * RA
        for h in range(HEADS):
            dw[h * RA : (h + 1) * RA, start : start + WIN] += d_bias[h, oi * RA : (oi + 1) * RA, :]
    dwv = dw[:, :SPAN]
    dw_hi = dwv.astype(BF)
    dw_lo = (dwv - dw_hi.astype(F32)).astype(BF)
    d_t2 = nt(dw_hi, perm) + nt(dw_lo, perm)
    d_t2 = jnp.concatenate((d_t2, jnp.zeros((HEADS * RA, 384 - SPAN), F32)), axis=1)
    table[...] = jnp.zeros_like(table)
    for h in range(HEADS):
        for b in range(3):
            table[b, pl.ds(h, RA, stride=8), :] = d_t2[h * RA : (h + 1) * RA, 128 * b : 128 * (b + 1)]

    mine_half = pl.multiple_of(core * 288, 32)
    send_half = pl.multiple_of((1 - core) * 288, 32)
    for i in range(9):
        for b in range(6):
            cols = slice(b * 128, (b + 1) * 128)
            mine_ref[i * 6 + b] = m_acc[pl.ds(mine_half + 32 * i, 32), cols]
            send_ref[i * 6 + b] = m_acc[pl.ds(send_half + 32 * i, 32), cols]
    zero = jnp.zeros((32, 128), BF)
    for ref, half in ((mine_ref, core), (send_ref, 1 - core)):
        for k in range(W_CHUNKS, 64):
            ref[k] = zero

        @pl.when(half == 0)
        def _(ref=ref):
            for k in range(5):
                ref[W_CHUNKS + k] = table[k % 3, 32 * (k // 3) : 32 * (k // 3) + 32, :].astype(BF)
            ref[W_CHUNKS + B_CHUNKS] = g_acc[:, :128].astype(BF)
            ref[W_CHUNKS + B_CHUNKS + 1] = g_acc[:, 128:].astype(BF)

        @pl.when(half == 1)
        def _(ref=ref):
            for k in range(5, 9):
                ref[W_CHUNKS + k - 5] = table[k % 3, 32 * (k // 3) : 32 * (k // 3) + 32, :].astype(BF)


def grad_kernel(dp_t, hid, xs, w_ref, table_ref, own_ref, halo_ref, gain_ref, gs, flat):
    g1 = table_ref[HEADS][:, :D]
    first = HALF_LON * RA
    gs[:, :first, :] = jnp.zeros((2, first, 128), F32)
    d_n1 = []
    for w in range(WINDOWS):
        d_n1.append(nn(w_ref[:, : 3 * D], dp_t[w]).T)
    d_n1 = jnp.concatenate(d_n1, axis=0).astype(BF).astype(F32)
    hat1, rstd1 = norm_stats(token_rows(xs, first, TOK))
    d_gain = jnp.sum(d_n1 * hat1, axis=0, keepdims=True)
    spare = jnp.zeros((1, 256 - D), F32)
    gain_ref[...] = jnp.concatenate(
        (d_gain[:, :128], jnp.concatenate((d_gain[:, 128:], spare), axis=1), jnp.zeros((30, 128), F32)), axis=0
    ).astype(BF)
    d_x = hid[...] + norm_back(d_n1 * g1, hat1, rstd1)
    gs[0, first:, :] = d_x[:, :128]
    gs[1, first:, : D - 128] = d_x[:, 128:]

    for l in range(2):
        for r in range(HALF_LAT):
            own_ref[l, r] = get_rows(gs, l * 6 + r, COLS)

    flat[...] = jnp.zeros_like(flat)
    inner = COLS - HALF_LON
    for r in range(HALF_LAT):
        late = r + HALF_LAT
        take_pair(gs, flat, NORTH_AT + r * 3 * inner, first + late, first + 6 + late, inner)
        take_pair(gs, flat, EAST_AT + r * 3 * HALF_LON, COLS * RA + r, COLS * RA + r + 6, HALF_LON)
        take_pair(gs, flat, CORNER_AT + r * 3 * HALF_LON, COLS * RA + late, COLS * RA + late + 6, HALF_LON)
    for k in range(64):
        halo_ref[k] = flat[HALO * k : HALO * (k + 1), :].astype(BF)


def join_kernel(mine_ref, got_ref, halo_ref, gain_ref, out_ref):
    for k in range(64):
        if k != GAIN_AT:
            out_ref[k, :32] = (mine_ref[k].astype(F32) + got_ref[k].astype(F32)).astype(BF)
        out_ref[k, 32:] = halo_ref[k]
    out_ref[GAIN_AT, :32] = gain_ref[...]


def reply_kernel(got_ref, out_ref):
    relay = lax.axis_index(CHIPS)
    is_bias = jnp.logical_and(relay >= W_CHUNKS, relay < W_CHUNKS + B_CHUNKS).astype(F32)
    total = jnp.zeros((32, 128), F32)
    bands = []
    for lat in range(8):
        s = got_ref[lat, :32].astype(F32)
        for j in range(1, 8):
            s = s + got_ref[j * 8 + lat, :32].astype(F32)
        bands.append(s)
        total = total + s
    by_lat = jnp.logical_or(relay < EAST_AT // HALO, relay >= CORNER_AT // HALO).astype(jnp.int32)
    by_lon = jnp.logical_and(relay >= EAST_AT // HALO, lax.axis_index("c") == 1).astype(jnp.int32)
    for lat in range(8):
        s = jnp.where(is_bias > 0.5, bands[lat], total).astype(BF)
        from_lat = lax.rem(lat + 7 * by_lat, 8)
        for j in range(8):
            out_ref[j * 8 + lat, :32] = s
            out_ref[j * 8 + lat, 32:] = got_ref[lax.rem(j + 7 * by_lon, 8) * 8 + from_lat, 32:]


def finish_kernel(
    a_ref, b_ref, own_ref,
    dx_ref, dg1_ref, dqkv_ref, dproj_ref, dg2_ref, dup_ref, ddown_ref, dt_ref,
    table, g_acc, line, lines, flat, grad_scale,
):
    core = lax.axis_index("c")
    for block in range(18):
        mine = core == block // 9
        tiles = []
        for b in range(6):
            chunk = block % 9 * 6 + b
            tiles.append(jnp.where(mine, a_ref[chunk, :32].astype(F32), b_ref[chunk, :32].astype(F32)) * grad_scale)
        rows = slice(block % 6 * 32, block % 6 * 32 + 32)
        if block < 6:
            for b in range(4):
                dqkv_ref[rows, b * 128 : (b + 1) * 128] = tiles[b]
            dqkv_ref[rows, 512:] = tiles[4][:, :64]
            dproj_ref[rows, :] = jnp.concatenate((tiles[4][:, 64:], tiles[5]), axis=1)
        else:
            out = dup_ref if block < 12 else ddown_ref
            for b in range(6):
                out[rows, b * 128 : (b + 1) * 128] = tiles[b]
    for ref, half in ((a_ref, core), (b_ref, 1 - core)):

        @pl.when(half == 0)
        def _(ref=ref):
            for k in range(5):
                table[k % 3, 32 * (k // 3) : 32 * (k // 3) + 32, :] = ref[W_CHUNKS + k, :32].astype(F32)
            g_acc[:, :128] = ref[W_CHUNKS + B_CHUNKS, :32].astype(F32) * grad_scale
            g_acc[:, 128:] = ref[W_CHUNKS + B_CHUNKS + 1, :32].astype(F32) * grad_scale

        @pl.when(half == 1)
        def _(ref=ref):
            for k in range(5, 9):
                table[k % 3, 32 * (k // 3) : 32 * (k // 3) + 32, :] = ref[W_CHUNKS + k - 5, :32].astype(F32)

    d_gain = (a_ref[GAIN_AT, :32].astype(F32) + b_ref[GAIN_AT, :32].astype(F32)) * grad_scale
    dg1_ref[:, :128] = d_gain[0:1, :]
    dg1_ref[:, 128:] = d_gain[1:2, : D - 128]
    dg2_ref[...] = g_acc[1:2, :D]
    for li in range(2):
        for ai in range(WIN_LAT):
            place = li * WIN_LAT + ai
            rows = jnp.concatenate([table[b, place * 8 : place * 8 + 8, :] for b in range(3)], axis=1)
            for lj in range(2):
                off = ((li * 2 + lj) * WIN_LAT + ai) * LINE
                lines[:, off : off + LINE] = rows[:, lj * LINE : (lj + 1) * LINE]
    for h in range(HEADS):
        dt_ref[h] = lines[h : h + 1, :]

    for k in range(64):
        ref = a_ref if k < EAST_AT // HALO else b_ref
        flat[HALO * k : HALO * (k + 1), :] = ref[k, 32:].astype(F32)
    inner = COLS - HALF_LON
    for r in range(HALF_LAT):
        north = open_pair(flat, NORTH_AT + r * 3 * inner, inner)
        east = open_pair(flat, EAST_AT + r * 3 * HALF_LON, HALF_LON)
        corner = open_pair(flat, CORNER_AT + r * 3 * HALF_LON, HALF_LON)
        for l in range(2):
            line[...] = own_ref[l, r].astype(F32)
            line[:HALF_LON, :] = east[l]
            dx_ref[l, r + HALF_LAT] = line[...].astype(BF)
            line[HALF_LON:, :] = north[l]
            line[:HALF_LON, :] = corner[l]
            dx_ref[l, r] = line[...].astype(BF)


def shift_pairs(lon_by, lat_by):
    pairs = []
    for lon in range(16):
        for lat in range(8):
            pairs.append((lon * 8 + lat, ((lon + lon_by) % 16) * 8 + (lat + lat_by) % 8))
    return pairs


def one_axis(length, by):
    return [(i, (i + by) % length) for i in range(length)]


def vmem_spec():
    return pl.BlockSpec(memory_space=pltpu.VMEM)


def prepare(table, weights):
    shape = jax.ShapeDtypeStruct
    return pl.pallas_call(
        prepare_kernel,
        out_shape=(shape((HEADS, WIN, WIN), F32), shape((3 * D, D), BF)),
        in_specs=[vmem_spec()] * 2,
        out_specs=[vmem_spec()] * 2,
        scratch_shapes=[
            pltpu.VMEM((3, 8 * RA, 128), F32),
            pltpu.VMEM((8, POSITIONS), F32),
            pltpu.VMEM((HEADS, WIN, WIN), F32),
        ],
        compiler_params=pltpu.CompilerParams(vmem_limit_bytes=VMEM),
    )(table, weights)


def pack_halos(both):
    shape = jax.ShapeDtypeStruct
    return pl.pallas_call(
        pack_kernel,
        out_shape=(
            shape((2, HALF_LAT, 128, 128), BF),
            shape((2, HALF_LAT, 3, HALF_LON, 128), BF),
            shape((2, HALF_LAT, 3, HALF_LON, 128), BF),
        ),
        in_specs=[vmem_spec()],
        out_specs=[vmem_spec()] * 3,
        compiler_params=pltpu.CompilerParams(vmem_limit_bytes=VMEM),
    )(both)


def run_block(both, na, nb, nc, weights, w_qkv_t, table, bias):
    shape = jax.ShapeDtypeStruct
    return pl.pallas_call(
        block_kernel,
        out_shape=(
            shape((64, 32, 128), BF),
            shape((64, 32, 128), BF),
            shape((WINDOWS, 3 * D, WIN), BF),
            shape((TOK, D), F32),
            shape((2, 54 * RA, 128), F32),
        ),
        in_specs=[vmem_spec()] * 8,
        out_specs=[vmem_spec()] * 5,
        scratch_shapes=[
            pltpu.VMEM((2, 54 * RA, 128), F32),
            pltpu.VMEM((WINDOWS, HEADS, WIN, WIN), BF),
            pltpu.VMEM((WINDOWS, 3 * D, WIN), BF),
            pltpu.VMEM((WINDOWS, D, WIN), BF),
            pltpu.VMEM((WINDOWS, D, WIN), BF),
            pltpu.VMEM((TOK, 2 * D), BF),
            pltpu.VMEM((WINDOWS * HEADS, WIN, WIN), BF),
            pltpu.VMEM((TOK, D), BF),
            pltpu.VMEM((HEADS, WIN, WIN), F32),
            pltpu.VMEM((3 * D, MLP), BF),
            pltpu.VMEM((32, 256), F32),
            pltpu.VMEM((HEADS * RA, 384), F32),
            pltpu.VMEM((3, 8 * RA, 128), F32),
        ],
        compiler_params=pltpu.CompilerParams(vmem_limit_bytes=VMEM),
    )(both, na, nb, nc, weights, w_qkv_t, table, bias)


def input_grad(d_packed_t, d_hidden, tokens, weights, table):
    shape = jax.ShapeDtypeStruct
    return pl.pallas_call(
        grad_kernel,
        out_shape=(
            shape((2, HALF_LAT, COLS, D), BF),
            shape((64, HALO, 128), BF),
            shape((32, 128), BF),
        ),
        in_specs=[vmem_spec()] * 5,
        out_specs=[vmem_spec()] * 3,
        scratch_shapes=[pltpu.VMEM((2, 54 * RA, 128), F32), pltpu.VMEM((FLAT, 128), F32)],
        compiler_params=pltpu.CompilerParams(vmem_limit_bytes=VMEM),
    )(d_packed_t, d_hidden, tokens, weights, table)


def local(tokens, cotangent, ln1_gain, w_qkv, w_proj, ln2_gain, w_up, w_down, bias_table):
    edge = ((0, 0),) * 3
    both = jnp.pad(tokens, ((0, 2),) + edge) + jnp.pad(cotangent, ((2, 0),) + edge)
    part_a, part_b, part_c = pack_halos(both)
    na = lax.ppermute(part_a, LAT, one_axis(8, -1))
    nb = lax.ppermute(part_b, LON, one_axis(16, -1))
    nc = lax.ppermute(part_c, LON + LAT, shift_pairs(-1, -1))

    weights = jnp.concatenate((w_qkv, w_proj, w_up, w_down.T), axis=1)
    gains = jnp.pad(jnp.stack((ln1_gain, ln2_gain)), ((0, 0), (0, POSITIONS - D)))
    table = jnp.concatenate((bias_table.reshape(HEADS, 1, POSITIONS), gains[:, None]), axis=0)
    bias, w_qkv_t = prepare(table, weights)
    mine, send, d_packed_t, d_hidden, shifted = run_block(both, na, nb, nc, weights, w_qkv_t, table, bias)

    pair = [(0, 1), (1, 0)]
    got = lax.ppermute(send, "c", pair)
    own, halo, gain = input_grad(d_packed_t, d_hidden, shifted, weights, table)
    chunks = jax.ShapeDtypeStruct((64, 32 + HALO, 128), BF)
    joined = pl.pallas_call(
        join_kernel,
        out_shape=chunks,
        in_specs=[vmem_spec()] * 4,
        out_specs=vmem_spec(),
        compiler_params=pltpu.CompilerParams(vmem_limit_bytes=VMEM),
    )(mine, got, halo, gain)
    spread = lax.all_to_all(joined, CHIPS, 0, 0, tiled=True)
    reply = pl.pallas_call(
        reply_kernel,
        out_shape=chunks,
        in_specs=[vmem_spec()],
        out_specs=vmem_spec(),
        compiler_params=pltpu.CompilerParams(vmem_limit_bytes=VMEM),
    )(spread)
    half_a = lax.all_to_all(reply, CHIPS, 0, 0, tiled=True)
    half_b = lax.ppermute(half_a, "c", pair)
    shape = jax.ShapeDtypeStruct
    total_tokens = 128 * tokens.shape[0] * tokens.shape[1] * tokens.shape[2]
    dx, dg1, dqkv, dproj, dg2, dup, ddown, dt = pl.pallas_call(
        functools.partial(finish_kernel, grad_scale=1.0 / math.sqrt(total_tokens)),
        out_shape=(
            shape(tokens.shape, BF),
            shape((1, D), F32),
            shape((D, 3 * D), F32),
            shape((D, D), F32),
            shape((1, D), F32),
            shape((D, MLP), F32),
            shape((D, MLP), F32),
            shape((HEADS, 1, POSITIONS), F32),
        ),
        in_specs=[vmem_spec()] * 3,
        out_specs=[vmem_spec()] * 8,
        scratch_shapes=[
            pltpu.VMEM((3, 8 * RA, 128), F32),
            pltpu.VMEM((32, 256), F32),
            pltpu.VMEM((COLS, D), F32),
            pltpu.VMEM((8, POSITIONS), F32),
            pltpu.VMEM((FLAT, 128), F32),
        ],
        compiler_params=pltpu.CompilerParams(vmem_limit_bytes=VMEM),
    )(half_a, half_b, own)
    return (
        dx,
        dg1.reshape(D),
        dqkv,
        dproj,
        dg2.reshape(D),
        dup,
        ddown.T,
        dt.reshape(1, HEADS, POSITIONS),
    )


def solution(mesh):
    parts = Mesh(mesh.devices.reshape(4, 2, 2, 2, 4), ("y", "zh", "c", "zl", "x"))
    grid = P(None, LAT, LON, None)
    in_specs = (grid, grid, P(), P(), P(), P(), P(), P(), P(LAT, None, None))
    out_specs = (grid, P(), P(), P(), P(), P(), P(), P(LAT, None, None))
    return jax.shard_map(local, mesh=parts, in_specs=in_specs, out_specs=out_specs, check_vma=False)
```

```python
import functools
import math

import jax
import jax.numpy as jnp
from jax import lax
from jax.experimental import pallas as pl
from jax.experimental.pallas import tpu as pltpu
from jax.sharding import Mesh
from jax.sharding import PartitionSpec as P

BF = jnp.bfloat16
F32 = jnp.float32
D = 192
HEADS = 6
DH = 32
MLP = 768
WIN_LAT = 6
WIN_LON = 12
HALF_LAT = 3
HALF_LON = 6
RA = 12
WIN = 144
COLS = 48
INNER = COLS - HALF_LON
WINDOWS = 4
OFFS = 2 * WIN_LON - 1
SPAN = OFFS * RA
LINE = WIN_LAT * OFFS
POSITIONS = 4 * WIN_LAT * LINE
SCALE = DH ** (-0.5)
W_CHUNKS = 54
GAIN_AT = 61
HALO = 8
NORTH_AT, EAST_AT, CORNER_AT, FLAT = 0, 384, 440, 512
B_CHUNKS = 5
VMEM = 24 * 1024 * 1024
LOG2E = 1.0 / math.log(2.0)
UNROLL = True
GROUP = 2
TOK = WINDOWS * WIN

LON = ("y", "zh", "c")
LAT = ("zl", "x")
CHIPS = ("y", "zh", "zl", "x")


def nn(a, b):
    return lax.dot_general(a, b, (((1,), (0,)), ((), ())), preferred_element_type=F32)


def nt(a, b):
    return lax.dot_general(a, b, (((1,), (1,)), ((), ())), preferred_element_type=F32)


def tn(a, b):
    return lax.dot_general(a, b, (((0,), (0,)), ((), ())), preferred_element_type=F32)


def put_parts(xs, ys, start, count, parts):
    rows = pl.ds(start, count, stride=RA)
    xs[0, rows, :] = parts[0]
    ys[0, rows, :] = parts[1]
    xs[1, rows, :] = parts[2]
    ys[1, rows, :] = pltpu.roll(parts[2], 64, 1)


def put_pair(xs, ys, start, count, ref, l, r):
    put_parts(xs, ys, start, count, [ref[l, r, k].astype(F32) for k in range(3)])


def take_pair(src, flat, at, first, second, count):
    first = pl.ds(first, count, stride=RA)
    second = pl.ds(second, count, stride=RA)
    lane = lax.broadcasted_iota(jnp.int32, (count, 128), 1)
    flat[at : at + count, :] = src[0, first, :]
    flat[at + count : at + 2 * count, :] = src[0, second, :]
    flat[at + 2 * count : at + 3 * count, :] = jnp.where(
        lane < 64, src[1, first, :], pltpu.roll(src[1, second, :], 64, 1)
    )


def open_pair(flat, at, count):
    pair = flat[at + 2 * count : at + 3 * count, :]
    return (
        jnp.concatenate((flat[at : at + count, :], pair[:, :64]), axis=1),
        jnp.concatenate((flat[at + count : at + 2 * count, :], pair[:, 64:]), axis=1),
    )


def get_rows(src, start, count):
    low = src[0, pl.ds(start, count, stride=RA), :]
    high = src[1, pl.ds(start, count, stride=RA), :]
    return jnp.concatenate((low, high[:, : D - 128]), axis=1).astype(BF)


def token_rows(src, start, count):
    return jnp.concatenate((src[0, start : start + count, :], src[1, start : start + count, : D - 128]), axis=1)


def each_window(body):
    if UNROLL:
        for w in range(0, WINDOWS, GROUP):
            body(range(w, w + GROUP))
    else:
        pl.loop(0, WINDOWS)(body)


def norm_stats(values):
    mean = jnp.mean(values, axis=-1, keepdims=True)
    centred = values - mean
    variance = jnp.mean(centred * centred, axis=-1, keepdims=True)
    rstd = lax.rsqrt(variance + 1e-05)
    return centred * rstd, rstd


def gelu_pair(u):
    cdf = 0.5 + 0.5 * lax.erf(u * (0.5**0.5))
    slope = cdf + u * jnp.exp(-0.5 * u * u) * (1.0 / math.sqrt(2.0 * math.pi))
    return u * cdf, slope


def norm_back(d_hat, hat, rstd):
    m1 = jnp.mean(d_hat, axis=-1, keepdims=True)
    m2 = jnp.mean(d_hat * hat, axis=-1, keepdims=True)
    return rstd * (d_hat - m1 - hat * m2)


def pack_kernel(both_ref, pa_ref, pb_ref, pc_ref):
    def parts(l, row, cols):
        x = both_ref[l, row].astype(F32)[cols]
        dy = both_ref[2 + l, row].astype(F32)[cols]
        return [x[:, :128], dy[:, :128], jnp.concatenate((x[:, 128:], dy[:, 128:]), axis=1)]

    for l in range(2):
        for r in range(HALF_LAT):
            rows = parts(l, r, slice(HALF_LON, COLS)) + [jnp.zeros((128 - 3 * INNER, 128), F32)]
            pa_ref[l, r] = jnp.concatenate(rows, axis=0).astype(BF)
            for k, rows in enumerate(parts(l, r + HALF_LAT, slice(0, HALF_LON))):
                pb_ref[l, r, k] = rows.astype(BF)
            for k, rows in enumerate(parts(l, r, slice(0, HALF_LON))):
                pc_ref[l, r, k] = rows.astype(BF)


def diagonal_order():
    row = lax.broadcasted_iota(jnp.int32, (SPAN, SPAN), 0)
    col = lax.broadcasted_iota(jnp.int32, (SPAN, SPAN), 1)
    step = lax.shift_right_logical(col * 5462, 16)
    return jnp.where(row == (col - step * RA) * OFFS + OFFS - 1 - step, 1.0, 0.0).astype(BF)


def prepare_kernel(table_ref, w_ref, bias_ref, wqkvt_ref, table, lines, rows_first):
    last = lax.axis_index(LAT) == lax.axis_size(LAT) - 1
    wqkvt_ref[...] = w_ref[:, : 3 * D].T
    for h in range(HEADS):
        lines[h : h + 1, :] = table_ref[h]
    table[...] = jnp.zeros_like(table)
    for li in range(2):
        for ai in range(WIN_LAT):
            place = li * WIN_LAT + ai
            parts = []
            for lj in range(2):
                off = ((li * 2 + lj) * WIN_LAT + ai) * LINE
                parts.append(lines[:, off : off + LINE])
            parts.append(jnp.zeros((8, 384 - SPAN), F32))
            both = jnp.concatenate(parts, axis=1)
            for b in range(3):
                table[b, place * 8 : place * 8 + 8, :] = both[:, 128 * b : 128 * (b + 1)]
    t2 = jnp.concatenate((table[0], table[1], table[2, :, : SPAN - 256]), axis=1)
    hi = t2.astype(BF)
    rest = t2 - hi.astype(F32)
    mid = rest.astype(BF)
    low = (rest - mid.astype(F32)).astype(BF)
    perm = diagonal_order()
    wide = (nn(hi, perm) + nn(mid, perm) + nn(low, perm)) * LOG2E
    wide = jnp.concatenate((wide, jnp.zeros((8 * RA, 384 - SPAN), F32)), axis=1)
    for b in range(3):
        table[b] = wide[:, 128 * b : 128 * (b + 1)]
    key_late = lax.rem(lax.broadcasted_iota(jnp.int32, (WIN, WIN), 0), WIN_LAT) >= HALF_LAT
    query_late = lax.rem(lax.broadcasted_iota(jnp.int32, (WIN, WIN), 1), WIN_LAT) >= HALF_LAT
    split = jnp.logical_and(key_late != query_late, last)
    mask_rows = jnp.where(split, -1e9 * LOG2E, 0.0)
    for h in range(HEADS):
        wide_h = jnp.concatenate([table[b, pl.ds(h, RA, stride=8), :] for b in range(3)], axis=1)
        for oi in range(WIN_LON):
            start = (WIN_LON - 1 - oi) * RA
            rows_first[h, oi * RA : (oi + 1) * RA, :] = wide_h[:, start : start + WIN]
    for h in range(HEADS):
        bias_ref[h] = rows_first[h].T + mask_rows


def block_kernel(
    both_ref, na_ref, nb_ref, nc_ref, w_ref, wqkvt, table_ref, bias,
    mine_ref, send_ref, dp_t, hid, xs,
    ys, probs, heads_t, o_t, do_t, kvs, dss,
    n1s, d_bias, m_acc, g_acc, dw, table,
):
    for l in range(2):
        for r in range(HALF_LAT):
            x = both_ref[l, r + HALF_LAT].astype(F32)
            dy = both_ref[2 + l, r + HALF_LAT].astype(F32)
            pair = jnp.concatenate((x[:, 128:], dy[:, 128:]), axis=1)
            put_parts(xs, ys, l * 6 + r, COLS, (x[:, :128], dy[:, :128], pair))
            north = na_ref[l, r].astype(F32)
            north = [north[k * INNER : (k + 1) * INNER] for k in range(3)]
            put_parts(xs, ys, HALF_LON * RA + l * 6 + r + HALF_LAT, INNER, north)
            put_pair(xs, ys, COLS * RA + l * 6 + r, HALF_LON, nb_ref, l, r)
            put_pair(xs, ys, COLS * RA + l * 6 + r + HALF_LAT, HALF_LON, nc_ref, l, r)

    g_acc[...] = jnp.zeros_like(g_acc)

    g1 = table_ref[HEADS][:, :D]
    g2 = table_ref[HEADS + 1][:, :D]
    w_proj = w_ref[:, 3 * D : 4 * D]
    first = HALF_LON * RA

    hat1, rstd1 = norm_stats(token_rows(xs, first, TOK))
    n1 = (hat1 * g1).astype(BF)
    n1s[...] = n1
    kvs[...] = nn(n1, w_ref[:, D : 3 * D]).astype(BF)

    def attend(ws):
        jobs = [(w, h) for w in ws for h in range(HEADS)]
        rows = {w: pl.ds(w * WIN, WIN) for w in ws}
        parts = [slice(h * DH, (h + 1) * DH) for h in range(HEADS)]
        scores = [
            nn(kvs[rows[w], parts[h]], heads_t[w, parts[h], :]) * (SCALE * LOG2E) + bias[h] for w, h in jobs
        ]
        tops = [jnp.max(s, axis=0, keepdims=True) for s in scores]
        powers = [jnp.exp2(s - top) for s, top in zip(scores, tops)]
        shares = [1.0 / jnp.sum(e, axis=0, keepdims=True) for e in powers]
        for k, (w, h) in enumerate(jobs):
            probs[w, h] = (powers[k] * shares[k]).astype(BF)
        for w, h in jobs:
            o_t[w, parts[h], :] = nn(heads_t[w, 2 * D + h * DH : 2 * D + (h + 1) * DH, :], probs[w, h]).astype(BF)

    for w in range(WINDOWS):
        heads_t[w] = nt(wqkvt[...], n1[w * WIN : (w + 1) * WIN]).astype(BF)
    each_window(attend)
    for w in range(WINDOWS):
        hid[w * WIN : (w + 1) * WIN, :] = tn(o_t[w], w_proj)

    hidden = token_rows(xs, first, TOK) + hid[...]
    hat2, rstd2 = norm_stats(hidden)
    n2 = (hat2 * g2).astype(BF)
    n2_t = n2.T
    dy = token_rows(ys, first, TOK)
    dyb = dy.astype(BF)
    dy_t = dyb.T
    d_n2 = jnp.zeros((TOK, D), F32)
    for j in range(3):
        cols = slice(j * 256, (j + 1) * 256)
        act, slope = gelu_pair(nn(n2, w_ref[:, 4 * D + j * 256 : 4 * D + (j + 1) * 256]))
        d_act = nn(dyb, w_ref[:, 4 * D + MLP + j * 256 : 4 * D + MLP + (j + 1) * 256]).astype(BF).astype(F32)
        d_u = (d_act * slope).astype(BF)
        m_acc[2 * D :, cols] = nn(dy_t, act.astype(BF)).astype(BF)
        m_acc[D : 2 * D, cols] = nn(n2_t, d_u).astype(BF)
        d_n2 = d_n2 + nt(d_u, w_ref[:, 4 * D + j * 256 : 4 * D + (j + 1) * 256])
    d_n2 = d_n2.astype(BF).astype(F32)
    g_acc[1:2, :D] = jnp.sum(d_n2 * hat2, axis=0, keepdims=True)
    d_hidden = dy + norm_back(d_n2 * g2, hat2, rstd2)
    dhb = d_hidden.astype(BF)
    hid[...] = d_hidden
    d_proj = jnp.zeros((D, D), F32)
    for w in range(WINDOWS):
        rows = slice(w * WIN, (w + 1) * WIN)
        d_proj = d_proj + nn(o_t[w], dhb[rows])
        do_t[w] = nt(w_proj, dhb[rows]).astype(BF)

    def attend_back(ws):
        jobs = [(w, h) for w in ws for h in range(HEADS)]
        rows = {w: pl.ds(w * WIN, WIN) for w in ws}
        parts = [slice(h * DH, (h + 1) * DH) for h in range(HEADS)]
        d_probs = [
            nn(kvs[rows[w], D + h * DH : D + (h + 1) * DH], do_t[w, parts[h], :]) for w, h in jobs
        ]
        for k, (w, h) in enumerate(jobs):
            pf = probs[w, h].astype(F32)
            prod = pf * d_probs[k]
            ds = prod - pf * jnp.sum(prod, axis=0, keepdims=True)
            d_bias[h] = ds if w == 0 else d_bias[h] + ds
            dss[k] = ds.astype(BF)
        for k, (w, h) in enumerate(jobs):
            part = parts[h]
            q_t = heads_t[w, part, :]
            k_t = heads_t[w, D + h * DH : D + (h + 1) * DH, :]
            dp_t[w, part, :] = (nn(k_t, dss[k]) * SCALE).astype(BF)
            dp_t[w, D + h * DH : D + (h + 1) * DH, :] = (nt(q_t, dss[k]) * SCALE).astype(BF)
            dp_t[w, 2 * D + h * DH : 2 * D + (h + 1) * DH, :] = nt(do_t[w, part, :], probs[w, h]).astype(BF)

    each_window(attend_back)

    core = lax.axis_index("c")
    perm = diagonal_order()
    dw[...] = jnp.zeros_like(dw)
    d_qkv = jnp.zeros((3 * D, D), F32)
    for w in range(WINDOWS):
        d_qkv = d_qkv + nn(dp_t[w], n1s[w * WIN : (w + 1) * WIN, :])
    m_acc[:D, :] = jnp.concatenate((d_qkv.T, d_proj), axis=1).astype(BF)

    for h in range(HEADS):
        d_bias[h] = d_bias[h].T
    for oi in range(WIN_LON):
        start = (WIN_LON - 1 - oi) * RA
        for h in range(HEADS):
            dw[h * RA : (h + 1) * RA, start : start + WIN] += d_bias[h, oi * RA : (oi + 1) * RA, :]
    dwv = dw[:, :SPAN]
    dw_hi = dwv.astype(BF)
    dw_lo = (dwv - dw_hi.astype(F32)).astype(BF)
    d_t2 = nt(dw_hi, perm) + nt(dw_lo, perm)
    d_t2 = jnp.concatenate((d_t2, jnp.zeros((HEADS * RA, 384 - SPAN), F32)), axis=1)
    table[...] = jnp.zeros_like(table)
    for h in range(HEADS):
        for b in range(3):
            table[b, pl.ds(h, RA, stride=8), :] = d_t2[h * RA : (h + 1) * RA, 128 * b : 128 * (b + 1)]

    mine_half = pl.multiple_of(core * 288, 32)
    send_half = pl.multiple_of((1 - core) * 288, 32)
    for i in range(9):
        for b in range(6):
            cols = slice(b * 128, (b + 1) * 128)
            mine_ref[i * 6 + b] = m_acc[pl.ds(mine_half + 32 * i, 32), cols]
            send_ref[i * 6 + b] = m_acc[pl.ds(send_half + 32 * i, 32), cols]
    zero = jnp.zeros((32, 128), BF)
    for ref, half in ((mine_ref, core), (send_ref, 1 - core)):
        for k in range(W_CHUNKS, 64):
            ref[k] = zero

        @pl.when(half == 0)
        def _(ref=ref):
            for k in range(5):
                ref[W_CHUNKS + k] = table[k % 3, 32 * (k // 3) : 32 * (k // 3) + 32, :].astype(BF)
            ref[W_CHUNKS + B_CHUNKS] = g_acc[:, :128].astype(BF)
            ref[W_CHUNKS + B_CHUNKS + 1] = g_acc[:, 128:].astype(BF)

        @pl.when(half == 1)
        def _(ref=ref):
            for k in range(5, 9):
                ref[W_CHUNKS + k - 5] = table[k % 3, 32 * (k // 3) : 32 * (k // 3) + 32, :].astype(BF)


def grad_kernel(dp_t, hid, xs, w_ref, table_ref, own_ref, halo_ref, gain_ref, gs, flat):
    g1 = table_ref[HEADS][:, :D]
    first = HALF_LON * RA
    gs[:, :first, :] = jnp.zeros((2, first, 128), F32)
    d_n1 = []
    for w in range(WINDOWS):
        d_n1.append(nn(w_ref[:, : 3 * D], dp_t[w]).T)
    d_n1 = jnp.concatenate(d_n1, axis=0).astype(BF).astype(F32)
    hat1, rstd1 = norm_stats(token_rows(xs, first, TOK))
    d_gain = jnp.sum(d_n1 * hat1, axis=0, keepdims=True)
    spare = jnp.zeros((1, 256 - D), F32)
    gain_ref[...] = jnp.concatenate(
        (d_gain[:, :128], jnp.concatenate((d_gain[:, 128:], spare), axis=1), jnp.zeros((30, 128), F32)), axis=0
    ).astype(BF)
    d_x = hid[...] + norm_back(d_n1 * g1, hat1, rstd1)
    gs[0, first:, :] = d_x[:, :128]
    gs[1, first:, : D - 128] = d_x[:, 128:]

    for l in range(2):
        for r in range(HALF_LAT):
            own_ref[l, r] = get_rows(gs, l * 6 + r, COLS)

    flat[...] = jnp.zeros_like(flat)
    inner = COLS - HALF_LON
    for r in range(HALF_LAT):
        late = r + HALF_LAT
        take_pair(gs, flat, NORTH_AT + r * 3 * inner, first + late, first + 6 + late, inner)
        take_pair(gs, flat, EAST_AT + r * 3 * HALF_LON, COLS * RA + r, COLS * RA + r + 6, HALF_LON)
        take_pair(gs, flat, CORNER_AT + r * 3 * HALF_LON, COLS * RA + late, COLS * RA + late + 6, HALF_LON)
    for k in range(64):
        halo_ref[k] = flat[HALO * k : HALO * (k + 1), :].astype(BF)


def join_kernel(mine_ref, got_ref, halo_ref, gain_ref, out_ref):
    for k in range(64):
        if k != GAIN_AT:
            out_ref[k, :32] = (mine_ref[k].astype(F32) + got_ref[k].astype(F32)).astype(BF)
        out_ref[k, 32:] = halo_ref[k]
    out_ref[GAIN_AT, :32] = gain_ref[...]


def reply_kernel(got_ref, out_ref):
    relay = lax.axis_index(CHIPS)
    is_bias = jnp.logical_and(relay >= W_CHUNKS, relay < W_CHUNKS + B_CHUNKS).astype(F32)
    total = jnp.zeros((32, 128), F32)
    bands = []
    for lat in range(8):
        s = got_ref[lat, :32].astype(F32)
        for j in range(1, 8):
            s = s + got_ref[j * 8 + lat, :32].astype(F32)
        bands.append(s)
        total = total + s
    by_lat = jnp.logical_or(relay < EAST_AT // HALO, relay >= CORNER_AT // HALO).astype(jnp.int32)
    by_lon = jnp.logical_and(relay >= EAST_AT // HALO, lax.axis_index("c") == 1).astype(jnp.int32)
    for lat in range(8):
        s = jnp.where(is_bias > 0.5, bands[lat], total).astype(BF)
        from_lat = lax.rem(lat + 7 * by_lat, 8)
        for j in range(8):
            out_ref[j * 8 + lat, :32] = s
            out_ref[j * 8 + lat, 32:] = got_ref[lax.rem(j + 7 * by_lon, 8) * 8 + from_lat, 32:]


def finish_kernel(
    a_ref, b_ref, own_ref,
    dx_ref, dg1_ref, dqkv_ref, dproj_ref, dg2_ref, dup_ref, ddown_ref, dt_ref,
    table, g_acc, line, lines, flat, grad_scale,
):
    core = lax.axis_index("c")
    for block in range(18):
        mine = core == block // 9
        tiles = []
        for b in range(6):
            chunk = block % 9 * 6 + b
            tiles.append(jnp.where(mine, a_ref[chunk, :32].astype(F32), b_ref[chunk, :32].astype(F32)) * grad_scale)
        rows = slice(block % 6 * 32, block % 6 * 32 + 32)
        if block < 6:
            for b in range(4):
                dqkv_ref[rows, b * 128 : (b + 1) * 128] = tiles[b]
            dqkv_ref[rows, 512:] = tiles[4][:, :64]
            dproj_ref[rows, :] = jnp.concatenate((tiles[4][:, 64:], tiles[5]), axis=1)
        else:
            out = dup_ref if block < 12 else ddown_ref
            for b in range(6):
                out[rows, b * 128 : (b + 1) * 128] = tiles[b]
    for ref, half in ((a_ref, core), (b_ref, 1 - core)):

        @pl.when(half == 0)
        def _(ref=ref):
            for k in range(5):
                table[k % 3, 32 * (k // 3) : 32 * (k // 3) + 32, :] = ref[W_CHUNKS + k, :32].astype(F32)
            g_acc[:, :128] = ref[W_CHUNKS + B_CHUNKS, :32].astype(F32) * grad_scale
            g_acc[:, 128:] = ref[W_CHUNKS + B_CHUNKS + 1, :32].astype(F32) * grad_scale

        @pl.when(half == 1)
        def _(ref=ref):
            for k in range(5, 9):
                table[k % 3, 32 * (k // 3) : 32 * (k // 3) + 32, :] = ref[W_CHUNKS + k - 5, :32].astype(F32)

    d_gain = (a_ref[GAIN_AT, :32].astype(F32) + b_ref[GAIN_AT, :32].astype(F32)) * grad_scale
    dg1_ref[:, :128] = d_gain[0:1, :]
    dg1_ref[:, 128:] = d_gain[1:2, : D - 128]
    dg2_ref[...] = g_acc[1:2, :D]
    for li in range(2):
        for ai in range(WIN_LAT):
            place = li * WIN_LAT + ai
            rows = jnp.concatenate([table[b, place * 8 : place * 8 + 8, :] for b in range(3)], axis=1)
            for lj in range(2):
                off = ((li * 2 + lj) * WIN_LAT + ai) * LINE
                lines[:, off : off + LINE] = rows[:, lj * LINE : (lj + 1) * LINE]
    for h in range(HEADS):
        dt_ref[h] = lines[h : h + 1, :]

    for k in range(64):
        ref = a_ref if k < EAST_AT // HALO else b_ref
        flat[HALO * k : HALO * (k + 1), :] = ref[k, 32:].astype(F32)
    inner = COLS - HALF_LON
    for r in range(HALF_LAT):
        north = open_pair(flat, NORTH_AT + r * 3 * inner, inner)
        east = open_pair(flat, EAST_AT + r * 3 * HALF_LON, HALF_LON)
        corner = open_pair(flat, CORNER_AT + r * 3 * HALF_LON, HALF_LON)
        for l in range(2):
            line[...] = own_ref[l, r].astype(F32)
            line[:HALF_LON, :] = east[l]
            dx_ref[l, r + HALF_LAT] = line[...].astype(BF)
            line[HALF_LON:, :] = north[l]
            line[:HALF_LON, :] = corner[l]
            dx_ref[l, r] = line[...].astype(BF)


def shift_pairs(lon_by, lat_by):
    pairs = []
    for lon in range(16):
        for lat in range(8):
            pairs.append((lon * 8 + lat, ((lon + lon_by) % 16) * 8 + (lat + lat_by) % 8))
    return pairs


def one_axis(length, by):
    return [(i, (i + by) % length) for i in range(length)]


def vmem_spec():
    return pl.BlockSpec(memory_space=pltpu.VMEM)


def prepare(table, weights):
    shape = jax.ShapeDtypeStruct
    return pl.pallas_call(
        prepare_kernel,
        out_shape=(shape((HEADS, WIN, WIN), F32), shape((3 * D, D), BF)),
        in_specs=[vmem_spec()] * 2,
        out_specs=[vmem_spec()] * 2,
        scratch_shapes=[
            pltpu.VMEM((3, 8 * RA, 128), F32),
            pltpu.VMEM((8, POSITIONS), F32),
            pltpu.VMEM((HEADS, WIN, WIN), F32),
        ],
        compiler_params=pltpu.CompilerParams(vmem_limit_bytes=VMEM),
    )(table, weights)


def pack_halos(both):
    shape = jax.ShapeDtypeStruct
    return pl.pallas_call(
        pack_kernel,
        out_shape=(
            shape((2, HALF_LAT, 128, 128), BF),
            shape((2, HALF_LAT, 3, HALF_LON, 128), BF),
            shape((2, HALF_LAT, 3, HALF_LON, 128), BF),
        ),
        in_specs=[vmem_spec()],
        out_specs=[vmem_spec()] * 3,
        compiler_params=pltpu.CompilerParams(vmem_limit_bytes=VMEM),
    )(both)


def run_block(both, na, nb, nc, weights, w_qkv_t, table, bias):
    shape = jax.ShapeDtypeStruct
    return pl.pallas_call(
        block_kernel,
        out_shape=(
            shape((64, 32, 128), BF),
            shape((64, 32, 128), BF),
            shape((WINDOWS, 3 * D, WIN), BF),
            shape((TOK, D), F32),
            shape((2, 54 * RA, 128), F32),
        ),
        in_specs=[vmem_spec()] * 8,
        out_specs=[vmem_spec()] * 5,
        scratch_shapes=[
            pltpu.VMEM((2, 54 * RA, 128), F32),
            pltpu.VMEM((WINDOWS, HEADS, WIN, WIN), BF),
            pltpu.VMEM((WINDOWS, 3 * D, WIN), BF),
            pltpu.VMEM((WINDOWS, D, WIN), BF),
            pltpu.VMEM((WINDOWS, D, WIN), BF),
            pltpu.VMEM((TOK, 2 * D), BF),
            pltpu.VMEM((WINDOWS * HEADS, WIN, WIN), BF),
            pltpu.VMEM((TOK, D), BF),
            pltpu.VMEM((HEADS, WIN, WIN), F32),
            pltpu.VMEM((3 * D, MLP), BF),
            pltpu.VMEM((32, 256), F32),
            pltpu.VMEM((HEADS * RA, 384), F32),
            pltpu.VMEM((3, 8 * RA, 128), F32),
        ],
        compiler_params=pltpu.CompilerParams(vmem_limit_bytes=VMEM),
    )(both, na, nb, nc, weights, w_qkv_t, table, bias)


def input_grad(d_packed_t, d_hidden, tokens, weights, table):
    shape = jax.ShapeDtypeStruct
    return pl.pallas_call(
        grad_kernel,
        out_shape=(
            shape((2, HALF_LAT, COLS, D), BF),
            shape((64, HALO, 128), BF),
            shape((32, 128), BF),
        ),
        in_specs=[vmem_spec()] * 5,
        out_specs=[vmem_spec()] * 3,
        scratch_shapes=[pltpu.VMEM((2, 54 * RA, 128), F32), pltpu.VMEM((FLAT, 128), F32)],
        compiler_params=pltpu.CompilerParams(vmem_limit_bytes=VMEM),
    )(d_packed_t, d_hidden, tokens, weights, table)


def local(tokens, cotangent, ln1_gain, w_qkv, w_proj, ln2_gain, w_up, w_down, bias_table):
    edge = ((0, 0),) * 3
    both = jnp.pad(tokens, ((0, 2),) + edge) + jnp.pad(cotangent, ((2, 0),) + edge)
    part_a, part_b, part_c = pack_halos(both)
    na = lax.ppermute(part_a, LAT, one_axis(8, -1))
    nb = lax.ppermute(part_b, LON, one_axis(16, -1))
    nc = lax.ppermute(part_c, LON + LAT, shift_pairs(-1, -1))

    weights = jnp.concatenate((w_qkv, w_proj, w_up, w_down.T), axis=1)
    gains = jnp.pad(jnp.stack((ln1_gain, ln2_gain)), ((0, 0), (0, POSITIONS - D)))
    table = jnp.concatenate((bias_table.reshape(HEADS, 1, POSITIONS), gains[:, None]), axis=0)
    bias, w_qkv_t = prepare(table, weights)
    mine, send, d_packed_t, d_hidden, shifted = run_block(both, na, nb, nc, weights, w_qkv_t, table, bias)

    pair = [(0, 1), (1, 0)]
    got = lax.ppermute(send, "c", pair)
    own, halo, gain = input_grad(d_packed_t, d_hidden, shifted, weights, table)
    chunks = jax.ShapeDtypeStruct((64, 32 + HALO, 128), BF)
    joined = pl.pallas_call(
        join_kernel,
        out_shape=chunks,
        in_specs=[vmem_spec()] * 4,
        out_specs=vmem_spec(),
        compiler_params=pltpu.CompilerParams(vmem_limit_bytes=VMEM),
    )(mine, got, halo, gain)
    spread = lax.all_to_all(joined, CHIPS, 0, 0, tiled=True)
    reply = pl.pallas_call(
        reply_kernel,
        out_shape=chunks,
        in_specs=[vmem_spec()],
        out_specs=vmem_spec(),
        compiler_params=pltpu.CompilerParams(vmem_limit_bytes=VMEM),
    )(spread)
    half_a = lax.all_to_all(reply, CHIPS, 0, 0, tiled=True)
    half_b = lax.ppermute(half_a, "c", pair)
    shape = jax.ShapeDtypeStruct
    total_tokens = 128 * tokens.shape[0] * tokens.shape[1] * tokens.shape[2]
    dx, dg1, dqkv, dproj, dg2, dup, ddown, dt = pl.pallas_call(
        functools.partial(finish_kernel, grad_scale=1.0 / math.sqrt(total_tokens)),
        out_shape=(
            shape(tokens.shape, BF),
            shape((1, D), F32),
            shape((D, 3 * D), F32),
            shape((D, D), F32),
            shape((1, D), F32),
            shape((D, MLP), F32),
            shape((D, MLP), F32),
            shape((HEADS, 1, POSITIONS), F32),
        ),
        in_specs=[vmem_spec()] * 3,
        out_specs=[vmem_spec()] * 8,
        scratch_shapes=[
            pltpu.VMEM((3, 8 * RA, 128), F32),
            pltpu.VMEM((32, 256), F32),
            pltpu.VMEM((COLS, D), F32),
            pltpu.VMEM((8, POSITIONS), F32),
            pltpu.VMEM((FLAT, 128), F32),
        ],
        compiler_params=pltpu.CompilerParams(vmem_limit_bytes=VMEM),
    )(half_a, half_b, own)
    return (
        dx,
        dg1.reshape(D),
        dqkv,
        dproj,
        dg2.reshape(D),
        dup,
        ddown.T,
        dt.reshape(1, HEADS, POSITIONS),
    )


def solution(mesh):
    parts = Mesh(mesh.devices.reshape(4, 2, 2, 2, 4), ("y", "zh", "c", "zl", "x"))
    grid = P(None, LAT, LON, None)
    in_specs = (grid, grid, P(), P(), P(), P(), P(), P(), P(LAT, None, None))
    out_specs = (grid, P(), P(), P(), P(), P(), P(), P(LAT, None, None))
    return jax.shard_map(local, mesh=parts, in_specs=in_specs, out_specs=out_specs, check_vma=False)
```
